32 devices in a mesh: rows: 4 (over y, core), seq: 8 (over z, x).
Axes of the slice: x: 2, y: 2, z: 4, core: 2. Of those that a mesh axis runs over, the one named last changes fastest.
Arguments:
- tokens: bfloat16 [8, 4096, 768], P('rows', 'seq'), may hold values from -6 to 6
- doc_starts: int32 [8, 8], P('rows'), may hold values from 0 to 4095, as said below
- norm_gain: float32 [768], replicated, may hold values from 0.5 to 1.5
- in_weight: bfloat16 [768, 3376], replicated, may hold values from -0.21875 to 0.21875
- conv_weight: float32 [4, 1792], replicated, may hold values from -3 to 3
- conv_bias: float32 [1792], replicated, may hold values from -3 to 3
- dt_bias: float32 [48], replicated, may hold values from -1 to 1
- decay_rate: float32 [48], replicated, may hold values from 0.00012207031 to 0.1
- skip_scale: float32 [24], replicated, may hold values from 0.5 to 2
- out_gain: float32 [1536], replicated, may hold values from 0.5 to 1.5
- out_weight: bfloat16 [1536, 768], replicated, may hold values from -0.15625 to 0.15625
- cotangent: bfloat16 [8, 4096, 768], P('rows', 'seq'), may hold values from -6 to 6
Outputs:
- mixed: bfloat16 [8, 4096, 768], P('rows', 'seq')
- tokens_grad: bfloat16 [8, 4096, 768], P('rows', 'seq')
- norm_gain_grad: float32 [768], replicated
- in_weight_grad: float32 [768, 3376], replicated
- conv_weight_grad: float32 [4, 1792], replicated
- conv_bias_grad: float32 [1792], replicated
- dt_bias_grad: float32 [48], replicated
- decay_rate_grad: float32 [48], replicated
- skip_scale_grad: float32 [24], replicated
- out_gain_grad: float32 [1536], replicated
- out_weight_grad: float32 [1536, 768], replicated
The draws below stay inside these ranges and needn't reach their ends.
Inputs may be any that keep to these rules, and one draw needn't show every extreme that they name: `doc_starts`: per row increasing, the first 0. In one row of each 2 consecutive rows the second lies in positions 1 to 511 and the others in the last 511 positions, the last being 4095; in every other row start k lies within 256 of k * 512.
All inputs are finite; a program needn't handle non-finite values.
Results may differ from the reference program's by a relative error of at most 0.0079.
Values sent between devices are 32-bit elements; how exact they have to be, the bound alone decides.
A program may use at most 384 MiB of HBM per device.

```python
import math
from functools import partial
import jax
import jax.numpy as jnp
from jax import lax

D = 768
INNER = 1536
HEADS = 24
HEAD = 64
STATE = 64
KW = 4
ROWS_DEV = 2
SEQ_DEV = 512
ROWS = 8
LENGTH = 4096
DOCS = 8


def spanning_row(row_key):
    first_key, rest_key = jax.random.split(row_key)
    second = jax.random.randint(first_key, (1,), 1, SEQ_DEV).astype(jnp.int32)
    picks = jax.random.permutation(rest_key, SEQ_DEV - 2)[:DOCS - 3]
    middle = (jnp.sort(picks) + (LENGTH - SEQ_DEV + 1)).astype(jnp.int32)
    ending = jnp.full((1,), LENGTH - 1, jnp.int32)
    return jnp.concatenate([jnp.zeros((1,), jnp.int32), second, middle, ending])


def packed_row(row_key):
    offsets = jax.random.randint(row_key, (DOCS - 1,), -(SEQ_DEV // 2), SEQ_DEV // 2).astype(jnp.int32)
    shifted = jnp.concatenate([jnp.zeros((1,), jnp.int32), offsets])
    return (jnp.arange(DOCS, dtype=jnp.int32) * SEQ_DEV + shifted).astype(jnp.int32)


def draw_doc_starts(key, part):
    key = jax.random.fold_in(key, 7)
    pick_key, rows_key = jax.random.split(key)
    groups = ROWS // ROWS_DEV
    chosen = jax.random.randint(pick_key, (groups,), 0, ROWS_DEV).astype(jnp.int32)
    row_keys = jax.random.split(rows_key, ROWS)
    long_rows = jax.vmap(spanning_row)(row_keys)
    short_rows = jax.vmap(packed_row)(row_keys)
    row_ids = jnp.arange(ROWS, dtype=jnp.int32)
    spans = row_ids % ROWS_DEV == jnp.repeat(chosen, ROWS_DEV)
    return jnp.where(spans[:, None], long_rows, short_rows).astype(jnp.int32)


def steps_of(stream_key, extent, shards, low, high):
    level, own = 1.0, jax.random.fold_in(stream_key, 6)
    for dim, parts in shards:
        heights = jnp.exp(jax.random.uniform(jax.random.fold_in(own, dim), (parts,), jnp.float32, low / len(shards), high / len(shards)))
        level = level * jnp.repeat(heights, extent[dim] // parts).reshape([-1 if axis == dim else 1 for axis in range(len(extent))])
    return level


def bell_draw(key, dims, scale, most, cuts=(), held_as=jnp.bfloat16):
    factor_of = steps_of(key, dims, cuts, -0.22, 0.18) if cuts else 1.0
    values = jax.random.normal(key, dims, jnp.float32) * scale * factor_of
    return jnp.minimum(jnp.maximum(values, -most), most).astype(held_as)


def setup_inputs(seed: int = 0) -> dict:
    streams_of = jax.random.split(jax.random.key(seed), 13)
    tokens = bell_draw(streams_of[0], (ROWS, LENGTH, D), 1.0, 6.0, ((0, 4), (1, 8)))
    doc_starts = draw_doc_starts(jax.random.fold_in(streams_of[12], 71), 0)
    norm_gain = jnp.clip(1.0 + 0.1 * jax.random.normal(streams_of[2], (D,), jnp.float32), 0.5, 1.5)
    in_weight = bell_draw(streams_of[3], (D, 2 * INNER + 4 * STATE + 2 * HEADS), D ** -0.5, 0.21875)
    conv_weight = bell_draw(streams_of[4], (KW, INNER + 4 * STATE), 0.5, 3.0, (), jnp.float32)
    conv_bias = bell_draw(streams_of[5], (INNER + 4 * STATE,), 0.5, 3.0, (), jnp.float32)
    dt_bias = jnp.clip(jax.random.uniform(streams_of[6], (2 * HEADS,), jnp.float32, -1.0, 1.0), -1.0, 1.0)
    decay_rate = jnp.clip(jnp.exp(jax.random.uniform(streams_of[7], (2 * HEADS,), jnp.float32, math.log(0.00012207031), math.log(0.1))), 0.00012207031, 0.1)
    skip_scale = jnp.clip(jax.random.uniform(streams_of[8], (HEADS,), jnp.float32, 0.5, 2.0), 0.5, 2.0)
    out_gain = jnp.clip(1.0 + 0.1 * jax.random.normal(streams_of[9], (INNER,), jnp.float32), 0.5, 1.5)
    out_weight = bell_draw(streams_of[10], (INNER, D), INNER ** -0.5, 0.15625)
    cotangent = bell_draw(streams_of[11], (ROWS, LENGTH, D), 1.0, 6.0, ((0, 4), (1, 8)))
    return {"tokens": tokens, "doc_starts": doc_starts, "norm_gain": norm_gain, "in_weight": in_weight, "conv_weight": conv_weight, "conv_bias": conv_bias, "dt_bias": dt_bias, "decay_rate": decay_rate, "skip_scale": skip_scale, "out_gain": out_gain, "out_weight": out_weight, "cotangent": cotangent}


EPS = 1e-05
HIGH = lax.Precision.HIGHEST

@jax.custom_vjp
def low(v):
    return lax.optimization_barrier(v.astype(jnp.bfloat16)).astype(jnp.float32)

@jax.custom_vjp
def low_back(v):
    return v

def low_keep(v):
    return (low(v), None)

def low_pass(kept, grad):
    return (grad,)

def back_keep(v):
    return (v, None)

def back_low(kept, grad):
    return (low(grad),)
low.defvjp(low_keep, low_pass)
low_back.defvjp(back_keep, back_low)

def rms_scale(values):
    return lax.rsqrt(lax.optimization_barrier(jnp.mean(values * values, axis=-1, keepdims=True)) + EPS)

def doc_index(starts, positions):
    return lax.optimization_barrier(jnp.sum((starts[..., None, :] <= positions[:, None]).astype(jnp.int32), axis=-1)).astype(jnp.int32)

def block_out(values, step_sizes, inputs, readers, logsum, labels, carried_state, edge_label):
    positions = jnp.arange(values.shape[0])
    visible = jnp.logical_and(positions[:, None] > positions[None, :], labels[:, None] == labels[None, :]).astype(jnp.float32)
    decays = jnp.exp(jnp.minimum(logsum[:, None, :] - logsum[None, :, :], 0.0))
    intersection = jnp.dot(readers, inputs.T, precision=HIGH)
    weights = decays * (visible * intersection)[:, :, None] * step_sizes[None, :, :]
    result = jnp.einsum('tsh,shp->thp', weights, values, precision=HIGH)
    carried = jnp.exp(logsum) * (labels == edge_label).astype(jnp.float32)[:, None]
    reading = jnp.einsum('tn,hnp->thp', readers, carried_state, precision=HIGH)
    return result + carried[:, :, None] * reading

def block_summary(values, step_sizes, inputs, logsum, labels, edge_label):
    final_log = logsum[-1]
    weights_tail = jnp.exp(final_log[None, :] - logsum) * (labels == labels[-1]).astype(jnp.float32)[:, None] * step_sizes
    local_sum = jnp.einsum('sh,sn,shp->hnp', weights_tail, inputs, values, precision=HIGH)
    passed = jnp.exp(final_log) * (labels[-1] == edge_label).astype(jnp.float32)
    return (passed, local_sum)

def scan_direction(values, step_sizes, inputs, readers, rate, labels, block_size):
    count = values.shape[0] // block_size
    log_decay = -step_sizes * rate

    def advance(carry, item):
        carried_state, edge_label = carry
        part_values, part_steps, part_inputs, part_readers, part_log, part_labels = item
        logsum = jnp.cumsum(part_log, axis=0)
        result = block_out(part_values, part_steps, part_inputs, part_readers, logsum, part_labels, carried_state, edge_label)
        passed, local_sum = block_summary(part_values, part_steps, part_inputs, logsum, part_labels, edge_label)
        new_state = (passed[:, None, None] * carried_state + local_sum).astype(carried_state.dtype)
        return ((new_state, part_labels[-1].astype(jnp.int32)), result)
    items = tuple((item.reshape((count, block_size) + item.shape[1:]) for item in (values, step_sizes, inputs, readers, log_decay, labels)))
    start = (jnp.zeros((HEADS, STATE, HEAD), values.dtype), jnp.int32(-1))
    _, results = lax.scan(jax.checkpoint(advance), start, items)
    return results.reshape(values.shape)

def forward(source, norm_gain, in_weight, conv_weight, conv_bias, dt_bias, decay_rate, skip_scale, out_gain, out_weight, labels):
    rounded = low(source * rms_scale(source) * norm_gain)
    projected = low_back(jnp.einsum('rld,dk->rlk', rounded, in_weight, precision=HIGH))
    split = 2 * INNER + 4 * STATE
    gate_part = projected[..., :INNER]
    conv_part = projected[..., INNER:split]
    step_part = projected[..., split:]
    length_here = conv_part.shape[1]
    padded = jnp.pad(conv_part, ((0, 0), (KW - 1, 0), (0, 0)))
    conv_out = conv_bias + sum((conv_weight[offset] * padded[:, offset:offset + length_here] for offset in range(KW)))
    activated = jax.nn.silu(conv_out)
    values = activated[..., :INNER].reshape(activated.shape[:2] + (HEADS, HEAD))
    pieces = [activated[..., INNER + member * STATE:INNER + (member + 1) * STATE] for member in range(4)]
    step_sizes = jax.nn.softplus(step_part + dt_bias)
    block_size = math.gcd(length_here, 256)

    def row_mix(item):
        row_values, row_steps, in_fwd, in_rev, read_fwd, read_rev, row_labels = item
        ahead = scan_direction(row_values, row_steps[:, :HEADS], in_fwd, read_fwd, decay_rate[:HEADS], row_labels, block_size)
        behind = scan_direction(jnp.flip(row_values, 0), jnp.flip(row_steps[:, HEADS:], 0), jnp.flip(in_rev, 0), jnp.flip(read_rev, 0), decay_rate[HEADS:], jnp.flip(row_labels, 0), block_size)
        return ahead + jnp.flip(behind, 0)
    scanned = lax.map(row_mix, (values, step_sizes, pieces[0], pieces[1], pieces[2], pieces[3], labels))
    combined = scanned + skip_scale[:, None] * values
    gated = combined.reshape(activated.shape[:2] + (INNER,)) * jax.nn.silu(gate_part)
    normed = low(gated * rms_scale(gated) * out_gain)
    return source + jnp.einsum('rle,ed->rld', normed, out_weight, precision=HIGH)

def reference(tokens, doc_starts, norm_gain, in_weight, conv_weight, conv_bias, dt_bias, decay_rate, skip_scale, out_gain, out_weight, cotangent):
    labels = doc_index(doc_starts, jnp.arange(LENGTH, dtype=jnp.int32))
    floats = tuple((item.astype(jnp.float32) for item in (tokens, norm_gain, in_weight, conv_weight, conv_bias, dt_bias, decay_rate, skip_scale, out_gain, out_weight)))
    result, backward = jax.vjp(partial(forward, labels=labels), *floats)
    grads = backward(cotangent.astype(jnp.float32))
    return (result.astype(jnp.bfloat16), grads[0].astype(jnp.bfloat16), grads[1], grads[2], grads[3], grads[4], grads[5], grads[6], grads[7], grads[8], grads[9])
```

```python
import jax
import jax.numpy as jnp
from jax import lax
from jax.experimental import pallas as pl
from jax.experimental.pallas import tpu as pltpu
from jax.sharding import PartitionSpec as P

D = 768
INNER = 1536
HEADS = 24
HEAD = 64
STATE = 64
KW = 4
EPS = 1e-05

C = 256
GC = 256
G = INNER // GC
HG = GC // HEAD
CONV = INNER + 4 * STATE
PAD = 16
LOG2E = 1.4426950408889634
F32, BF16 = jnp.float32, jnp.bfloat16
NN, NT, TN = ((1,), (0,)), ((1,), (1,)), ((0,), (0,))
MESH = pl.DeviceIdType.MESH
VMEM_LIMIT = 60 * 1024 * 1024


def mm(a, b, dims=NN):
    return lax.dot_general(a, b, (dims, ((), ())), preferred_element_type=F32)


def split2(a):
    hi = a.astype(BF16)
    return hi, (a - hi.astype(F32)).astype(BF16)


def split3(a):
    hi = a.astype(BF16)
    rest = a - hi.astype(F32)
    mid = rest.astype(BF16)
    return hi, mid, (rest - mid.astype(F32)).astype(BF16)


def mm2(a, b, dims=NN):
    hi, lo = split2(a)
    return mm(hi, b, dims) + mm(lo, b, dims)


def mm3(a, b, dims=NN):
    hi, mid, lo = split3(a)
    return mm(hi, b, dims) + mm(mid, b, dims) + mm(lo, b, dims)


def mm22(a, b, dims=NN):
    ahi, alo = split2(a)
    bhi, blo = split2(b)
    return mm(ahi, bhi, dims) + mm(alo, bhi, dims) + mm(ahi, blo, dims)


def sigmoid(x):
    return 1.0 / (1.0 + jnp.exp(-x))


def softplus(x):
    return jnp.maximum(x, 0.0) + jnp.log1p(jnp.exp(-jnp.abs(x)))


def iota(shape, dim):
    return lax.broadcasted_iota(jnp.int32, shape, dim)


def cols(g, width=GC):
    return pl.ds(pl.multiple_of(g * width, width), width)


class Exchange:
    def __init__(self, n, rows, chunks, x_ref, y_ref, passes, scratch):
        self.n, self.rows, self.chunks = n, rows, chunks
        self.x, self.y, self.passes = x_ref, y_ref, passes
        (self.st, self.rp, self.qs, self.qr, self.pm, self.pp) = scratch[:6]
        (self.ps, self.pr, self.as_, self.ar, self.bs, self.br) = scratch[6:]
        self.me = lax.axis_index("seq")
        self.partner = self.me + 1 - 2 * (self.me % 2)
        self.has_before = self.me >= 2
        self.has_after = self.me < n - 2

    @staticmethod
    def scratch(rows):
        state = pltpu.VMEM((G, 2, rows, STATE, GC), F32)
        small = pltpu.VMEM((8, INNER), F32)
        dma = pltpu.SemaphoreType.DMA
        return [
            state, state, state, state, small, small,
            dma((1,)), dma((1,)), dma((G,)), dma((G,)), dma((2, G)), dma((2, G)),
        ]

    def greet(self):
        barrier = pltpu.get_barrier_semaphore()

        def hello(to):
            pl.semaphore_signal(barrier, inc=1, device_id={"seq": to}, device_id_type=MESH)

        @pl.when(jnp.logical_not(self.has_before))
        def _():
            self.qr[:, 0] = jnp.zeros_like(self.qr[:, 0])

        @pl.when(jnp.logical_not(self.has_after))
        def _():
            self.qr[:, 1] = jnp.zeros_like(self.qr[:, 1])

        hello(self.partner)
        pl.when(self.has_before)(lambda: hello(self.me - 2))
        pl.when(self.has_after)(lambda: hello(self.me + 2))

    def met(self):
        peers = 1 + self.has_before.astype(jnp.int32) + self.has_after.astype(jnp.int32)
        pl.semaphore_wait(pltpu.get_barrier_semaphore(), peers)

    def pass_copy(self):
        return pltpu.make_async_remote_copy(
            self.pm, self.pp, self.ps.at[0], self.pr.at[0],
            device_id={"seq": self.partner}, device_id_type=MESH)

    def pair_copy(self, g):
        return pltpu.make_async_remote_copy(
            self.st.at[g], self.rp.at[g], self.as_.at[g], self.ar.at[g],
            device_id={"seq": self.partner}, device_id_type=MESH)

    def chain_copy(self, d, g):
        return pltpu.make_async_remote_copy(
            self.qs.at[g, d], self.qr.at[g, d], self.bs.at[d, g], self.br.at[d, g],
            device_id={"seq": self.me + 2 if d == 0 else self.me - 2}, device_id_type=MESH)

    def order(self, d):
        return range(self.chunks) if d == 0 else range(self.chunks - 1, -1, -1)

    def passing(self, d, b, where):
        row = 8 * self.passes[d] + b
        return self.p_ref[row : row + 1, where]

    def set_passes(self, p_ref):
        self.p_ref = p_ref

    def totals_of_passes(self):
        self.pm[...] = jnp.zeros_like(self.pm)
        for d in range(2):
            for r in range(self.rows):
                total = None
                for c in self.order(d):
                    one = self.passing(d, r * self.chunks + c, slice(None))
                    total = one if total is None else total * one
                self.pm[d * self.rows + r : d * self.rows + r + 1, :] = total

    def totals(self, g):
        for d in range(2):
            for r in range(self.rows):
                total = None
                for c in self.order(d):
                    b = r * self.chunks + c
                    one = self.x[b, d, :, cols(g)]
                    total = one if total is None else self.passing(d, b, cols(g)) * total + one
                self.st[g, d, r] = total

    def chain(self, d, g):
        has_in, has_out = (
            (self.has_before, self.has_after) if d == 0 else (self.has_after, self.has_before))
        copy = self.chain_copy(d, g)
        pl.when(has_in)(copy.wait_recv)
        first = self.me % 2 == d
        for r in range(self.rows):
            row = d * self.rows + r
            mine, theirs = self.st[g, d, r], self.rp[g, d, r]
            p_mine = self.pm[row : row + 1, cols(g)]
            p_theirs = self.pp[row : row + 1, cols(g)]
            before = self.qr[g, d, r]
            middle = jnp.where(first, p_mine, p_theirs) * before + jnp.where(first, mine, theirs)
            self.qs[g, d, r] = (
                jnp.where(first, p_theirs, p_mine) * middle + jnp.where(first, theirs, mine))
            state = jnp.where(first, before, middle)
            order = list(self.order(d))
            for i, c in enumerate(order):
                b = r * self.chunks + c
                self.y[b, d, :, cols(g)] = state
                if i < len(order) - 1:
                    state = (
                        self.passing(d, b, cols(g)) * state + self.x[b, d, :, cols(g)])
        pl.when(has_out)(copy.start)

    def advance(self, step):
        late = self.n // 2 - 1
        place = self.me // 2

        @pl.when(jnp.logical_and(step >= 1, step < G + 1))
        def _():
            self.pair_copy(step - 1).wait_recv()

        @pl.when(step == 1)
        def _():
            self.pass_copy().wait_recv()

        for d in range(2):
            g = step - 1 - (place if d == 0 else late - place)
            pl.when(jnp.logical_and(g >= 0, g < G))(lambda d=d, g=g: self.chain(d, g))

    def steps(self):
        return G + self.n // 2

    def finish(self):
        self.pass_copy().wait_send()

        @pl.loop(0, G)
        def _(g):
            self.pair_copy(g).wait_send()
            pl.when(self.has_after)(self.chain_copy(0, g).wait_send)
            pl.when(self.has_before)(self.chain_copy(1, g).wait_send)


def pieces(x):
    return [x[:, i * STATE : (i + 1) * STATE] for i in range(4)]


def front_kernel(
    n, rows, length,
    tok, halo, ngain, w, wst, cw, cb, dtb, rate, skip, mask, labcol, sel,
    rounded_o, c_o, p_o, xact_o, y_o, rows_o, q_o, q2_o, pexp_o, sin_o,
    rext, vhi, vlo, gc, sloc, *scratch,
):
    k = pl.program_id(0)
    chunks = length // C
    blocks = rows * chunks
    ex = Exchange(n, rows, chunks, sloc, sin_o, (0, 1), scratch)
    ex.set_passes(pexp_o)

    def convolved(r):
        p = mm(rext[r], w[...])
        p_o[r] = p
        first = PAD - (KW - 1)
        out = cb[...]
        for i in range(KW):
            out = out + cw[i : i + 1, :] * p[first + i : first + i + length]
        c_o[r * length : (r + 1) * length, :] = out
        return out * sigmoid(out)

    @pl.when(k == 0)
    def _():
        ex.greet()
        for r in range(rows):
            here = slice(r * length, (r + 1) * length)
            source = tok[here, :].astype(F32)
            for part, at in ((halo[r], slice(0, PAD)), (source, slice(PAD, PAD + length))):
                scale = lax.rsqrt(jnp.mean(part * part, axis=-1, keepdims=True) + EPS)
                rext[r, at, :] = (part * scale * ngain[...]).astype(BF16)
            rounded_o[here, :] = rext[r, PAD:, :]
            xact_o[here, :] = convolved(r)
        upto = (iota((C, C), 0) <= iota((C, C), 1)).astype(BF16)
        t_id, s_id = iota((C, C), 0), iota((C, C), 1)
        for b in range(blocks):
            here = slice(b * C, (b + 1) * C)
            raw = mm(wst[...], rounded_o[here, :], NT)
            step = softplus(raw + dtb[...])
            log = -LOG2E * rate[...] * step
            total = mm3(log, upto)
            size = jnp.log(step) * LOG2E
            lf, rc = total[:HEADS], total[HEADS:] - log[HEADS:]
            end_f, end_r = total[:HEADS, C - 1 : C], total[HEADS:, C - 1 : C]
            sf, sr = lf - size[:HEADS], rc + size[HEADS:]
            m = mask[b]
            e_f = jnp.exp2(lf) * m[0:1]
            w_f = jnp.exp2(end_f - lf) * step[:HEADS] * m[1:2]
            e_r = jnp.exp2(end_r - rc) * m[2:3]
            w_r = jnp.exp2(rc) * step[HEADS:] * m[3:4]
            none = jnp.zeros((32, C), F32)
            rows_o[b] = jnp.concatenate([step, lf, rc, sf, sr, raw], axis=0)
            q = jnp.concatenate([e_f, w_f, e_r, w_r, none], axis=0).T
            q_o[b] = q
            q2_o[b] = jnp.concatenate([lf, rc, sf, sr, none], axis=0).T
            pexp_o[b : b + 1, :] = mm3(q[C - 8 :], sel[0])[7:8]
            pexp_o[8 + b : 9 + b, :] = mm3(q[:8], sel[2])[0:1]
            in_f, in_r, rd_f, rd_r = pieces(xact_o[here, :])
            gf, gr = mm22(rd_f, in_f, NT), mm22(rd_r, in_r, NT)
            same = jnp.logical_and(labcol[b] == m[6:7], t_id != s_id)
            gc[b] = jnp.where(same, jnp.where(t_id > s_id, gf, gr), 0.0)
        ex.totals_of_passes()

    @pl.when(jnp.logical_and(k >= 1, k <= G))
    def _():
        g = k - 1
        for r in range(rows):
            v = convolved(r)
            hi, lo = split2(v)
            vhi[g, r * length : (r + 1) * length, :] = hi
            vlo[g, r * length : (r + 1) * length, :] = lo
            for c in range(chunks):
                b = r * chunks + c
                vb = v[c * C : (c + 1) * C]
                x = xact_o[b * C : (b + 1) * C, :].astype(BF16)
                for d in range(2):
                    scale = mm2(q_o[b], sel[2 * d + 1, :, cols(g)])
                    sloc[b, d, :, cols(g)] = mm(
                        x[:, d * STATE : (d + 1) * STATE], (scale * vb).astype(BF16), TN)
        ex.totals(g)

        @pl.when(g == 0)
        def _():
            ex.met()
            ex.pass_copy().start()

        ex.pair_copy(g).start()

    @pl.when(k > 0)
    def _():
        ex.advance(k - 1)

    @pl.when(jnp.logical_and(k > G, k <= 2 * G))
    def _():
        g = k - 1 - G
        later = iota((C, C), 0) > iota((C, C), 1)
        low = iota((C, 128), 1) < HEAD
        for b in range(blocks):
            here = slice(b * C, (b + 1) * C)
            q2 = pltpu.roll(q2_o[b], 128 - HG * g, 1)
            for pair in range(HG // 2):
                at = slice(pair * 128, (pair + 1) * 128)
                v2 = jnp.concatenate([vhi[g, here, at], vlo[g, here, at]], axis=1)
                outs = []
                for h in (2 * pair, 2 * pair + 1):
                    lt, rt = q2[:, h : h + 1], q2[:, HEADS + h : HEADS + h + 1]
                    ls = rows_o[b, pl.ds(96 + HG * g + h, 1), :]
                    rs = rows_o[b, pl.ds(96 + HEADS + HG * g + h, 1), :]
                    x = jnp.exp2(jnp.where(later, lt - ls, rs - rt))
                    o = mm((gc[b] * x).astype(BF16), v2)
                    outs.append(o[:, :128] + o[:, 128:])
                v = vhi[g, here, at].astype(F32) + vlo[g, here, at].astype(F32)
                y_o[here, at] = jnp.where(low, outs[0], outs[1]) + skip[:, at] * v

    @pl.when(k == pl.num_programs(0) - 1)
    def _():
        ex.finish()


def middle_kernel(
    y, rounded, tok, cot, q, xact, sin, wg, wo, ogain, sel,
    mixed_o, dy_o, dgate_o, ds_o, dread_o, dq_o, wo_grad, ogain_grad, wg_grad,
):
    k = pl.program_id(0)
    x = xact[...].astype(BF16)
    rd_f, rd_r = x[:, 2 * STATE : 3 * STATE], x[:, 3 * STATE :]
    s_f, s_r = sin[0, 0].astype(BF16), sin[0, 1].astype(BF16)
    e_f, e_r = mm2(q[0], sel[0]), mm2(q[0], sel[2])
    r_f, r_r = mm(rd_f, s_f), mm(rd_r, s_r)
    yv = y[...] + e_f * r_f + e_r * r_r
    gate = mm(rounded[...], wg[...])
    sg = sigmoid(gate)
    silu = gate * sg
    gated = yv * silu
    scale = lax.rsqrt(jnp.mean(gated * gated, axis=-1, keepdims=True) + EPS)
    normed = gated * scale
    out = (normed * ogain[...]).astype(BF16)
    mixed_o[...] = (tok[...].astype(F32) + mm(out, wo[...])).astype(BF16)
    dout = mm(cot[...], wo[...], NT)
    go = jnp.sum(dout * normed, axis=0, keepdims=True)
    dn = dout * ogain[...]
    dgated = scale * (dn - normed * jnp.mean(dn * normed, axis=-1, keepdims=True))
    dy = dgated * silu
    dy_o[...] = dy
    dgate = (dgated * yv * sg * (1.0 + gate * (1.0 - sg))).astype(BF16)
    dgate_o[...] = dgate
    u_f, u_r = e_f * dy, e_r * dy
    dq_o[0] = mm2(u_f * r_f, sel[0], NT) + mm2(u_r * r_r, sel[2], NT)
    u_f, u_r = u_f.astype(BF16), u_r.astype(BF16)
    ds_o[0, 1] = mm(rd_f, u_f, TN)
    ds_o[0, 0] = mm(rd_r, u_r, TN)
    dread_o[...] = jnp.concatenate([mm(u_f, s_f, NT), mm(u_r, s_r, NT)], axis=1)

    @pl.when(k == 0)
    def _():
        wo_grad[...] = mm(out, cot[...], TN)
        wg_grad[...] = mm(rounded[...], dgate, TN)
        ogain_grad[...] = jnp.broadcast_to(go, ogain_grad.shape)

    @pl.when(k > 0)
    def _():
        wo_grad[...] += mm(out, cot[...], TN)
        wg_grad[...] += mm(rounded[...], dgate, TN)
        ogain_grad[...] += go


def back_kernel(
    n, rows, length, far,
    c_i, dy_i, xact, cx, rows_i, q_i, q2_i, pexp, sin, ds, dread, dq_i, mask, labcol, dtb, rate, skip, sel,
    dc_o, draw_o, skip_o, small_o,
    gct, dgt, dvs, dss, dts, dqs, dins, pgs, z, *scratch,
):
    k = pl.program_id(0)
    chunks = length // C
    blocks = rows * chunks
    ex = Exchange(n, rows, chunks, ds, z, (1, 0), scratch)
    ex.set_passes(pexp)
    later = iota((C, C), 1) > iota((C, C), 0)

    @pl.when(k == 0)
    def _():
        ex.greet()
        ex.totals_of_passes()

        @pl.loop(0, G)
        def _(g):
            ex.totals(g)

        ex.met()
        ex.pass_copy().start()

        @pl.loop(0, G)
        def _(g):
            ex.pair_copy(g).start()

        differ = iota((C, C), 0) != iota((C, C), 1)
        for b in range(blocks):
            in_f, in_r, rd_f, rd_r = pieces(xact[b * C : (b + 1) * C, :])
            gf, gr = mm22(in_f, rd_f, NT), mm22(in_r, rd_r, NT)
            same = jnp.logical_and(labcol[b] == mask[b, 6:7], differ)
            gct[b] = jnp.where(same, jnp.where(later, gf, gr), 0.0)
        dgt[...] = jnp.zeros_like(dgt)
        dss[...] = jnp.zeros_like(dss)
        dins[...] = jnp.zeros_like(dins)
        pgs[...] = jnp.zeros_like(pgs)
        dqs[...] = dq_i[...]

    @pl.when(k < G)
    def _():
        g = k
        low = iota((C, 128), 1) < HEAD
        lane = iota((C, 128), 1)
        ones = jnp.ones((8, C), BF16)
        skips = jnp.zeros((1, GC), F32)
        for b in range(blocks):
            here = slice(b * C, (b + 1) * C)
            q2 = pltpu.roll(q2_i[b], 128 - HG * g, 1)
            cv = c_i[here, :]
            v = cv * sigmoid(cv)
            dy = dy_i[here, :]
            skips += jnp.sum(dy * v, axis=0, keepdims=True)
            dyhi, dylo = split2(dy)
            vb = v.astype(BF16)
            for pair in range(HG // 2):
                at = slice(pair * 128, (pair + 1) * 128)
                dy2 = jnp.concatenate([dyhi[:, at], dylo[:, at]], axis=1)
                outs = []
                for i in range(2):
                    h = 2 * pair + i
                    mine = low if i == 0 else jnp.logical_not(low)
                    dyh = jnp.where(mine, dyhi[:, at], jnp.zeros((), BF16))
                    dw = mm(vb[:, at], dyh, NT)
                    lt = rows_i[b, pl.ds(48 + HG * g + h, 1), :]
                    rt = rows_i[b, pl.ds(48 + HEADS + HG * g + h, 1), :]
                    ls, rs = q2[:, 48 + h : 49 + h], q2[:, 72 + h : 73 + h]
                    x = jnp.exp2(jnp.where(later, lt - ls, rs - rt))
                    dwx = dw * x
                    dgt[b] += dwx
                    gb = gct[b]
                    o = mm((gb * x).astype(BF16), dy2)
                    outs.append(o[:, :128] + o[:, 128:])
                    de = dwx * gb
                    de_f = jnp.where(later, de, 0.0).astype(BF16)
                    de_r = jnp.where(later, 0.0, de).astype(BF16)
                    hot_f = (lane == HG * g + h).astype(BF16)
                    hot_r = (lane == HEADS + HG * g + h).astype(BF16)
                    dss[b] += mm(de_f, hot_f) + mm(de_r, hot_r)
                    dts[b, pl.ds(HG * g + h, 1), :] = mm(ones, de_f)[0:1]
                    dts[b, pl.ds(HEADS + HG * g + h, 1), :] = mm(ones, de_r)[0:1]
                dvs[g, here, at] = jnp.where(low, outs[0], outs[1]) + skip[:, at] * dy[:, at]
        skip_o[...] = jnp.broadcast_to(skips, skip_o.shape)

    ex.advance(k)

    @pl.when(jnp.logical_and(k >= far, k < far + G))
    def _():
        g = k - far
        for b in range(blocks):
            here = slice(b * C, (b + 1) * C)
            cv = c_i[here, :]
            sg = sigmoid(cv)
            v = cv * sg
            x = xact[here, :].astype(BF16)
            dv = dvs[g, here, :]
            for d in range(2):
                zf = z[b, 1 - d, :, cols(g)]
                zb = zf.astype(BF16)
                pick = sel[2 * d + 1, :, cols(g)]
                weight = mm2(q_i[b], pick)
                m = mm(x[:, d * STATE : (d + 1) * STATE], zb)
                dv += weight * m
                u = weight * v
                dqs[b] += mm2(u * m, pick, NT)
                at = slice(d * STATE, (d + 1) * STATE)
                dins[b, :, at] += mm(u.astype(BF16), zb, NT)
                pgs[8 * d + b : 8 * d + b + 1, cols(g)] = pexp[
                    8 * d + b : 8 * d + b + 1, cols(g)
                ] * jnp.sum(zf * sin[b, d, :, cols(g)], axis=0, keepdims=True)
            dc_o[here, :] = dv * (sg * (1.0 + cv * (1.0 - sg)))

    @pl.when(k == far + G)
    def _():
        ex.finish()
        differ = iota((C, C), 0) != iota((C, C), 1)
        from_t = (iota((C, C), 0) >= iota((C, C), 1)).astype(BF16)
        after_t = (iota((C, C), 0) > iota((C, C), 1)).astype(BF16)
        pg_f, pg_r = mm22(sel[0].astype(F32), pgs[0:8], NT), mm22(sel[2].astype(F32), pgs[8:16], NT)
        sums = jnp.zeros((2 * HEADS, 128), F32)
        for b in range(blocks):
            here = slice(b * C, (b + 1) * C)
            same = jnp.logical_and(labcol[b] == mask[b, 6:7], differ)
            dg = jnp.where(same, dgt[b], 0.0)
            dg_f = jnp.where(later, dg, 0.0).astype(BF16)
            dg_r = jnp.where(later, 0.0, dg).astype(BF16)
            in_f, in_r, rd_f, rd_r = pieces(xact[here, :].astype(BF16))
            dx = jnp.concatenate(
                [
                    dins[b, :, :STATE] + mm(dg_f, rd_f),
                    dins[b, :, STATE:] + mm(dg_r, rd_r),
                    dread[here, :STATE] + mm(dg_f, in_f, TN),
                    dread[here, STATE:] + mm(dg_r, in_r, TN),
                ],
                axis=1,
            )
            cv = cx[here, :]
            sg = sigmoid(cv)
            dc_o[here, :] = dx * (sg * (1.0 + cv * (1.0 - sg)))
            dq, col, row = dqs[b].T, dss[b].T, dts[b]
            e_f, w_f, e_r, w_r = [dq[i * HEADS : (i + 1) * HEADS] for i in range(4)]
            cs_f, cs_r = col[:HEADS], col[HEADS : 2 * HEADS]
            d_lf = row[:HEADS] - cs_f + e_f - w_f
            d_rc = cs_r - row[HEADS:] - e_r + w_r
            d_size = jnp.concatenate([cs_f + w_f, cs_r + w_r], axis=0)
            end_f = jnp.sum(w_f, axis=1, keepdims=True) + pg_f[:HEADS, b : b + 1]
            end_r = jnp.sum(e_r, axis=1, keepdims=True) + pg_r[2 * HEADS : 3 * HEADS, b : b + 1]
            d_log = jnp.concatenate(
                [mm3(d_lf, from_t) + end_f, mm3(d_rc, after_t) + end_r], axis=0)
            step, raw = rows_i[b, 0:48], rows_i[b, 144:192] + dtb[...]
            sg = sigmoid(raw)
            ratio = jnp.where(raw < -15.0, 1.0, sg / jnp.maximum(step, 1e-30))
            d_raw = -rate[...] * d_log * sg + d_size * ratio
            draw_o[:, here] = d_raw.astype(BF16)
            bias = jnp.sum(d_raw, axis=1, keepdims=True)
            rates = -jnp.sum(step * d_log, axis=1, keepdims=True)
            at = iota((2 * HEADS, 128), 1)
            sums += jnp.where(at == 0, bias, jnp.where(at == 1, rates, 0.0))
        small_o[...] = sums


def last_kernel(
    rows, length,
    dc, halo, p_i, dgate, draw, rounded, tok, cot, ngain, cw, w, wst,
    tg_o, wc_grad, ws_grad, cw_grad, cb_grad, ng_grad,
    acc,
):
    k = pl.program_id(0)
    groups = CONV // GC

    @pl.when(k == 0)
    def _():
        acc[...] = mm(draw[...], wst[...], TN)
        ws_grad[...] = mm(draw[...], rounded[...])

    @pl.when(k < groups)
    def _():
        parts = []
        taps = [jnp.zeros((1, GC), F32) for _ in range(KW)]
        bias = jnp.zeros((1, GC), F32)
        for r in range(rows):
            own = dc[r * length : (r + 1) * length, :]
            ext = jnp.concatenate([own, halo[r]], axis=0)
            total = None
            for i in range(KW):
                one = cw[i : i + 1, :] * ext[KW - 1 - i : KW - 1 - i + length]
                total = one if total is None else total + one
                first = PAD - (KW - 1) + i
                taps[i] += jnp.sum(own * p_i[r, first : first + length, :], axis=0, keepdims=True)
            bias += jnp.sum(own, axis=0, keepdims=True)
            parts.append(total.astype(BF16))
        both = jnp.concatenate(parts, axis=0)
        wc_grad[...] = mm(rounded[...], both, TN)
        acc[...] += mm(both, w[...], NT)
        cw_grad[...] = jnp.concatenate(taps + [jnp.zeros((4, GC), F32)], axis=0)
        cb_grad[...] = jnp.broadcast_to(bias, cb_grad.shape)

    @pl.when(k >= groups)
    def _():
        acc[...] += mm(dgate[...], w[...], NT)

    @pl.when(k == groups + G - 1)
    def _():
        gains = jnp.zeros((1, D), F32)
        for b in range(rows * length // C):
            here = slice(b * C, (b + 1) * C)
            source = tok[here, :].astype(F32)
            scale = lax.rsqrt(jnp.mean(source * source, axis=-1, keepdims=True) + EPS)
            m = source * scale
            d_rounded = acc[here, :]
            gains += jnp.sum(d_rounded * m, axis=0, keepdims=True)
            nn = d_rounded * ngain[...]
            d_source = scale * (nn - m * jnp.mean(nn * m, axis=-1, keepdims=True))
            tg_o[here, :] = (cot[here, :].astype(F32) + d_source).astype(BF16)
        ng_grad[...] = jnp.broadcast_to(gains, ng_grad.shape)


def selectors():
    lane = lax.broadcasted_iota(jnp.int32, (4, 128, INNER), 1)
    kind = lax.broadcasted_iota(jnp.int32, (4, 128, INNER), 0)
    head = lax.broadcasted_iota(jnp.int32, (4, 128, INNER), 2) // HEAD
    return (lane == kind * HEADS + head).astype(BF16)


def shifted(value, axis, steps):
    count = lax.axis_size(axis)
    leading, last = max(0, -steps), min(count, count - steps)
    return lax.ppermute(value, axis, [(i, i + steps) for i in range(leading, last)])


def whole(shape):
    zeros = (0,) * len(shape)
    return pl.BlockSpec(shape, lambda k: zeros)


def struct(shape, dtype=F32):
    return jax.ShapeDtypeStruct(shape, dtype)


def on_device(
    tokens, doc_starts, norm_gain, in_weight, conv_weight, conv_bias, dt_bias, decay_rate,
    skip_scale, out_gain, out_weight, cotangent,
):
    n = lax.axis_size("seq")
    rows, length, _ = tokens.shape
    chunks = length // C
    blocks = rows * chunks
    count = rows * length
    place = lax.axis_index("seq")

    positions = place * length - 1 + jnp.arange(length + 2, dtype=jnp.int32)
    labels = jnp.sum(
        (doc_starts[:, None, :] <= positions[None, :, None]).astype(F32), axis=-1)
    own = labels[:, 1 : length + 1].reshape(blocks, C)
    before = labels[:, :length].reshape(blocks, C)[:, :1]
    after = labels[:, 2:].reshape(blocks, C)[:, C - 1 :]
    mask = jnp.stack(
        [
            (own == before).astype(F32),
            (own == own[:, C - 1 :]).astype(F32),
            (own == after).astype(F32),
            (own == own[:, :1]).astype(F32),
            own, own, own, own,
        ],
        axis=1,
    )
    labcol = own[:, :, None]
    sel = selectors()
    skip = jnp.repeat(skip_scale, HEAD)[None, :]
    wst = in_weight[:, 2 * INNER + 4 * STATE :].T
    cb = conv_bias[None, :]
    dtb, rate = dt_bias[:, None], decay_rate[:, None]
    ngain, ogain = norm_gain[None, :], out_gain[None, :]
    tok, cot = tokens.reshape(count, D), cotangent.reshape(count, D)
    rim = shifted(tokens[:, length - 8 :].astype(F32), "seq", 1)
    keep = (jnp.arange(8) >= 8 - (KW - 1)).astype(F32)[None, :, None]
    halo = jnp.pad(rim * keep, ((0, 0), (PAD - 8, 0), (0, 0)))

    params = dict(vmem_limit_bytes=VMEM_LIMIT)
    dims = ("arbitrary",)

    def col(k):
        return jnp.where(k == 0, G, jnp.minimum(k - 1, G - 1))

    def ycol(k):
        return jnp.clip(k - 1 - G, 0, G - 1)

    front_steps = max(2 * G, G + n // 2) + 1
    rounded, c, p, xact, y, rowsv, q, q2, pexp, sin = pl.pallas_call(
        lambda *refs: front_kernel(n, rows, length, *refs),
        grid=(front_steps,),
        in_specs=[
            whole((count, D)), whole((rows, PAD, D)), whole((1, D)),
            pl.BlockSpec((D, GC), lambda k: (0, G + col(k))),
            whole((2 * HEADS, D)),
            pl.BlockSpec((KW, GC), lambda k: (0, col(k))),
            pl.BlockSpec((1, GC), lambda k: (0, col(k))),
            whole((2 * HEADS, 1)), whole((2 * HEADS, 1)),
            pl.BlockSpec((1, GC), lambda k: (0, ycol(k))),
            whole((blocks, 8, C)), whole((blocks, C, 1)), whole((4, 128, INNER)),
        ],
        out_specs=[
            whole((count, D)),
            pl.BlockSpec((count, GC), lambda k: (0, col(k))),
            pl.BlockSpec((rows, PAD + length, GC), lambda k: (0, 0, col(k))),
            whole((count, GC)),
            pl.BlockSpec((count, GC), lambda k: (0, ycol(k))),
            whole((blocks, 192, C)), whole((blocks, C, 128)), whole((blocks, C, 128)),
            whole((16, INNER)), whole((blocks, 2, STATE, INNER)),
        ],
        out_shape=[
            struct((count, D), BF16), struct((count, CONV)), struct((rows, PAD + length, CONV)),
            struct((count, GC)), struct((count, INNER)), struct((blocks, 192, C)),
            struct((blocks, C, 128)), struct((blocks, C, 128)), struct((16, INNER)),
            struct((blocks, 2, STATE, INNER)),
        ],
        scratch_shapes=[
            pltpu.VMEM((rows, PAD + length, D), BF16),
            pltpu.VMEM((G, count, GC), BF16), pltpu.VMEM((G, count, GC), BF16),
            pltpu.VMEM((blocks, C, C), F32), pltpu.VMEM((blocks, 2, STATE, INNER), F32),
            *Exchange.scratch(rows),
        ],
        compiler_params=pltpu.CompilerParams(
            dimension_semantics=dims, collective_id=0, has_side_effects=True, **params),
        name="front",
    )(tok, halo, ngain, in_weight, wst, conv_weight, cb, dtb, rate, skip, mask, labcol, sel)

    def by_block(shape):
        zeros = (0,) * (len(shape) - 1)
        return pl.BlockSpec(shape, lambda k: (k,) + zeros)

    mixed, dy, dgate, ds, dread, dq, wo_grad, ogain_grad, wg_grad = pl.pallas_call(
        middle_kernel,
        grid=(blocks,),
        in_specs=[
            by_block((C, INNER)), by_block((C, D)), by_block((C, D)), by_block((C, D)),
            by_block((1, C, 128)), by_block((C, GC)), by_block((1, 2, STATE, INNER)),
            whole((D, INNER)), whole((INNER, D)), whole((1, INNER)), whole((4, 128, INNER)),
        ],
        out_specs=[
            by_block((C, D)), by_block((C, INNER)), by_block((C, INNER)),
            by_block((1, 2, STATE, INNER)), by_block((C, 128)), by_block((1, C, 128)),
            whole((INNER, D)), whole((8, INNER)), whole((D, INNER)),
        ],
        out_shape=[
            struct((count, D), BF16), struct((count, INNER)), struct((count, INNER), BF16),
            struct((blocks, 2, STATE, INNER)), struct((count, 128)), struct((blocks, C, 128)),
            struct((INNER, D)), struct((8, INNER)), struct((D, INNER)),
        ],
        compiler_params=pltpu.CompilerParams(dimension_semantics=dims, **params),
        name="middle",
    )(y, rounded, tok, cot, q, xact, sin, in_weight, out_weight, ogain, sel)

    far = max(G, n // 2 + 1)

    def vcol(k):
        return jnp.where(k < far, jnp.minimum(k, G - 1), jnp.minimum(k - far, G - 1))

    def first_pass(k):
        return jnp.minimum(k, G - 1)

    def second_pass(k):
        return jnp.clip(k - far, 0, G)

    dc, draw, skips, small = pl.pallas_call(
        lambda *refs: back_kernel(n, rows, length, far, *refs),
        grid=(far + G + 1,),
        in_specs=[
            pl.BlockSpec((count, GC), lambda k: (0, vcol(k))),
            pl.BlockSpec((count, GC), lambda k: (0, first_pass(k))),
            whole((count, GC)),
            pl.BlockSpec((count, GC), lambda k: (0, G)),
            whole((blocks, 192, C)), whole((blocks, C, 128)), whole((blocks, C, 128)),
            whole((16, INNER)), whole((blocks, 2, STATE, INNER)),
            whole((blocks, 2, STATE, INNER)), whole((count, 128)), whole((blocks, C, 128)),
            whole((blocks, 8, C)), whole((blocks, C, 1)),
            whole((2 * HEADS, 1)), whole((2 * HEADS, 1)),
            pl.BlockSpec((1, GC), lambda k: (0, first_pass(k))),
            whole((4, 128, INNER)),
        ],
        out_specs=[
            pl.BlockSpec((count, GC), lambda k: (0, second_pass(k))),
            whole((2 * HEADS, count)),
            pl.BlockSpec((8, GC), lambda k: (0, first_pass(k))),
            whole((2 * HEADS, 128)),
        ],
        out_shape=[
            struct((count, CONV)), struct((2 * HEADS, count), BF16), struct((8, INNER)),
            struct((2 * HEADS, 128)),
        ],
        scratch_shapes=[
            pltpu.VMEM((blocks, C, C), F32), pltpu.VMEM((blocks, C, C), F32),
            pltpu.VMEM((G, count, GC), F32), pltpu.VMEM((blocks, C, 128), F32),
            pltpu.VMEM((blocks, 2 * HEADS, C), F32), pltpu.VMEM((blocks, C, 128), F32),
            pltpu.VMEM((blocks, C, 128), F32), pltpu.VMEM((16, INNER), F32),
            pltpu.VMEM((blocks, 2, STATE, INNER), F32),
            *Exchange.scratch(rows),
        ],
        compiler_params=pltpu.CompilerParams(
            dimension_semantics=dims, collective_id=1, has_side_effects=True, **params),
        name="back",
    )(c, dy, xact, c, rowsv, q, q2, pexp, sin, ds, dread, dq, mask, labcol, dtb, rate, skip, sel)

    spill = shifted(dc.reshape(rows, length, CONV)[:, :8], "seq", -1)
    groups = CONV // GC

    def conv_col(k):
        return jnp.minimum(k, groups - 1)

    tg, wc_grad, ws_grad, cw_grad, cb_grad, ng_grad = pl.pallas_call(
        lambda *refs: last_kernel(rows, length, *refs),
        grid=(groups + G,),
        in_specs=[
            pl.BlockSpec((count, GC), lambda k: (0, conv_col(k))),
            pl.BlockSpec((rows, 8, GC), lambda k: (0, 0, conv_col(k))),
            pl.BlockSpec((rows, PAD + length, GC), lambda k: (0, 0, conv_col(k))),
            pl.BlockSpec((count, GC), lambda k: (0, jnp.clip(k - groups, 0, G - 1))),
            whole((2 * HEADS, count)), whole((count, D)), whole((count, D)), whole((count, D)),
            whole((1, D)),
            pl.BlockSpec((KW, GC), lambda k: (0, conv_col(k))),
            pl.BlockSpec((D, GC), lambda k: (0, jnp.where(k < groups, G + k, k - groups))),
            whole((2 * HEADS, D)),
        ],
        out_specs=[
            whole((count, D)),
            pl.BlockSpec((D, GC), lambda k: (0, conv_col(k))),
            whole((2 * HEADS, D)),
            pl.BlockSpec((8, GC), lambda k: (0, conv_col(k))),
            pl.BlockSpec((8, GC), lambda k: (0, conv_col(k))),
            whole((8, D)),
        ],
        out_shape=[
            struct((count, D), BF16), struct((D, CONV)), struct((2 * HEADS, D)),
            struct((8, CONV)), struct((8, CONV)), struct((8, D)),
        ],
        scratch_shapes=[pltpu.VMEM((count, D), F32)],
        compiler_params=pltpu.CompilerParams(dimension_semantics=dims, **params),
        name="last",
    )(dc, spill, p, dgate, draw, rounded, tok, cot, ngain, conv_weight, in_weight, wst)

    in_weight_grad = jnp.concatenate([wg_grad, wc_grad, ws_grad.T], axis=1)
    totals = lax.psum(
        (
            ng_grad[0], in_weight_grad, cw_grad[:KW], cb_grad[0], small[:, 0], small[:, 1],
            jnp.sum(skips[0].reshape(HEADS, HEAD), axis=1), ogain_grad[0], wo_grad,
        ),
        ("rows", "seq"),
    )
    return (mixed.reshape(tokens.shape), tg.reshape(tokens.shape)) + totals


def solution(mesh):
    local = P("rows", "seq", None)
    return jax.shard_map(
        on_device,
        mesh=mesh,
        in_specs=(local, P("rows", None)) + (P(),) * 9 + (local,),
        out_specs=(local, local) + (P(),) * 9,
        check_vma=False,
    )
```

```python
import jax
import jax.numpy as jnp
from jax import lax
from jax.experimental import pallas as pl
from jax.experimental.pallas import tpu as pltpu
from jax.sharding import PartitionSpec as P

D = 768
INNER = 1536
HEADS = 24
HEAD = 64
STATE = 64
KW = 4
EPS = 1e-05

C = 256
GC = 256
G = INNER // GC
HG = GC // HEAD
CONV = INNER + 4 * STATE
PAD = 16
LOG2E = 1.4426950408889634
F32, BF16 = jnp.float32, jnp.bfloat16
NN, NT, TN = ((1,), (0,)), ((1,), (1,)), ((0,), (0,))
MESH = pl.DeviceIdType.MESH
VMEM_LIMIT = 60 * 1024 * 1024


def mm(a, b, dims=NN):
    return lax.dot_general(a, b, (dims, ((), ())), preferred_element_type=F32)


def split2(a):
    hi = a.astype(BF16)
    return hi, (a - hi.astype(F32)).astype(BF16)


def split3(a):
    hi = a.astype(BF16)
    rest = a - hi.astype(F32)
    mid = rest.astype(BF16)
    return hi, mid, (rest - mid.astype(F32)).astype(BF16)


def mm2(a, b, dims=NN):
    hi, lo = split2(a)
    return mm(hi, b, dims) + mm(lo, b, dims)


def mm3(a, b, dims=NN):
    hi, mid, lo = split3(a)
    return mm(hi, b, dims) + mm(mid, b, dims) + mm(lo, b, dims)


def mm22(a, b, dims=NN):
    ahi, alo = split2(a)
    bhi, blo = split2(b)
    return mm(ahi, bhi, dims) + mm(alo, bhi, dims) + mm(ahi, blo, dims)


def sigmoid(x):
    return 1.0 / (1.0 + jnp.exp(-x))


def softplus(x):
    return jnp.maximum(x, 0.0) + jnp.log1p(jnp.exp(-jnp.abs(x)))


def iota(shape, dim):
    return lax.broadcasted_iota(jnp.int32, shape, dim)


def cols(g, width=GC):
    return pl.ds(pl.multiple_of(g * width, width), width)


class Exchange:
    def __init__(self, n, rows, chunks, x_ref, y_ref, passes, scratch):
        self.n, self.rows, self.chunks = n, rows, chunks
        self.x, self.y, self.passes = x_ref, y_ref, passes
        (self.st, self.rp, self.qs, self.qr, self.pm, self.pp) = scratch[:6]
        (self.ps, self.pr, self.as_, self.ar, self.bs, self.br) = scratch[6:]
        self.me = lax.axis_index("seq")
        self.partner = self.me + 1 - 2 * (self.me % 2)
        self.has_before = self.me >= 2
        self.has_after = self.me < n - 2

    @staticmethod
    def scratch(rows):
        state = pltpu.VMEM((G, 2, rows, STATE, GC), F32)
        small = pltpu.VMEM((8, INNER), F32)
        dma = pltpu.SemaphoreType.DMA
        return [
            state, state, state, state, small, small,
            dma((1,)), dma((1,)), dma((G,)), dma((G,)), dma((2, G)), dma((2, G)),
        ]

    def clear(self):
        @pl.when(jnp.logical_not(self.has_before))
        def _():
            self.qr[:, 0] = jnp.zeros_like(self.qr[:, 0])

        @pl.when(jnp.logical_not(self.has_after))
        def _():
            self.qr[:, 1] = jnp.zeros_like(self.qr[:, 1])

    def greet(self):
        barrier = pltpu.get_barrier_semaphore()

        def hello(to):
            pl.semaphore_signal(barrier, inc=1, device_id={"seq": to}, device_id_type=MESH)

        hello(self.partner)
        pl.when(self.has_before)(lambda: hello(self.me - 2))
        pl.when(self.has_after)(lambda: hello(self.me + 2))

    def met(self):
        peers = 1 + self.has_before.astype(jnp.int32) + self.has_after.astype(jnp.int32)
        pl.semaphore_wait(pltpu.get_barrier_semaphore(), peers)

    def pass_copy(self):
        return pltpu.make_async_remote_copy(
            self.pm, self.pp, self.ps.at[0], self.pr.at[0],
            device_id={"seq": self.partner}, device_id_type=MESH)

    def pair_copy(self, g):
        return pltpu.make_async_remote_copy(
            self.st.at[g], self.rp.at[g], self.as_.at[g], self.ar.at[g],
            device_id={"seq": self.partner}, device_id_type=MESH)

    def chain_copy(self, d, g):
        return pltpu.make_async_remote_copy(
            self.qs.at[g, d], self.qr.at[g, d], self.bs.at[d, g], self.br.at[d, g],
            device_id={"seq": self.me + 2 if d == 0 else self.me - 2}, device_id_type=MESH)

    def order(self, d):
        return range(self.chunks) if d == 0 else range(self.chunks - 1, -1, -1)

    def passing(self, d, b, where):
        row = 8 * self.passes[d] + b
        return self.p_ref[row : row + 1, where]

    def set_passes(self, p_ref):
        self.p_ref = p_ref

    def totals_of_passes(self):
        self.pm[...] = jnp.zeros_like(self.pm)
        for d in range(2):
            for r in range(self.rows):
                total = None
                for c in self.order(d):
                    one = self.passing(d, r * self.chunks + c, slice(None))
                    total = one if total is None else total * one
                self.pm[d * self.rows + r : d * self.rows + r + 1, :] = total

    def totals(self, g):
        for d in range(2):
            for r in range(self.rows):
                total = None
                for c in self.order(d):
                    b = r * self.chunks + c
                    one = self.x[b, d, :, cols(g)]
                    total = one if total is None else self.passing(d, b, cols(g)) * total + one
                self.st[g, d, r] = total

    def chain(self, d, g):
        has_in, has_out = (
            (self.has_before, self.has_after) if d == 0 else (self.has_after, self.has_before))
        copy = self.chain_copy(d, g)
        pl.when(has_in)(copy.wait_recv)
        first = self.me % 2 == d
        for r in range(self.rows):
            row = d * self.rows + r
            mine, theirs = self.st[g, d, r], self.rp[g, d, r]
            p_mine = self.pm[row : row + 1, cols(g)]
            p_theirs = self.pp[row : row + 1, cols(g)]
            before = self.qr[g, d, r]
            middle = jnp.where(first, p_mine, p_theirs) * before + jnp.where(first, mine, theirs)
            self.qs[g, d, r] = (
                jnp.where(first, p_theirs, p_mine) * middle + jnp.where(first, theirs, mine))
            state = jnp.where(first, before, middle)
            order = list(self.order(d))
            for i, c in enumerate(order):
                b = r * self.chunks + c
                self.y[b, d, :, cols(g)] = state
                if i < len(order) - 1:
                    state = (
                        self.passing(d, b, cols(g)) * state + self.x[b, d, :, cols(g)])
        pl.when(has_out)(copy.start)

    def advance(self, step):
        late = self.n // 2 - 1
        place = self.me // 2

        @pl.when(jnp.logical_and(step >= 1, step < G + 1))
        def _():
            self.pair_copy(step - 1).wait_recv()

        @pl.when(step == 1)
        def _():
            self.pass_copy().wait_recv()

        for d in range(2):
            g = step - 1 - (place if d == 0 else late - place)
            pl.when(jnp.logical_and(g >= 0, g < G))(lambda d=d, g=g: self.chain(d, g))

    def steps(self):
        return G + self.n // 2

    def finish(self):
        self.pass_copy().wait_send()

        @pl.loop(0, G)
        def _(g):
            self.pair_copy(g).wait_send()
            pl.when(self.has_after)(self.chain_copy(0, g).wait_send)
            pl.when(self.has_before)(self.chain_copy(1, g).wait_send)


PIECE = 256


class Reduce:
    STAGES = 8

    def __init__(self, count, half, scratch, out, far):
        self.count, self.half, self.out, self.far = count, half, out, far
        (self.acc, self.r0, self.r1, self.r2, self.r3, self.send, self.recv, self.local) = scratch
        rows, seq = lax.axis_index("rows"), lax.axis_index("seq")
        self.y, self.core, self.z, self.x = rows // 2, rows % 2, seq // 2, seq % 2

    @staticmethod
    def scratch(count):
        def slot(*shape):
            return pltpu.VMEM((count,) + shape + (D,), F32)

        dma = pltpu.SemaphoreType.DMA
        return [
            slot(128), slot(128), slot(64), slot(32), slot(3, 8),
            dma((12, count)), dma((12, count)), dma((2, count)),
        ]

    def device(self, x, y, z, core):
        return {"rows": y * 2 + core, "seq": z * 2 + x}

    def peers(self):
        x, y, z, core = self.x, self.y, self.z, self.core
        return [(x, y, z, 1 - core), (1 - x, y, z, core), (x, 1 - y, z, core)] + [
            (x, y, lax.rem(z + d, 4), core) for d in (1, 2, 3)]

    def greet(self):
        for peer in self.peers():
            pl.semaphore_signal(
                pltpu.get_barrier_semaphore(), inc=1, device_id=self.device(*peer),
                device_id_type=MESH)

    def met(self):
        pl.semaphore_wait(pltpu.get_barrier_semaphore(), 6)

    def turn(self, p):
        odd = lax.rem(p, 2)
        x, y, z, core = self.x, self.y, self.z, self.core
        a = jnp.where(odd == 0, x, y)
        b = jnp.where(odd == 0, y, x)
        flip_x, flip_y = (1 - x, y, z, core), (x, 1 - y, z, core)
        one = tuple(jnp.where(odd == 0, i, j) for i, j in zip(flip_x, flip_y))
        two = tuple(jnp.where(odd == 0, i, j) for i, j in zip(flip_y, flip_x))
        return a, b, one, two

    def copies(self, s, p):
        x, y, z, core = self.x, self.y, self.z, self.core
        a, b, one, two = self.turn(p)

        def at(ref, start, size):
            return ref.at[p, pl.ds(pl.multiple_of(start, 8), size)]

        def final(start, size):
            start = p * PIECE + core * 128 + start
            return self.out.at[pl.ds(pl.multiple_of(start, 8), size)]

        def copy(src, dst, kind, to):
            return pltpu.make_async_remote_copy(
                src, dst, self.send.at[kind, p], self.recv.at[kind, p],
                device_id=self.device(*to), device_id_type=MESH)

        keep2 = a * 64 + b * 32
        if s == 0:
            return [copy(self.half(p, 1 - core), self.r0.at[p], 0, (x, y, z, 1 - core))]
        if s == 1:
            return [copy(at(self.acc, (1 - a) * 64, 64), self.r1.at[p], 1, one)]
        if s == 2:
            return [copy(at(self.acc, a * 64 + (1 - b) * 32, 32), self.r2.at[p], 2, two)]
        if s in (3, 4):
            found = []
            for d in (1, 2, 3):
                zz = lax.rem(z + d, 4)
                if s == 3:
                    src, dst = at(self.acc, keep2 + zz * 8, 8), self.r3.at[p, d - 1]
                else:
                    src, dst = at(self.acc, keep2 + z * 8, 8), final(keep2 + z * 8, 8)
                found.append(copy(src, dst, 3 * (s - 2) + d - 1, (x, y, zz, core)))
            return found
        if s == 5:
            return [copy(final(keep2, 32), final(keep2, 32), 9, two)]
        if s == 6:
            return [copy(final(a * 64, 64), final(a * 64, 64), 10, one)]
        return [copy(final(0, 128), final(0, 128), 11, (x, y, z, 1 - core))]

    def own_in(self, p):
        return pltpu.make_async_copy(self.half(p, self.core), self.acc.at[p], self.local.at[0, p])

    def own_out(self, p):
        a, b, _, _ = self.turn(p)
        start = pl.multiple_of(a * 64 + b * 32 + self.z * 8, 8)
        to = p * PIECE + self.core * 128 + start
        return pltpu.make_async_copy(
            self.acc.at[p, pl.ds(start, 8)], self.out.at[pl.ds(pl.multiple_of(to, 8), 8)],
            self.local.at[1, p])

    def stage(self, s, p):
        a, b, _, _ = self.turn(p)
        if s:
            for copy in self.copies(s - 1, p):
                copy.wait_recv()
        if s == 0:
            if self.far:
                self.own_in(p).start()
        elif s == 1:
            if self.far:
                self.own_in(p).wait()
                self.acc[p] += self.r0[p]
            else:
                self.acc[p] = self.half(p, self.core)[...] + self.r0[p]
        elif s == 2:
            at = pl.ds(pl.multiple_of(a * 64, 64), 64)
            self.acc[p, at] += self.r1[p]
        elif s == 3:
            at = pl.ds(pl.multiple_of(a * 64 + b * 32, 32), 32)
            self.acc[p, at] += self.r2[p]
        elif s == 4:
            at = pl.ds(pl.multiple_of(a * 64 + b * 32 + self.z * 8, 8), 8)
            self.acc[p, at] += self.r3[p, 0] + self.r3[p, 1] + self.r3[p, 2]
            self.own_out(p).start()
        elif s == 5:
            self.own_out(p).wait()
        if s < self.STAGES:
            for copy in self.copies(s, p):
                copy.start()

    SPACE = 2

    def ticks(self):
        return self.count + self.SPACE * self.STAGES

    def tick(self, t):
        for s in range(self.STAGES, -1, -1):
            p = t - self.SPACE * s
            pl.when(jnp.logical_and(p >= 0, p < self.count))(lambda s=s, p=p: self.stage(s, p))

    def finish(self):
        @pl.loop(0, self.count)
        def _(p):
            for s in range(self.STAGES):
                for copy in self.copies(s, p):
                    copy.wait_send()


def pieces(x):
    return [x[:, i * STATE : (i + 1) * STATE] for i in range(4)]


def front_kernel(
    n, rows, length,
    tok, halo, ngain, w, wst, cw, cb, dtb, rate, skip, mask, labcol, sel,
    rounded_o, c_o, p_o, xact_o, y_o, rows_o, q_o, q2_o, pexp_o, sin_o,
    rext, vhi, vlo, gc, sloc, *scratch,
):
    k = pl.program_id(0)
    chunks = length // C
    blocks = rows * chunks
    ex = Exchange(n, rows, chunks, sloc, sin_o, (0, 1), scratch)
    ex.set_passes(pexp_o)

    def convolved(r):
        p = mm(rext[r], w[...], NT)
        p_o[r] = p
        first = PAD - (KW - 1)
        out = cb[...]
        for i in range(KW):
            out = out + cw[i : i + 1, :] * p[first + i : first + i + length]
        c_o[r * length : (r + 1) * length, :] = out
        return out * sigmoid(out)

    @pl.when(k == 0)
    def _():
        ex.clear()
        ex.greet()
        for r in range(rows):
            here = slice(r * length, (r + 1) * length)
            source = tok[here, :].astype(F32)
            for part, at in ((halo[r], slice(0, PAD)), (source, slice(PAD, PAD + length))):
                scale = lax.rsqrt(jnp.mean(part * part, axis=-1, keepdims=True) + EPS)
                rext[r, at, :] = (part * scale * ngain[...]).astype(BF16)
            rounded_o[here, :] = rext[r, PAD:, :]
            xact_o[here, :] = convolved(r)
        upto = (iota((C, C), 0) <= iota((C, C), 1)).astype(BF16)
        t_id, s_id = iota((C, C), 0), iota((C, C), 1)
        for b in range(blocks):
            here = slice(b * C, (b + 1) * C)
            raw = mm(wst[...], rounded_o[here, :], NT)
            step = softplus(raw + dtb[...])
            log = -LOG2E * rate[...] * step
            total = mm3(log, upto)
            size = jnp.log(step) * LOG2E
            lf, rc = total[:HEADS], total[HEADS:] - log[HEADS:]
            end_f, end_r = total[:HEADS, C - 1 : C], total[HEADS:, C - 1 : C]
            sf, sr = lf - size[:HEADS], rc + size[HEADS:]
            m = mask[b]
            e_f = jnp.exp2(lf) * m[0:1]
            w_f = jnp.exp2(end_f - lf) * step[:HEADS] * m[1:2]
            e_r = jnp.exp2(end_r - rc) * m[2:3]
            w_r = jnp.exp2(rc) * step[HEADS:] * m[3:4]
            none = jnp.zeros((32, C), F32)
            rows_o[b] = jnp.concatenate([step, lf, rc, sf, sr, raw], axis=0)
            q = jnp.concatenate([e_f, w_f, e_r, w_r, none], axis=0).T
            q_o[b] = q
            q2_o[b] = jnp.concatenate([lf, rc, sf, sr, none], axis=0).T
            pexp_o[b : b + 1, :] = mm3(q[C - 8 :], sel[0])[7:8]
            pexp_o[8 + b : 9 + b, :] = mm3(q[:8], sel[2])[0:1]
            in_f, in_r, rd_f, rd_r = pieces(xact_o[here, :])
            gf, gr = mm22(rd_f, in_f, NT), mm22(rd_r, in_r, NT)
            same = jnp.logical_and(labcol[b] == m[6:7], t_id != s_id)
            gc[b] = jnp.where(same, jnp.where(t_id > s_id, gf, gr), 0.0)
        ex.totals_of_passes()

    @pl.when(jnp.logical_and(k >= 1, k <= G))
    def _():
        g = k - 1
        for r in range(rows):
            v = convolved(r)
            hi, lo = split2(v)
            vhi[g, r * length : (r + 1) * length, :] = hi
            vlo[g, r * length : (r + 1) * length, :] = lo
            for c in range(chunks):
                b = r * chunks + c
                vb = v[c * C : (c + 1) * C]
                x = xact_o[b * C : (b + 1) * C, :].astype(BF16)
                for d in range(2):
                    scale = mm2(q_o[b], sel[2 * d + 1, :, cols(g)])
                    sloc[b, d, :, cols(g)] = mm(
                        x[:, d * STATE : (d + 1) * STATE], (scale * vb).astype(BF16), TN)
        ex.totals(g)

        @pl.when(g == 0)
        def _():
            ex.met()
            ex.pass_copy().start()

        ex.pair_copy(g).start()

    @pl.when(k > 0)
    def _():
        ex.advance(k - 1)

    @pl.when(jnp.logical_and(k > G, k <= 2 * G))
    def _():
        g = k - 1 - G
        later = iota((C, C), 0) > iota((C, C), 1)
        low = iota((C, 128), 1) < HEAD
        for b in range(blocks):
            here = slice(b * C, (b + 1) * C)
            q2 = pltpu.roll(q2_o[b], 128 - HG * g, 1)
            for pair in range(HG // 2):
                at = slice(pair * 128, (pair + 1) * 128)
                v2 = jnp.concatenate([vhi[g, here, at], vlo[g, here, at]], axis=1)
                outs = []
                for h in (2 * pair, 2 * pair + 1):
                    lt, rt = q2[:, h : h + 1], q2[:, HEADS + h : HEADS + h + 1]
                    ls = rows_o[b, pl.ds(96 + HG * g + h, 1), :]
                    rs = rows_o[b, pl.ds(96 + HEADS + HG * g + h, 1), :]
                    x = jnp.exp2(jnp.where(later, lt - ls, rs - rt))
                    o = mm((gc[b] * x).astype(BF16), v2)
                    outs.append(o[:, :128] + o[:, 128:])
                v = vhi[g, here, at].astype(F32) + vlo[g, here, at].astype(F32)
                y_o[here, at] = jnp.where(low, outs[0], outs[1]) + skip[:, at] * v

    @pl.when(k == pl.num_programs(0) - 1)
    def _():
        ex.finish()


def middle_kernel(
    y, rounded, tok, cot, q, xact, sin, wg, wo, ogain, sel,
    mixed_o, dy_o, drounded_o, ds_o, dread_o, dq_o, ogain_grad, w_grad,
):
    k = pl.program_id(0)
    x = xact[...].astype(BF16)
    rd_f, rd_r = x[:, 2 * STATE : 3 * STATE], x[:, 3 * STATE :]
    s_f, s_r = sin[0, 0].astype(BF16), sin[0, 1].astype(BF16)
    e_f, e_r = mm2(q[0], sel[0]), mm2(q[0], sel[2])
    r_f, r_r = mm(rd_f, s_f), mm(rd_r, s_r)
    yv = y[...] + e_f * r_f + e_r * r_r
    gate = mm(rounded[...], wg[...], NT)
    sg = sigmoid(gate)
    silu = gate * sg
    gated = yv * silu
    scale = lax.rsqrt(jnp.mean(gated * gated, axis=-1, keepdims=True) + EPS)
    normed = gated * scale
    out = (normed * ogain[...]).astype(BF16)
    mixed_o[...] = (tok[...].astype(F32) + mm(out, wo[...])).astype(BF16)
    dout = mm(cot[...], wo[...], NT)
    go = jnp.sum(dout * normed, axis=0, keepdims=True)
    dn = dout * ogain[...]
    dgated = scale * (dn - normed * jnp.mean(dn * normed, axis=-1, keepdims=True))
    dy = dgated * silu
    dy_o[...] = dy
    dgate = (dgated * yv * sg * (1.0 + gate * (1.0 - sg))).astype(BF16)
    drounded_o[...] = mm(dgate, wg[...])
    u_f, u_r = e_f * dy, e_r * dy
    dq_o[0] = mm2(u_f * r_f, sel[0], NT) + mm2(u_r * r_r, sel[2], NT)
    u_f, u_r = u_f.astype(BF16), u_r.astype(BF16)
    ds_o[0, 1] = mm(rd_f, u_f, TN)
    ds_o[0, 0] = mm(rd_r, u_r, TN)
    dread_o[...] = jnp.concatenate([mm(u_f, s_f, NT), mm(u_r, s_r, NT)], axis=1)

    @pl.when(k == 0)
    def _():
        w_grad[:INNER] = mm(dgate, rounded[...], TN)
        w_grad[INNER:] = mm(out, cot[...], TN)
        ogain_grad[...] = jnp.broadcast_to(go, ogain_grad.shape)

    @pl.when(k > 0)
    def _():
        w_grad[:INNER] += mm(dgate, rounded[...], TN)
        w_grad[INNER:] += mm(out, cot[...], TN)
        ogain_grad[...] += go


def back_kernel(
    n, rows, length, far, shared,
    c_i, dy_i, xact, cx, rows_i, q_i, q2_i, pexp, sin, ds, dread, dq_i, mask, labcol, dtb, rate, skip, sel, w_grad,
    dc_o, draw_o, skip_o, small_o, total_o,
    gct, dgt, dvs, dss, dts, dqs, dins, pgs, z, *scratch,
):
    k = pl.program_id(0)
    chunks = length // C
    blocks = rows * chunks
    ex = Exchange(n, rows, chunks, ds, z, (1, 0), scratch[:12])
    ex.set_passes(pexp)
    later = iota((C, C), 1) > iota((C, C), 0)
    if shared:

        def half(p, c):
            return w_grad.at[pl.ds(pl.multiple_of(p * PIECE + c * 128, 128), 128)]

        red = Reduce(2 * INNER // PIECE, half, scratch[12:], total_o, True)

    @pl.when(k == 0)
    def _():
        ex.clear()
        (red if shared else ex).greet()
        ex.totals_of_passes()

        @pl.loop(0, G)
        def _(g):
            ex.totals(g)

        (red if shared else ex).met()
        ex.pass_copy().start()

        @pl.loop(0, G)
        def _(g):
            ex.pair_copy(g).start()

        differ = iota((C, C), 0) != iota((C, C), 1)
        for b in range(blocks):
            in_f, in_r, rd_f, rd_r = pieces(xact[b * C : (b + 1) * C, :])
            gf, gr = mm22(in_f, rd_f, NT), mm22(in_r, rd_r, NT)
            same = jnp.logical_and(labcol[b] == mask[b, 6:7], differ)
            gct[b] = jnp.where(same, jnp.where(later, gf, gr), 0.0)
        dgt[...] = jnp.zeros_like(dgt)
        dss[...] = jnp.zeros_like(dss)
        dins[...] = jnp.zeros_like(dins)
        pgs[...] = jnp.zeros_like(pgs)
        dqs[...] = dq_i[...]

    @pl.when(k < G)
    def _():
        g = k
        low = iota((C, 128), 1) < HEAD
        lane = iota((C, 128), 1)
        ones = jnp.ones((8, C), BF16)
        skips = jnp.zeros((1, GC), F32)
        for b in range(blocks):
            here = slice(b * C, (b + 1) * C)
            q2 = pltpu.roll(q2_i[b], 128 - HG * g, 1)
            cv = c_i[here, :]
            v = cv * sigmoid(cv)
            dy = dy_i[here, :]
            skips += jnp.sum(dy * v, axis=0, keepdims=True)
            dyhi, dylo = split2(dy)
            vb = v.astype(BF16)
            for pair in range(HG // 2):
                at = slice(pair * 128, (pair + 1) * 128)
                dy2 = jnp.concatenate([dyhi[:, at], dylo[:, at]], axis=1)
                outs = []
                for i in range(2):
                    h = 2 * pair + i
                    mine = low if i == 0 else jnp.logical_not(low)
                    dyh = jnp.where(mine, dyhi[:, at], jnp.zeros((), BF16))
                    dw = mm(vb[:, at], dyh, NT)
                    lt = rows_i[b, pl.ds(48 + HG * g + h, 1), :]
                    rt = rows_i[b, pl.ds(48 + HEADS + HG * g + h, 1), :]
                    ls, rs = q2[:, 48 + h : 49 + h], q2[:, 72 + h : 73 + h]
                    x = jnp.exp2(jnp.where(later, lt - ls, rs - rt))
                    dwx = dw * x
                    dgt[b] += dwx
                    gb = gct[b]
                    o = mm((gb * x).astype(BF16), dy2)
                    outs.append(o[:, :128] + o[:, 128:])
                    de = dwx * gb
                    de_f = jnp.where(later, de, 0.0).astype(BF16)
                    de_r = jnp.where(later, 0.0, de).astype(BF16)
                    hot_f = (lane == HG * g + h).astype(BF16)
                    hot_r = (lane == HEADS + HG * g + h).astype(BF16)
                    dss[b] += mm(de_f, hot_f) + mm(de_r, hot_r)
                    dts[b, pl.ds(HG * g + h, 1), :] = mm(ones, de_f)[0:1]
                    dts[b, pl.ds(HEADS + HG * g + h, 1), :] = mm(ones, de_r)[0:1]
                dvs[g, here, at] = jnp.where(low, outs[0], outs[1]) + skip[:, at] * dy[:, at]
        skip_o[...] = jnp.broadcast_to(skips, skip_o.shape)

    if shared:
        red.tick(2 * k)
    ex.advance(k)

    @pl.when(jnp.logical_and(k >= far, k < far + G))
    def _():
        g = k - far
        for b in range(blocks):
            here = slice(b * C, (b + 1) * C)
            cv = c_i[here, :]
            sg = sigmoid(cv)
            v = cv * sg
            x = xact[here, :].astype(BF16)
            dv = dvs[g, here, :]
            for d in range(2):
                zf = z[b, 1 - d, :, cols(g)]
                zb = zf.astype(BF16)
                pick = sel[2 * d + 1, :, cols(g)]
                weight = mm2(q_i[b], pick)
                m = mm(x[:, d * STATE : (d + 1) * STATE], zb)
                dv += weight * m
                u = weight * v
                dqs[b] += mm2(u * m, pick, NT)
                at = slice(d * STATE, (d + 1) * STATE)
                dins[b, :, at] += mm(u.astype(BF16), zb, NT)
                pgs[8 * d + b : 8 * d + b + 1, cols(g)] = pexp[
                    8 * d + b : 8 * d + b + 1, cols(g)
                ] * jnp.sum(zf * sin[b, d, :, cols(g)], axis=0, keepdims=True)
            dc_o[here, :] = dv * (sg * (1.0 + cv * (1.0 - sg)))

    if shared:
        red.tick(2 * k + 1)

    @pl.when(k == far + G)
    def _():
        ex.finish()
        differ = iota((C, C), 0) != iota((C, C), 1)
        from_t = (iota((C, C), 0) >= iota((C, C), 1)).astype(BF16)
        after_t = (iota((C, C), 0) > iota((C, C), 1)).astype(BF16)
        pg_f, pg_r = mm22(sel[0].astype(F32), pgs[0:8], NT), mm22(sel[2].astype(F32), pgs[8:16], NT)
        sums = jnp.zeros((2 * HEADS, 128), F32)
        for b in range(blocks):
            here = slice(b * C, (b + 1) * C)
            same = jnp.logical_and(labcol[b] == mask[b, 6:7], differ)
            dg = jnp.where(same, dgt[b], 0.0)
            dg_f = jnp.where(later, dg, 0.0).astype(BF16)
            dg_r = jnp.where(later, 0.0, dg).astype(BF16)
            in_f, in_r, rd_f, rd_r = pieces(xact[here, :].astype(BF16))
            dx = jnp.concatenate(
                [
                    dins[b, :, :STATE] + mm(dg_f, rd_f),
                    dins[b, :, STATE:] + mm(dg_r, rd_r),
                    dread[here, :STATE] + mm(dg_f, in_f, TN),
                    dread[here, STATE:] + mm(dg_r, in_r, TN),
                ],
                axis=1,
            )
            cv = cx[here, :]
            sg = sigmoid(cv)
            dc_o[here, :] = dx * (sg * (1.0 + cv * (1.0 - sg)))
            dq, col, row = dqs[b].T, dss[b].T, dts[b]
            e_f, w_f, e_r, w_r = [dq[i * HEADS : (i + 1) * HEADS] for i in range(4)]
            cs_f, cs_r = col[:HEADS], col[HEADS : 2 * HEADS]
            d_lf = row[:HEADS] - cs_f + e_f - w_f
            d_rc = cs_r - row[HEADS:] - e_r + w_r
            d_size = jnp.concatenate([cs_f + w_f, cs_r + w_r], axis=0)
            end_f = jnp.sum(w_f, axis=1, keepdims=True) + pg_f[:HEADS, b : b + 1]
            end_r = jnp.sum(e_r, axis=1, keepdims=True) + pg_r[2 * HEADS : 3 * HEADS, b : b + 1]
            d_log = jnp.concatenate(
                [mm3(d_lf, from_t) + end_f, mm3(d_rc, after_t) + end_r], axis=0)
            step, raw = rows_i[b, 0:48], rows_i[b, 144:192] + dtb[...]
            sg = sigmoid(raw)
            ratio = jnp.where(raw < -15.0, 1.0, sg / jnp.maximum(step, 1e-30))
            d_raw = -rate[...] * d_log * sg + d_size * ratio
            draw_o[:, here] = d_raw.astype(BF16)
            bias = jnp.sum(d_raw, axis=1, keepdims=True)
            rates = -jnp.sum(step * d_log, axis=1, keepdims=True)
            at = iota((2 * HEADS, 128), 1)
            sums += jnp.where(at == 0, bias, jnp.where(at == 1, rates, 0.0))
        small_o[...] = sums
        if shared:

            @pl.loop(2 * (far + G + 1), red.ticks())
            def _(t):
                red.tick(t)

            red.finish()


def last_kernel(
    rows, length, shared,
    dc, halo, p_i, drounded, draw, rounded, tok, cot, ngain, cw, w, wst, small, ogain_grad, skips,
    tg_o, total_o,
    acc, *scratch,
):
    k = pl.program_id(0)
    groups = CONV // GC
    st = scratch[0] if shared else total_o
    if shared:

        def half(p, c):
            return st.at[p, pl.ds(pl.multiple_of(c * 128, 128), 128)]

        red = Reduce(groups + 1, half, scratch[1:], total_o, False)

    @pl.when(k == 0)
    def _():
        if shared:
            red.greet()
        acc[...] = drounded[...] + mm(draw[...], wst[...], TN)
        st[groups] = jnp.zeros((PIECE, D), F32)
        st[groups, 0:48] = mm(draw[...], rounded[...])
        st[groups, 48:96, 0:128] = small[...]
        for i in range(2):
            st[groups, 104 + 8 * i : 112 + 8 * i] = ogain_grad[:, i * D : (i + 1) * D]
            st[groups, 120 + 8 * i : 128 + 8 * i] = skips[:, i * D : (i + 1) * D]

    parts = []
    taps = [jnp.zeros((1, GC), F32) for _ in range(KW)]
    bias = jnp.zeros((1, GC), F32)
    for r in range(rows):
        own = dc[r * length : (r + 1) * length, :]
        ext = jnp.concatenate([own, halo[r]], axis=0)
        total = None
        for i in range(KW):
            one = cw[i : i + 1, :] * ext[KW - 1 - i : KW - 1 - i + length]
            total = one if total is None else total + one
            first = PAD - (KW - 1) + i
            taps[i] += jnp.sum(own * p_i[r, first : first + length, :], axis=0, keepdims=True)
        bias += jnp.sum(own, axis=0, keepdims=True)
        parts.append(total.astype(BF16))
    both = jnp.concatenate(parts, axis=0)
    st[k] = mm(both, rounded[...], TN)
    line = pl.multiple_of(136 + 8 * (k // 3), 8)
    lane = pl.multiple_of(GC * lax.rem(k, 3), GC)
    st[groups, pl.ds(line, 8), pl.ds(lane, GC)] = jnp.concatenate(
        taps + [bias, jnp.zeros((3, GC), F32)], axis=0)
    if shared:
        pl.when(k == 0)(red.met)
        red.tick(k)
    acc[...] += mm(both, w[...])

    @pl.when(k == groups - 1)
    def _():
        gains = jnp.zeros((1, D), F32)
        for b in range(rows * length // C):
            here = slice(b * C, (b + 1) * C)
            source = tok[here, :].astype(F32)
            scale = lax.rsqrt(jnp.mean(source * source, axis=-1, keepdims=True) + EPS)
            m = source * scale
            d_rounded = acc[here, :]
            gains += jnp.sum(d_rounded * m, axis=0, keepdims=True)
            nn = d_rounded * ngain[...]
            d_source = scale * (nn - m * jnp.mean(nn * m, axis=-1, keepdims=True))
            tg_o[here, :] = (cot[here, :].astype(F32) + d_source).astype(BF16)
        st[groups, 96:104] = jnp.broadcast_to(gains, (8, D))
        if shared:

            @pl.loop(groups, red.ticks())
            def _(t):
                red.tick(t)

            red.finish()


def selectors():
    lane = lax.broadcasted_iota(jnp.int32, (4, 128, INNER), 1)
    kind = lax.broadcasted_iota(jnp.int32, (4, 128, INNER), 0)
    head = lax.broadcasted_iota(jnp.int32, (4, 128, INNER), 2) // HEAD
    return (lane == kind * HEADS + head).astype(BF16)


def shifted(value, axis, steps):
    count = lax.axis_size(axis)
    leading, last = max(0, -steps), min(count, count - steps)
    return lax.ppermute(value, axis, [(i, i + steps) for i in range(leading, last)])


def whole(shape):
    zeros = (0,) * len(shape)
    return pl.BlockSpec(shape, lambda k: zeros, pipeline_mode=pl.Buffered(1))


def struct(shape, dtype=F32):
    return jax.ShapeDtypeStruct(shape, dtype)


def on_device(
    tokens, doc_starts, norm_gain, in_weight, conv_weight, conv_bias, dt_bias, decay_rate,
    skip_scale, out_gain, out_weight, cotangent,
):
    n = lax.axis_size("seq")
    rows, length, _ = tokens.shape
    chunks = length // C
    blocks = rows * chunks
    count = rows * length
    place = lax.axis_index("seq")

    positions = place * length - 1 + jnp.arange(length + 2, dtype=jnp.int32)
    labels = jnp.sum(
        (doc_starts[:, None, :] <= positions[None, :, None]).astype(F32), axis=-1)
    own = labels[:, 1 : length + 1].reshape(blocks, C)
    before = labels[:, :length].reshape(blocks, C)[:, :1]
    after = labels[:, 2:].reshape(blocks, C)[:, C - 1 :]
    mask = jnp.stack(
        [
            (own == before).astype(F32),
            (own == own[:, C - 1 :]).astype(F32),
            (own == after).astype(F32),
            (own == own[:, :1]).astype(F32),
            own, own, own, own,
        ],
        axis=1,
    )
    labcol = own[:, :, None]
    sel = selectors()
    skip = jnp.repeat(skip_scale, HEAD)[None, :]
    weight = in_weight.T
    wst = weight[2 * INNER + 4 * STATE :]
    cb = conv_bias[None, :]
    dtb, rate = dt_bias[:, None], decay_rate[:, None]
    ngain, ogain = norm_gain[None, :], out_gain[None, :]
    tok, cot = tokens.reshape(count, D), cotangent.reshape(count, D)
    rim = shifted(tokens[:, length - 8 :].astype(F32), "seq", 1)
    keep = (jnp.arange(8) >= 8 - (KW - 1)).astype(F32)[None, :, None]
    halo = jnp.pad(rim * keep, ((0, 0), (PAD - 8, 0), (0, 0)))

    params = dict(vmem_limit_bytes=VMEM_LIMIT)
    dims = ("arbitrary",)

    def col(k):
        return jnp.where(k == 0, G, jnp.minimum(k - 1, G - 1))

    def ycol(k):
        return jnp.clip(k - 1 - G, 0, G - 1)

    front_steps = max(2 * G, G + n // 2) + 1
    rounded, c, p, xact, y, rowsv, q, q2, pexp, sin = pl.pallas_call(
        lambda *refs: front_kernel(n, rows, length, *refs),
        grid=(front_steps,),
        in_specs=[
            whole((count, D)), whole((rows, PAD, D)), whole((1, D)),
            pl.BlockSpec((GC, D), lambda k: (G + col(k), 0)),
            whole((2 * HEADS, D)),
            pl.BlockSpec((KW, GC), lambda k: (0, col(k))),
            pl.BlockSpec((1, GC), lambda k: (0, col(k))),
            whole((2 * HEADS, 1)), whole((2 * HEADS, 1)),
            pl.BlockSpec((1, GC), lambda k: (0, ycol(k))),
            whole((blocks, 8, C)), whole((blocks, C, 1)), whole((4, 128, INNER)),
        ],
        out_specs=[
            whole((count, D)),
            pl.BlockSpec((count, GC), lambda k: (0, col(k))),
            pl.BlockSpec((rows, PAD + length, GC), lambda k: (0, 0, col(k))),
            whole((count, GC)),
            pl.BlockSpec((count, GC), lambda k: (0, ycol(k))),
            whole((blocks, 192, C)), whole((blocks, C, 128)), whole((blocks, C, 128)),
            whole((16, INNER)), whole((blocks, 2, STATE, INNER)),
        ],
        out_shape=[
            struct((count, D), BF16), struct((count, CONV)), struct((rows, PAD + length, CONV)),
            struct((count, GC)), struct((count, INNER)), struct((blocks, 192, C)),
            struct((blocks, C, 128)), struct((blocks, C, 128)), struct((16, INNER)),
            struct((blocks, 2, STATE, INNER)),
        ],
        scratch_shapes=[
            pltpu.VMEM((rows, PAD + length, D), BF16),
            pltpu.VMEM((G, count, GC), BF16), pltpu.VMEM((G, count, GC), BF16),
            pltpu.VMEM((blocks, C, C), F32), pltpu.VMEM((blocks, 2, STATE, INNER), F32),
            *Exchange.scratch(rows),
        ],
        compiler_params=pltpu.CompilerParams(
            dimension_semantics=dims, collective_id=0, has_side_effects=True, **params),
        name="front",
    )(tok, halo, ngain, weight, wst, conv_weight, cb, dtb, rate, skip, mask, labcol, sel)

    def by_block(shape):
        zeros = (0,) * (len(shape) - 1)
        return pl.BlockSpec(shape, lambda k: (k,) + zeros)

    mixed, dy, drounded, ds, dread, dq, ogain_grad, w_grad = pl.pallas_call(
        middle_kernel,
        grid=(blocks,),
        in_specs=[
            by_block((C, INNER)), by_block((C, D)), by_block((C, D)), by_block((C, D)),
            by_block((1, C, 128)), by_block((C, GC)), by_block((1, 2, STATE, INNER)),
            whole((INNER, D)), whole((INNER, D)), whole((1, INNER)), whole((4, 128, INNER)),
        ],
        out_specs=[
            by_block((C, D)), by_block((C, INNER)), by_block((C, D)),
            by_block((1, 2, STATE, INNER)), by_block((C, 128)), by_block((1, C, 128)),
            whole((8, INNER)), whole((2 * INNER, D)),
        ],
        out_shape=[
            struct((count, D), BF16), struct((count, INNER)), struct((count, D)),
            struct((blocks, 2, STATE, INNER)), struct((count, 128)), struct((blocks, C, 128)),
            struct((8, INNER)), struct((2 * INNER, D)),
        ],
        compiler_params=pltpu.CompilerParams(dimension_semantics=dims, **params),
        name="middle",
    )(y, rounded, tok, cot, q, xact, sin, weight, out_weight, ogain, sel)

    far = max(G, n // 2 + 1)
    shared = n == 8 and lax.axis_size("rows") == 4
    anywhere = pl.BlockSpec(memory_space=pl.ANY)

    def vcol(k):
        return jnp.where(k < far, jnp.minimum(k, G - 1), jnp.minimum(k - far, G - 1))

    def first_pass(k):
        return jnp.minimum(k, G - 1)

    def second_pass(k):
        return jnp.clip(k - far, 0, G)

    dc, draw, skips, small, out_first = pl.pallas_call(
        lambda *refs: back_kernel(n, rows, length, far, shared, *refs),
        grid=(far + G + 1,),
        in_specs=[
            pl.BlockSpec((count, GC), lambda k: (0, vcol(k))),
            pl.BlockSpec((count, GC), lambda k: (0, first_pass(k))),
            whole((count, GC)),
            pl.BlockSpec((count, GC), lambda k: (0, G)),
            whole((blocks, 192, C)), whole((blocks, C, 128)), whole((blocks, C, 128)),
            whole((16, INNER)), whole((blocks, 2, STATE, INNER)),
            whole((blocks, 2, STATE, INNER)), whole((count, 128)), whole((blocks, C, 128)),
            whole((blocks, 8, C)), whole((blocks, C, 1)),
            whole((2 * HEADS, 1)), whole((2 * HEADS, 1)),
            pl.BlockSpec((1, GC), lambda k: (0, first_pass(k))),
            whole((4, 128, INNER)), anywhere,
        ],
        out_specs=[
            pl.BlockSpec((count, GC), lambda k: (0, second_pass(k))),
            whole((2 * HEADS, count)),
            pl.BlockSpec((8, GC), lambda k: (0, first_pass(k))),
            whole((2 * HEADS, 128)), anywhere,
        ],
        out_shape=[
            struct((count, CONV)), struct((2 * HEADS, count), BF16), struct((8, INNER)),
            struct((2 * HEADS, 128)), struct((2 * INNER, D)),
        ],
        scratch_shapes=[
            pltpu.VMEM((blocks, C, C), F32), pltpu.VMEM((blocks, C, C), F32),
            pltpu.VMEM((G, count, GC), F32), pltpu.VMEM((blocks, C, 128), F32),
            pltpu.VMEM((blocks, 2 * HEADS, C), F32), pltpu.VMEM((blocks, C, 128), F32),
            pltpu.VMEM((blocks, C, 128), F32), pltpu.VMEM((16, INNER), F32),
            pltpu.VMEM((blocks, 2, STATE, INNER), F32),
            *Exchange.scratch(rows), *(Reduce.scratch(2 * INNER // PIECE) if shared else []),
        ],
        compiler_params=pltpu.CompilerParams(
            dimension_semantics=dims, collective_id=1, has_side_effects=True, **params),
        name="back",
    )(c, dy, xact, c, rowsv, q, q2, pexp, sin, ds, dread, dq, mask, labcol, dtb, rate, skip, sel, w_grad)

    spill = shifted(dc.reshape(rows, length, CONV)[:, :8], "seq", -1)
    groups = CONV // GC

    total_shape = (groups + 1, PIECE, D)
    tg, out_last = pl.pallas_call(
        lambda *refs: last_kernel(rows, length, shared, *refs),
        grid=(groups,),
        in_specs=[
            pl.BlockSpec((count, GC), lambda k: (0, k)),
            pl.BlockSpec((rows, 8, GC), lambda k: (0, 0, k)),
            pl.BlockSpec((rows, PAD + length, GC), lambda k: (0, 0, k)),
            whole((count, D)), whole((2 * HEADS, count)),
            whole((count, D)), whole((count, D)), whole((count, D)), whole((1, D)),
            pl.BlockSpec((KW, GC), lambda k: (0, k)),
            pl.BlockSpec((GC, D), lambda k: (G + k, 0)),
            whole((2 * HEADS, D)), whole((2 * HEADS, 128)), whole((8, INNER)), whole((8, INNER)),
        ],
        out_specs=[whole((count, D)), anywhere if shared else whole(total_shape)],
        out_shape=[
            struct((count, D), BF16),
            struct((total_shape[0] * PIECE, D) if shared else total_shape),
        ],
        scratch_shapes=[
            pltpu.VMEM((count, D), F32),
            *([pltpu.VMEM(total_shape, F32), *Reduce.scratch(groups + 1)] if shared else []),
        ],
        compiler_params=pltpu.CompilerParams(
            dimension_semantics=dims, **(dict(collective_id=2, has_side_effects=True) if shared else {}),
            **params),
        name="last",
    )(dc, spill, p, drounded, draw, rounded, tok, cot, ngain, conv_weight, weight, wst, small,
      ogain_grad, skips)

    if not shared:
        out_first, out_last = lax.psum((w_grad, out_last.reshape(-1, D)), ("rows", "seq"))
    in_weight_grad = jnp.concatenate([out_first[:INNER], out_last[: CONV + 48]], axis=0).T
    rest = out_last[CONV:]
    taps = rest[136:160].reshape(3, 8, D).transpose(1, 0, 2).reshape(8, 3 * D)[:, :CONV]
    skip_grad = jnp.sum(rest[120:136:8].reshape(HEADS, HEAD), axis=1)
    return (
        mixed.reshape(tokens.shape), tg.reshape(tokens.shape), rest[96], in_weight_grad,
        taps[:KW], taps[KW], rest[48:96, 0], rest[48:96, 1], skip_grad,
        rest[104:120:8].reshape(INNER), out_first[INNER:],
    )


def solution(mesh):
    local = P("rows", "seq", None)
    return jax.shard_map(
        on_device,
        mesh=mesh,
        in_specs=(local, P("rows", None)) + (P(),) * 9 + (local,),
        out_specs=(local, local) + (P(),) * 9,
        check_vma=False,
    )
```

```python
import jax
import jax.numpy as jnp
from jax import lax
from jax.experimental import pallas as pl
from jax.experimental.pallas import tpu as pltpu
from jax.sharding import PartitionSpec as P

D = 768
INNER = 1536
HEADS = 24
HEAD = 64
STATE = 64
KW = 4
EPS = 1e-05

C = 256
GC = 256
G = INNER // GC
HG = GC // HEAD
CONV = INNER + 4 * STATE
PAD = 16
LOG2E = 1.4426950408889634
F32, BF16 = jnp.float32, jnp.bfloat16
NN, NT, TN = ((1,), (0,)), ((1,), (1,)), ((0,), (0,))
MESH = pl.DeviceIdType.MESH
VMEM_LIMIT = 60 * 1024 * 1024


def mm(a, b, dims=NN):
    return lax.dot_general(a, b, (dims, ((), ())), preferred_element_type=F32)


def split2(a):
    hi = a.astype(BF16)
    return hi, (a - hi.astype(F32)).astype(BF16)


def split3(a):
    hi = a.astype(BF16)
    rest = a - hi.astype(F32)
    mid = rest.astype(BF16)
    return hi, mid, (rest - mid.astype(F32)).astype(BF16)


def mm2(a, b, dims=NN):
    hi, lo = split2(a)
    return mm(hi, b, dims) + mm(lo, b, dims)


def mm3(a, b, dims=NN):
    hi, mid, lo = split3(a)
    return mm(hi, b, dims) + mm(mid, b, dims) + mm(lo, b, dims)


def mm22(a, b, dims=NN):
    ahi, alo = split2(a)
    bhi, blo = split2(b)
    return mm(ahi, bhi, dims) + mm(alo, bhi, dims) + mm(ahi, blo, dims)


def sigmoid(x):
    return 1.0 / (1.0 + jnp.exp(-x))


def softplus(x):
    return jnp.maximum(x, 0.0) + jnp.log1p(jnp.exp(-jnp.abs(x)))


def iota(shape, dim):
    return lax.broadcasted_iota(jnp.int32, shape, dim)


def pick(kind, g):
    return (iota((128, GC), 0) == kind * HEADS + HG * g + (iota((128, GC), 1) >> 6)).astype(BF16)


def pick_all(kind):
    return (iota((128, INNER), 0) == kind * HEADS + (iota((128, INNER), 1) >> 6)).astype(BF16)


def cols(g, width=GC):
    return pl.ds(pl.multiple_of(g * width, width), width)


class Exchange:
    def __init__(self, n, rows, chunks, x_ref, y_ref, passes, scratch, start=1, gap=1):
        self.n, self.rows, self.chunks, self.start, self.gap = n, rows, chunks, start, gap
        self.x, self.y, self.passes = x_ref, y_ref, passes
        (self.st, self.rp, self.qr, self.pm, self.pp) = scratch[:5]
        (self.ps, self.pr, self.as_, self.ar, self.bs, self.br) = scratch[5:]
        self.me = lax.axis_index("seq")
        self.partner = self.me + 1 - 2 * (self.me % 2)
        self.has_before = self.me >= 2
        self.has_after = self.me < n - 2

    @staticmethod
    def scratch(rows):
        state = pltpu.VMEM((G, 2, rows, STATE, GC), F32)
        small = pltpu.VMEM((8, INNER), F32)
        dma = pltpu.SemaphoreType.DMA
        return [
            state, state, state, small, small,
            dma((1,)), dma((1,)), dma((G,)), dma((G,)), dma((2, G)), dma((2, G)),
        ]

    def clear(self):
        @pl.when(jnp.logical_not(self.has_before))
        def _():
            self.qr[:, 0] = jnp.zeros_like(self.qr[:, 0])

        @pl.when(jnp.logical_not(self.has_after))
        def _():
            self.qr[:, 1] = jnp.zeros_like(self.qr[:, 1])

    def peers(self, halo):
        found = [(self.partner, True), (self.me - 2, self.has_before), (self.me + 2, self.has_after)]
        if halo:
            other = 2 * self.me - self.partner
            found.append((other, jnp.logical_and(other >= 0, other < self.n)))
        return found

    def greet(self, halo=False):
        for to, there in self.peers(halo):

            @pl.when(there)
            def _(to=to):
                pl.semaphore_signal(
                    pltpu.get_barrier_semaphore(), inc=1, device_id={"seq": to}, device_id_type=MESH)

    def met(self, halo=False):
        count = sum(jnp.asarray(there, jnp.int32) for _, there in self.peers(halo))
        pl.semaphore_wait(pltpu.get_barrier_semaphore(), count)

    def pass_copy(self):
        return pltpu.make_async_remote_copy(
            self.pm, self.pp, self.ps.at[0], self.pr.at[0],
            device_id={"seq": self.partner}, device_id_type=MESH)

    def pair_copy(self, g):
        return pltpu.make_async_remote_copy(
            self.st.at[g], self.rp.at[g], self.as_.at[g], self.ar.at[g],
            device_id={"seq": self.partner}, device_id_type=MESH)

    def chain_copy(self, d, g):
        return pltpu.make_async_remote_copy(
            self.st.at[g, d], self.qr.at[g, d], self.bs.at[d, g], self.br.at[d, g],
            device_id={"seq": self.me + 2 if d == 0 else self.me - 2}, device_id_type=MESH)

    def order(self, d):
        return range(self.chunks) if d == 0 else range(self.chunks - 1, -1, -1)

    def passing(self, d, b, where):
        row = 8 * self.passes[d] + b
        return self.p_ref[row : row + 1, where]

    def set_passes(self, p_ref):
        self.p_ref = p_ref

    def totals_of_passes(self):
        self.pm[...] = jnp.zeros_like(self.pm)
        for d in range(2):
            for r in range(self.rows):
                total = None
                for c in self.order(d):
                    one = self.passing(d, r * self.chunks + c, slice(None))
                    total = one if total is None else total * one
                self.pm[d * self.rows + r : d * self.rows + r + 1, :] = total

    def totals(self, g):
        for d in range(2):
            for r in range(self.rows):
                total = None
                for c in self.order(d):
                    b = r * self.chunks + c
                    one = self.x[b, d, :, cols(g)]
                    total = one if total is None else self.passing(d, b, cols(g)) * total + one
                self.st[g, d, r] = total

    def chain(self, d, g):
        has_in, has_out = (
            (self.has_before, self.has_after) if d == 0 else (self.has_after, self.has_before))
        copy = self.chain_copy(d, g)
        pl.when(has_in)(copy.wait_recv)
        first = self.me % 2 == d
        for r in range(self.rows):
            row = d * self.rows + r
            mine, theirs = self.st[g, d, r], self.rp[g, d, r]
            p_mine = self.pm[row : row + 1, cols(g)]
            p_theirs = self.pp[row : row + 1, cols(g)]
            before = self.qr[g, d, r]
            middle = jnp.where(first, p_mine, p_theirs) * before + jnp.where(first, mine, theirs)
            self.st[g, d, r] = (
                jnp.where(first, p_theirs, p_mine) * middle + jnp.where(first, theirs, mine))
            state = jnp.where(first, before, middle)
            order = list(self.order(d))
            for i, c in enumerate(order):
                b = r * self.chunks + c
                here = state
                if i < len(order) - 1:
                    state = (
                        self.passing(d, b, cols(g)) * state + self.x[b, d, :, cols(g)])
                self.y[b, d, :, cols(g)] = here
        pl.when(has_out)(copy.start)

    def advance(self, step):
        late = self.n // 2 - 1
        place = self.me // 2

        def due(delay, run):
            q = step - self.start - delay
            g = lax.div(jnp.maximum(q, 0), self.gap)
            pl.when(jnp.logical_and(q == g * self.gap, g < G))(lambda: run(g))

        due(0, lambda g: self.pair_copy(g).wait())

        @pl.when(step == self.start)
        def _():
            self.pass_copy().wait_recv()

        due(place, lambda g: self.chain(0, g))
        due(late - place, lambda g: self.chain(1, g))

    def steps(self):
        return self.start + self.gap * (G - 1) + self.n // 2

    def finish(self):
        self.pass_copy().wait_send()

        @pl.loop(0, G)
        def _(g):
            pl.when(self.has_after)(self.chain_copy(0, g).wait_send)
            pl.when(self.has_before)(self.chain_copy(1, g).wait_send)


PIECE = 256


class Reduce:
    STAGES = 8
    SPACE = 2
    LAG = 5

    def __init__(self, far, near_count, half, near, out, scratch):
        self.far, self.near_count, self.half, self.near, self.out = far, near_count, half, near, out
        (self.own, self.r0, self.r1, self.r2, self.r3, self.send, self.recv, self.local) = scratch
        rows, seq = lax.axis_index("rows"), lax.axis_index("seq")
        self.y, self.core, self.z, self.x = rows // 2, rows % 2, seq // 2, seq % 2

    @staticmethod
    def scratch(far):
        def slot(*shape):
            return pltpu.VMEM(shape + (D,), F32)

        dma = pltpu.SemaphoreType.DMA
        return [
            slot(2, 128), slot(far, 128), slot(far, 64), slot(far, 32), slot(far, 24),
            dma((12, far)), dma((12, far)), dma((2, far)),
        ]

    def device(self, x, y, z, core):
        return {"rows": y * 2 + core, "seq": z * 2 + x}

    def greet(self):
        barrier = pltpu.get_barrier_semaphore()
        x, y, z, core = self.x, self.y, self.z, self.core
        peers = [(x, y, z, 1 - core), (1 - x, y, z, core), (x, 1 - y, z, core)] + [
            (x, y, lax.rem(z + d, 4), core) for d in (1, 2, 3)]
        for peer in peers:
            pl.semaphore_signal(barrier, inc=1, device_id=self.device(*peer), device_id_type=MESH)

        @pl.when(self.has_next())
        def _():
            pl.semaphore_signal(
                barrier, inc=1, device_id=self.device(1 - x, y, z + 2 * x - 1, core),
                device_id_type=MESH)

    def has_next(self):
        return jnp.where(self.x == 0, self.z > 0, self.z < 3)

    def met(self):
        pl.semaphore_wait(pltpu.get_barrier_semaphore(), 6 + self.has_next().astype(jnp.int32))

    def turn(self, p):
        return jnp.where(p >= self.far, lax.rem(p, 2), lax.rem(p, 4)) == 1

    def slot(self, p):
        return jnp.where(p < self.far, p, p - self.far)

    def places(self, p):
        x_first = self.turn(p)
        a, b = jnp.where(x_first, self.x, self.y), jnp.where(x_first, self.y, self.x)
        return a * 64, a * 64 + b * 32, a * 64 + b * 32 + self.z * 8

    def copies(self, s, p):
        x, y, z, core = self.x, self.y, self.z, self.core
        i = self.slot(p)
        one, two, three = self.places(p)
        flip_x, flip_y, flip_core = (1 - x, y, z, core), (x, 1 - y, z, core), (x, y, z, 1 - core)

        def mine(start, size):
            return self.r0.at[i, pl.ds(pl.multiple_of(start, 8), size)]

        def final(start, size):
            return self.out.at[pl.ds(pl.multiple_of(p * PIECE + core * 128 + start, 8), size)]

        def copy(src, dst, kind, to):
            return pltpu.make_async_remote_copy(
                src, dst, self.send.at[kind, i], self.recv.at[kind, i],
                device_id=self.device(*to), device_id_type=MESH)

        def over_z(src, dst, kind):
            peers = [(lax.rem(z + d, 4), d - 1) for d in (1, 2, 3)]
            return [copy(src(zz), dst(d), kind + d, (x, y, zz, core)) for zz, d in peers]

        x_first = self.turn(p)
        first = tuple(jnp.where(x_first, u, v) for u, v in zip(flip_x, flip_y))
        second = tuple(jnp.where(x_first, u, v) for u, v in zip(flip_y, flip_x))
        if s == 1:
            return [copy(mine(64 - one, 64), self.r1.at[i], 1, first)]
        if s == 2:
            return [copy(mine(one + 32 - (two - one), 32), self.r2.at[i], 2, second)]
        if s == 3:
            return over_z(
                lambda zz: mine(two + zz * 8, 8), lambda d: self.r3.at[i, pl.ds(8 * d, 8)], 3)
        if s == 4:
            return over_z(lambda zz: mine(three, 8), lambda d: final(three, 8), 6)
        if s == 5:
            return [copy(final(two, 32), final(two, 32), 9, second)]
        if s == 6:
            return [copy(final(one, 64), final(one, 64), 10, first)]
        return [copy(final(0, 128), final(0, 128), 11, flip_core)]

    def near_half(self, p, c):
        return self.near.at[p - self.far, pl.ds(pl.multiple_of(c * 128, 128), 128)]

    def core_copy(self, p, near):
        i = self.slot(p)
        half = (self.near_half if near else self.half)(p, 1 - self.core)
        return pltpu.make_async_remote_copy(
            half, self.r0.at[i], self.send.at[0, i], self.recv.at[0, i],
            device_id=self.device(self.x, self.y, self.z, 1 - self.core), device_id_type=MESH)

    def own_in(self, p):
        return pltpu.make_async_copy(
            self.half(p, self.core), self.own.at[lax.rem(p, 2)], self.local.at[0, self.slot(p)])

    def own_out(self, p):
        i, start = self.slot(p), pl.multiple_of(self.places(p)[2], 8)
        to = p * PIECE + self.core * 128 + start
        return pltpu.make_async_copy(
            self.r0.at[i, pl.ds(start, 8)], self.out.at[pl.ds(pl.multiple_of(to, 8), 8)],
            self.local.at[1, i])

    def begin(self, p):
        @pl.when(p < self.far)
        def _():
            self.own_in(p).start()
            self.core_copy(p, False).start()

        @pl.when(p >= self.far)
        def _():
            self.core_copy(p, True).start()

    def add_core(self, p):
        i = self.slot(p)

        @pl.when(p < self.far)
        def _():
            self.core_copy(p, False).wait()
            self.own_in(p).wait()
            self.r0[i] += self.own[lax.rem(p, 2)]

        @pl.when(p >= self.far)
        def _():
            self.core_copy(p, True).wait()
            self.r0[i] += self.near_half(p, self.core)[...]

    def stage(self, s, p):
        i = self.slot(p)
        starts = self.places(p)
        if s == 1:
            self.add_core(p)
        else:
            for copy in self.copies(s - 1, p):
                copy.wait_recv()

        def kept(which, size):
            return pl.ds(pl.multiple_of(starts[which], 8), size)

        if s == 2:
            self.r0[i, kept(0, 64)] += self.r1[i]
        elif s == 3:
            self.r0[i, kept(1, 32)] += self.r2[i]
        elif s == 4:
            self.r0[i, kept(2, 8)] += self.r3[i, 0:8] + self.r3[i, 8:16] + self.r3[i, 16:24]
            self.own_out(p).start()
        elif s == 5:
            self.own_out(p).wait()
            for done in (1, 2, 3, 4):
                for copy in self.copies(done, p):
                    copy.wait_send()
        if s < self.STAGES:
            for copy in self.copies(s, p):
                copy.start()
        else:
            for done in (5, 6, 7):
                for copy in self.copies(done, p):
                    copy.wait_send()

    def ticks(self):
        return self.far + self.near_count + self.LAG + self.SPACE * self.STAGES

    def tick(self, t):
        for s in range(self.STAGES, -1, -1):
            q = t - self.SPACE * s
            p = jnp.where(q < self.far, q, q - self.LAG)
            due = jnp.logical_and(q >= 0, p < self.far + self.near_count)
            due = jnp.logical_and(due, jnp.logical_or(q < self.far, p >= self.far))

            @pl.when(due)
            def _(s=s, p=p):
                if s == 0:
                    self.begin(p)
                else:
                    self.stage(s, p)


def pieces(x):
    return [x[:, i * STATE : (i + 1) * STATE] for i in range(4)]


START, GAP = 3, 2


def front_kernel(
    n, rows, length, docs,
    tok, ngain, w, weight, cw, cb_i, dtb_i, rate_i, skip_i, starts,
    rounded_o, c_o, p_o, xact_o, y_o, rows_o, q_o, q2_o, pexp_o, sin_o, wide_o, tall_o,
    rext, vhi, vlo, gc, sloc, wst, hsend, hrecv, loads, hs, hr, *scratch,
):
    k = pl.program_id(0)
    chunks = length // C
    blocks = rows * chunks
    ex = Exchange(n, rows, chunks, sloc, sin_o, (0, 1), scratch, START, GAP)
    ex.set_passes(pexp_o)

    def convolved(r, g):
        p = mm(rext[r], w[...], NT)
        p_o[r] = p
        first = PAD - (KW - 1)
        out = wide_o[0:1, cols(g)]
        for i in range(KW):
            out = out + cw[i : i + 1, :] * p[first + i : first + i + length]
        c_o[r * length : (r + 1) * length, :] = out
        return out * sigmoid(out)

    def normed(source):
        scale = lax.rsqrt(jnp.mean(source * source, axis=-1, keepdims=True) + EPS)
        return (source * scale * ngain[...][None, :]).astype(BF16)

    def label_at(r, position):
        found = jnp.int32(0)
        for d in range(docs):
            found += (starts[r, d] <= position).astype(jnp.int32)
        return found.astype(F32)

    def load_steps():
        return pltpu.make_async_copy(
            weight.at[pl.ds(2 * INNER + 4 * STATE, 2 * HEADS)], wst, loads.at[0])

    def halo_copy():
        return pltpu.make_async_remote_copy(
            hsend, hrecv, hs.at[0], hr.at[0],
            device_id={"seq": ex.me + 1}, device_id_type=MESH)

    def tall(ref, count):
        line = jnp.concatenate([ref[...], jnp.zeros((128 - count,), F32)])[None, :]
        return jnp.broadcast_to(line, (8, 128))

    @pl.when(k == 0)
    def _():
        load_steps().start()

        @pl.when(ex.me == 0)
        def _():
            hrecv[...] = jnp.zeros_like(hrecv)

        ex.clear()
        ex.greet(True)
        for r in range(rows):
            hsend[r] = tok[(r + 1) * length - 16 : (r + 1) * length, :].astype(F32)[8:]
        ex.met(True)
        pl.when(ex.me < n - 1)(halo_copy().start)
        for r in range(rows):
            here = slice(r * length, (r + 1) * length)
            out = normed(tok[here, :].astype(F32))
            rext[r, PAD:, :] = out
            rounded_o[here, :] = out
        dtb, rate = tall(dtb_i, 2 * HEADS).T[:48, 0:1], tall(rate_i, 2 * HEADS).T[:48, 0:1]
        lane = iota((48, 128), 1)
        tall_o[...] = jnp.where(lane == 0, dtb, jnp.where(lane == 1, rate, 0.0))
        pick_f, pick_r = pick_all(0), pick_all(2)
        wide_o[0:8, 0:CONV] = jnp.broadcast_to(cb_i[...][None, :], (8, CONV))
        wide_o[8:16, 0:INNER] = mm3(tall(skip_i, HEADS), pick_f)
        upto = (iota((C, C), 0) <= iota((C, C), 1)).astype(BF16)
        load_steps().wait()
        for b in range(blocks):
            here = slice(b * C, (b + 1) * C)
            r, begin = b // chunks, ex.me * length + (b % chunks) * C
            own = jnp.zeros((1, C), F32)
            for d in range(docs):
                own += (starts[r, d] <= begin + iota((1, C), 1)).astype(F32)
            before, first = label_at(r, begin - 1), label_at(r, begin)
            last, after = label_at(r, begin + C - 1), label_at(r, begin + C)
            m0, m1, m2, m3 = [(own == edge).astype(F32) for edge in (before, last, after, first)]
            raw = mm(wst[...], rounded_o[here, :], NT)
            step = softplus(raw + dtb)
            log = -LOG2E * rate * step
            total = mm3(log, upto)
            size = jnp.log(step) * LOG2E
            lf, rc = total[:HEADS], total[HEADS:] - log[HEADS:]
            end_f, end_r = total[:HEADS, C - 1 : C], total[HEADS:, C - 1 : C]
            sf, sr = lf - size[:HEADS], rc + size[HEADS:]
            e_f = jnp.exp2(lf) * m0
            w_f = jnp.exp2(end_f - lf) * step[:HEADS] * m1
            e_r = jnp.exp2(end_r - rc) * m2
            w_r = jnp.exp2(rc) * step[HEADS:] * m3
            labels = jnp.broadcast_to(own, (8, C))
            none = jnp.zeros((24, C), F32)
            rows_o[b] = jnp.concatenate([step, lf, rc, sf, sr, raw, labels], axis=0)
            q = jnp.concatenate([e_f, w_f, e_r, w_r, labels, none], axis=0).T
            q_o[b] = q
            q2_o[b] = jnp.concatenate([lf, rc, sf, sr, labels, none], axis=0).T
            pexp_o[b : b + 1, :] = mm3(q[C - 8 :], pick_f)[7:8]
            pexp_o[8 + b : 9 + b, :] = mm3(q[:8], pick_r)[0:1]
        ex.totals_of_passes()
        pl.when(ex.me > 0)(halo_copy().wait_recv)
        for r in range(rows):
            rext[r, 0:PAD, :] = normed(jnp.concatenate([jnp.zeros((8, D), F32), hrecv[r]], axis=0))
            xact_o[r * length : (r + 1) * length, :] = convolved(r, G)

    @pl.when(jnp.logical_and(k >= 1, k <= G))
    def _():
        g = k - 1
        picks = [pick(1, g), pick(3, g)]
        for r in range(rows):
            v = convolved(r, g)
            hi, lo = split2(v)
            vhi[g, r * length : (r + 1) * length, :] = hi
            vlo[g, r * length : (r + 1) * length, :] = lo
            for c in range(chunks):
                b = r * chunks + c
                vb = v[c * C : (c + 1) * C]
                x = xact_o[b * C : (b + 1) * C, :].astype(BF16)
                for d in range(2):
                    scale = mm2(q_o[b], picks[d])
                    sloc[b, d, :, cols(g)] = mm(
                        x[:, d * STATE : (d + 1) * STATE], (scale * vb).astype(BF16), TN)
        ex.totals(g)
        pl.when(g == 0)(ex.pass_copy().start)
        ex.pair_copy(g).start()

    pl.when(k > 0)(lambda: ex.advance(k - 1))

    @pl.when(k == G + 1)
    def _():
        t_id, s_id = iota((C, C), 0), iota((C, C), 1)
        for b in range(blocks):
            in_f, in_r, rd_f, rd_r = pieces(xact_o[b * C : (b + 1) * C, :])
            gf, gr = mm22(rd_f, in_f, NT), mm22(rd_r, in_r, NT)
            same = jnp.logical_and(q2_o[b][:, 96:97] == rows_o[b, 192:193], t_id != s_id)
            gc[b] = jnp.where(same, jnp.where(t_id > s_id, gf, gr), 0.0)

    @pl.when(jnp.logical_and(k > G, k <= 2 * G))
    def _():
        g = k - 1 - G
        later = iota((C, C), 0) > iota((C, C), 1)
        low = iota((C, 128), 1) < HEAD
        skip = wide_o[8:9, cols(g)]
        for b in range(blocks):
            here = slice(b * C, (b + 1) * C)
            q2 = pltpu.roll(q2_o[b], 128 - HG * g, 1)
            for pair in range(HG // 2):
                at = slice(pair * 128, (pair + 1) * 128)
                v2 = jnp.concatenate([vhi[g, here, at], vlo[g, here, at]], axis=1)
                outs = []
                for h in (2 * pair, 2 * pair + 1):
                    lt, rt = q2[:, h : h + 1], q2[:, HEADS + h : HEADS + h + 1]
                    ls = rows_o[b, pl.ds(96 + HG * g + h, 1), :]
                    rs = rows_o[b, pl.ds(96 + HEADS + HG * g + h, 1), :]
                    x = jnp.exp2(jnp.where(later, lt - ls, rs - rt))
                    o = mm((gc[b] * x).astype(BF16), v2)
                    outs.append(o[:, :128] + o[:, 128:])
                v = vhi[g, here, at].astype(F32) + vlo[g, here, at].astype(F32)
                y_o[here, at] = jnp.where(low, outs[0], outs[1]) + skip[:, at] * v

    @pl.when(k == pl.num_programs(0) - 1)
    def _():
        ex.finish()
        pl.when(ex.me < n - 1)(halo_copy().wait_send)


def middle_kernel(
    y, rounded, tok, cot, q, xact, sin, wg, wo, ogain,
    mixed_o, dy_o, drounded_o, ds_o, dread_o, dq_o, ogain_grad, w_grad,
):
    k = pl.program_id(0)
    x = xact[...].astype(BF16)
    rd_f, rd_r = x[:, 2 * STATE : 3 * STATE], x[:, 3 * STATE :]
    s_f, s_r = sin[0, 0].astype(BF16), sin[0, 1].astype(BF16)
    pick_f, pick_r = pick_all(0), pick_all(2)
    e_f, e_r = mm2(q[0], pick_f), mm2(q[0], pick_r)
    r_f, r_r = mm(rd_f, s_f), mm(rd_r, s_r)
    yv = y[...] + e_f * r_f + e_r * r_r
    gate = mm(rounded[...], wg[...], NT)
    sg = sigmoid(gate)
    silu = gate * sg
    gated = yv * silu
    scale = lax.rsqrt(jnp.mean(gated * gated, axis=-1, keepdims=True) + EPS)
    normed = gated * scale
    out = (normed * ogain[...][None, :]).astype(BF16)
    mixed_o[...] = (tok[...].astype(F32) + mm(out, wo[...])).astype(BF16)
    dout = mm(cot[...], wo[...], NT)
    go = jnp.sum(dout * normed, axis=0, keepdims=True)
    dn = dout * ogain[...][None, :]
    dgated = scale * (dn - normed * jnp.mean(dn * normed, axis=-1, keepdims=True))
    dy = dgated * silu
    dy_o[...] = dy
    dgate = (dgated * yv * sg * (1.0 + gate * (1.0 - sg))).astype(BF16)
    drounded_o[...] = mm(dgate, wg[...])
    u_f, u_r = e_f * dy, e_r * dy
    dq_o[0] = mm2(u_f * r_f, pick_f, NT) + mm2(u_r * r_r, pick_r, NT)
    u_f, u_r = u_f.astype(BF16), u_r.astype(BF16)
    ds_o[0, 1] = mm(rd_f, u_f, TN)
    ds_o[0, 0] = mm(rd_r, u_r, TN)
    dread_o[...] = jnp.concatenate([mm(u_f, s_f, NT), mm(u_r, s_r, NT)], axis=1)

    @pl.when(k == 0)
    def _():
        w_grad[:INNER] = mm(dgate, rounded[...], TN)
        w_grad[INNER:] = mm(out, cot[...], TN)
        ogain_grad[...] = jnp.broadcast_to(go, ogain_grad.shape)

    @pl.when(k > 0)
    def _():
        w_grad[:INNER] += mm(dgate, rounded[...], TN)
        w_grad[INNER:] += mm(out, cot[...], TN)
        ogain_grad[...] += go


def steps_backward(dq, col, row, pg_f, pg_r, raw, step, rate):
    from_t = (iota((C, C), 0) >= iota((C, C), 1)).astype(BF16)
    after_t = (iota((C, C), 0) > iota((C, C), 1)).astype(BF16)
    e_f, w_f, e_r, w_r = [dq[i * HEADS : (i + 1) * HEADS] for i in range(4)]
    cs_f, cs_r = col[:HEADS], col[HEADS : 2 * HEADS]
    d_lf = row[:HEADS] - cs_f + e_f - w_f
    d_rc = cs_r - row[HEADS:] - e_r + w_r
    d_size = jnp.concatenate([cs_f + w_f, cs_r + w_r], axis=0)
    end_f = jnp.sum(w_f, axis=1, keepdims=True) + pg_f
    end_r = jnp.sum(e_r, axis=1, keepdims=True) + pg_r
    d_log = jnp.concatenate([mm3(d_lf, from_t) + end_f, mm3(d_rc, after_t) + end_r], axis=0)
    sg = sigmoid(raw)
    ratio = jnp.where(raw < -15.0, 1.0, sg / jnp.maximum(step, 1e-30))
    d_raw = -rate * d_log * sg + d_size * ratio
    bias = jnp.sum(d_raw, axis=1, keepdims=True)
    rates = -jnp.sum(step * d_log, axis=1, keepdims=True)
    at = iota((2 * HEADS, 128), 1)
    return d_raw, jnp.where(at == 0, bias, jnp.where(at == 1, rates, 0.0))


def back_kernel(
    n, rows, length, far, shared,
    c_i, dy_i, p_i, cw, w, sin,
    xact, rows_i, q_i, q2_i, pexp, dread, dq_i, wide, tall,
    rounded, tok, cot, ngain, ogain_grad,
    ds_i, drounded, w_grad, weight,
    tg_o, total_o, *scratch,
):
    (gct, dgt, dvs, dss, dts, dqs, dins, pgs, z, acc, draw, wst, near, hsend, hrecv, loads, hs, hr) = (
        scratch[:18])
    k = pl.program_id(0)
    chunks = length // C
    blocks = rows * chunks
    near_count = G + 2
    st = near if shared else total_o
    ex = Exchange(n, rows, chunks, z, z, (1, 0), scratch[18:29])
    ex.set_passes(pexp)
    later = iota((C, C), 1) > iota((C, C), 0)
    if shared:

        def half(p, c):
            return w_grad.at[pl.ds(pl.multiple_of(p * PIECE + c * 128, 128), 128)]

        red = Reduce(2 * INNER // PIECE, near_count, half, near, total_o, scratch[29:])

    def load_states():
        return pltpu.make_async_copy(ds_i, z, loads.at[0])

    def load_sum():
        return pltpu.make_async_copy(drounded, acc, loads.at[1])

    def load_steps():
        return pltpu.make_async_copy(
            weight.at[pl.ds(2 * INNER + 4 * STATE, 2 * HEADS)], wst, loads.at[2])

    def halo_copy(g):
        return pltpu.make_async_remote_copy(
            hsend.at[g], hrecv.at[g], hs.at[g], hr.at[g],
            device_id={"seq": ex.me - 1}, device_id_type=MESH)

    @pl.when(k == 0)
    def _():
        load_states().start()
        load_sum().start()
        load_steps().start()

        @pl.when(ex.me == n - 1)
        def _():
            hrecv[...] = jnp.zeros_like(hrecv)

        ex.clear()
        if shared:
            red.greet()
        else:
            ex.greet(True)
        ex.totals_of_passes()
        load_states().wait()

        @pl.loop(0, G)
        def _(g):
            ex.totals(g)

        if shared:
            red.met()
        else:
            ex.met(True)
        ex.pass_copy().start()

        @pl.loop(0, G)
        def _(g):
            ex.pair_copy(g).start()

        if shared:
            red.tick(0)
        differ = iota((C, C), 0) != iota((C, C), 1)
        for b in range(blocks):
            in_f, in_r, rd_f, rd_r = pieces(xact[b * C : (b + 1) * C, :])
            gf, gr = mm22(in_f, rd_f, NT), mm22(in_r, rd_r, NT)
            same = jnp.logical_and(q2_i[b][:, 96:97] == rows_i[b, 192:193], differ)
            gct[b] = jnp.where(same, jnp.where(later, gf, gr), 0.0)
        dgt[...] = jnp.zeros_like(dgt)
        dss[...] = jnp.zeros_like(dss)
        dins[...] = jnp.zeros_like(dins)
        pgs[...] = jnp.zeros_like(pgs)
        dqs[...] = dq_i[...]
        st[G + 1] = jnp.zeros((PIECE, D), F32)
        load_sum().wait()
        load_steps().wait()

    if shared:

        @pl.when(jnp.logical_and(k > 0, k <= far + 1))
        def _():
            red.tick(2 * k)

    @pl.when(k < G)
    def _():
        g = k
        low = iota((C, 128), 1) < HEAD
        lane = iota((C, 128), 1)
        ones = jnp.ones((8, C), BF16)
        skips = jnp.zeros((1, GC), F32)
        skip = wide[8:9, cols(g)]
        for b in range(blocks):
            here = slice(b * C, (b + 1) * C)
            q2 = pltpu.roll(q2_i[b], 128 - HG * g, 1)
            cv = c_i[here, :]
            v = cv * sigmoid(cv)
            dy = dy_i[here, :]
            skips += jnp.sum(dy * v, axis=0, keepdims=True)
            dyhi, dylo = split2(dy)
            vb = v.astype(BF16)
            for pair in range(HG // 2):
                at = slice(pair * 128, (pair + 1) * 128)
                dy2 = jnp.concatenate([dyhi[:, at], dylo[:, at]], axis=1)
                outs = []
                for i in range(2):
                    h = 2 * pair + i
                    mine = low if i == 0 else jnp.logical_not(low)
                    dyh = jnp.where(mine, dyhi[:, at], jnp.zeros((), BF16))
                    dw = mm(vb[:, at], dyh, NT)
                    lt = rows_i[b, pl.ds(48 + HG * g + h, 1), :]
                    rt = rows_i[b, pl.ds(48 + HEADS + HG * g + h, 1), :]
                    ls, rs = q2[:, 48 + h : 49 + h], q2[:, 72 + h : 73 + h]
                    x = jnp.exp2(jnp.where(later, lt - ls, rs - rt))
                    dwx = dw * x
                    dgt[b] += dwx
                    gb = gct[b]
                    o = mm((gb * x).astype(BF16), dy2)
                    outs.append(o[:, :128] + o[:, 128:])
                    de = dwx * gb
                    de_f = jnp.where(later, de, 0.0).astype(BF16)
                    de_r = jnp.where(later, 0.0, de).astype(BF16)
                    hot_f = (lane == HG * g + h).astype(BF16)
                    hot_r = (lane == HEADS + HG * g + h).astype(BF16)
                    dss[b] += mm(de_f, hot_f) + mm(de_r, hot_r)
                    dts[b, pl.ds(HG * g + h, 1), :] = mm(ones, de_f)[0:1]
                    dts[b, pl.ds(HEADS + HG * g + h, 1), :] = mm(ones, de_r)[0:1]
                dvs[g, here, at] = jnp.where(low, outs[0], outs[1]) + skip[:, at] * dy[:, at]
        line = pl.multiple_of(120 + 8 * (g // 3), 8)
        st[G + 1, pl.ds(line, 8), cols(lax.rem(g, 3))] = jnp.broadcast_to(skips, (8, GC))

    ex.advance(k)

    def send_halo(g):
        for r in range(rows):
            hsend[g, r] = dvs[g, r * length : r * length + 8, :]
        pl.when(ex.me > 0)(halo_copy(g).start)

    @pl.when(jnp.logical_and(k >= far, k < far + G))
    def _():
        g = k - far
        picks = [pick(1, g), pick(3, g)]
        for b in range(blocks):
            here = slice(b * C, (b + 1) * C)
            cv = c_i[here, :]
            sg = sigmoid(cv)
            v = cv * sg
            x = xact[here, :].astype(BF16)
            dv = dvs[g, here, :]
            for d in range(2):
                zf = z[b, 1 - d, :, cols(g)]
                zb = zf.astype(BF16)
                weight = mm2(q_i[b], picks[d])
                m = mm(x[:, d * STATE : (d + 1) * STATE], zb)
                dv += weight * m
                u = weight * v
                dqs[b] += mm2(u * m, picks[d], NT)
                at = slice(d * STATE, (d + 1) * STATE)
                dins[b, :, at] += mm(u.astype(BF16), zb, NT)
                pgs[8 * d + b : 8 * d + b + 1, cols(g)] = pexp[
                    8 * d + b : 8 * d + b + 1, cols(g)
                ] * jnp.sum(zf * sin[b, d], axis=0, keepdims=True)
            dvs[g, here, :] = dv * (sg * (1.0 + cv * (1.0 - sg)))
        send_halo(g)

    @pl.when(k == far + G)
    def _():
        differ = iota((C, C), 0) != iota((C, C), 1)
        for b in range(blocks):
            here = slice(b * C, (b + 1) * C)
            same = jnp.logical_and(q2_i[b][:, 96:97] == rows_i[b, 192:193], differ)
            dg = jnp.where(same, dgt[b], 0.0)
            dg_f = jnp.where(later, dg, 0.0).astype(BF16)
            dg_r = jnp.where(later, 0.0, dg).astype(BF16)
            in_f, in_r, rd_f, rd_r = pieces(xact[here, :].astype(BF16))
            dx = jnp.concatenate(
                [
                    dins[b, :, :STATE] + mm(dg_f, rd_f),
                    dins[b, :, STATE:] + mm(dg_r, rd_r),
                    dread[here, :STATE] + mm(dg_f, in_f, TN),
                    dread[here, STATE:] + mm(dg_r, in_r, TN),
                ],
                axis=1,
            )
            cv = c_i[here, :]
            sg = sigmoid(cv)
            dvs[G, here, :] = dx * (sg * (1.0 + cv * (1.0 - sg)))
        send_halo(G)
        pg_f = mm2(pgs[0:8], pick_all(0), NT).T
        pg_r = mm2(pgs[8:16], pick_all(2), NT).T
        sums = jnp.zeros((2 * HEADS, 128), F32)
        for b in range(blocks):
            d_raw, small = steps_backward(
                dqs[b].T, dss[b].T, dts[b], pg_f[:HEADS, b : b + 1],
                pg_r[2 * HEADS : 3 * HEADS, b : b + 1], rows_i[b, 144:192] + tall[:, 0:1],
                rows_i[b, 0:48], tall[:, 1:2])
            draw[:, b * C : (b + 1) * C] = d_raw.astype(BF16)
            sums += small
        st[G + 1, 0:48] = mm(draw[...], rounded[...])
        st[G + 1, 48:96, 0:128] = sums

    if shared:

        @pl.when(jnp.logical_and(k > 0, k <= far))
        def _():
            red.tick(2 * k + 1)

        @pl.when(k == 0)
        def _():
            red.tick(1)

        @pl.when(k == far + 1)
        def _():
            red.tick(2 * k + 1)
            red.tick(2 * k + 2)

    @pl.when(k > far)
    def _():
        g = k - far - 1
        pl.when(ex.me < n - 1)(halo_copy(g).wait_recv)
        parts = []
        taps = [jnp.zeros((1, GC), F32) for _ in range(KW)]
        bias = jnp.zeros((1, GC), F32)
        for r in range(rows):
            own = dvs[g, r * length : (r + 1) * length, :]
            ext = jnp.concatenate([own, hrecv[g, r]], axis=0)
            total = None
            for i in range(KW):
                one = cw[i : i + 1, :] * ext[KW - 1 - i : KW - 1 - i + length]
                total = one if total is None else total + one
                first = PAD - (KW - 1) + i
                taps[i] += jnp.sum(own * p_i[r, first : first + length, :], axis=0, keepdims=True)
            bias += jnp.sum(own, axis=0, keepdims=True)
            parts.append(total.astype(BF16))
        both = jnp.concatenate(parts, axis=0)
        st[g] = mm(both, rounded[...], TN)
        line = pl.multiple_of(136 + 8 * (g // 3), 8)
        st[G + 1, pl.ds(line, 8), cols(lax.rem(g, 3))] = jnp.concatenate(
            taps + [bias, jnp.zeros((3, GC), F32)], axis=0)
        if shared:
            red.tick(red.far + red.LAG + g)
        acc[...] += mm(both, w[...])

    @pl.when(k == far + G + 1)
    def _():
        acc[...] += mm(draw[...], wst[...], TN)
        gains = jnp.zeros((1, D), F32)
        for b in range(blocks):
            here = slice(b * C, (b + 1) * C)
            source = tok[here, :].astype(F32)
            scale = lax.rsqrt(jnp.mean(source * source, axis=-1, keepdims=True) + EPS)
            m = source * scale
            d_rounded = acc[here, :]
            gains += jnp.sum(d_rounded * m, axis=0, keepdims=True)
            nn = d_rounded * ngain[...][None, :]
            d_source = scale * (nn - m * jnp.mean(nn * m, axis=-1, keepdims=True))
            tg_o[here, :] = (cot[here, :].astype(F32) + d_source).astype(BF16)
        st[G + 1, 96:104] = jnp.broadcast_to(gains, (8, D))
        for i in range(2):
            st[G + 1, 104 + 8 * i : 112 + 8 * i] = ogain_grad[:, i * D : (i + 1) * D]
        if shared:

            @pl.loop(red.far + red.LAG + G + 1, red.ticks())
            def _(t):
                red.tick(t)

        ex.finish()

        @pl.loop(0, G + 1)
        def _(g):
            pl.when(ex.me > 0)(halo_copy(g).wait_send)


def finish_kernel(
    total, in_o, out_o, ng_o, cw_o, cb_o, dtb_o, rate_o, skip_o, og_o, held, arrive, leave,
):
    count = total.shape[0] // PIECE
    gates = INNER // PIECE

    def read(i):
        return pltpu.make_async_copy(
            total.at[pl.ds(i * PIECE, PIECE)], held.at[i], arrive.at[i])

    def write(i):
        size = PIECE
        if i < gates:
            to = in_o.at[pl.ds(i * PIECE, PIECE)]
        elif i < 2 * gates:
            to = out_o.at[pl.ds((i - gates) * PIECE, PIECE)]
        else:
            size = PIECE if i < count - 1 else 2 * HEADS
            to = in_o.at[pl.ds((i - gates) * PIECE, size)]
        return pltpu.make_async_copy(held.at[i, pl.ds(0, size)], to, leave.at[i])

    for i in range(count):
        read(i).start()
    for i in range(count):
        read(i).wait()
        write(i).start()
    rest = held.at[count - 1]
    ng_o[...] = rest[96:97, :][0]
    og_o[...] = jnp.concatenate([rest[104:105, :], rest[112:113, :]], axis=1)[0]
    lines = jnp.concatenate([rest[120:128, :], rest[128:136, :]], axis=1)
    skip_o[...] = mm3(lines, pick_all(0), NT)[0, 0:HEADS]
    both = jnp.concatenate([rest[48:96, 0:128], jnp.zeros((80, 128), F32)], axis=0).T
    dtb_o[...] = both[0, 0 : 2 * HEADS]
    rate_o[...] = both[1, 0 : 2 * HEADS]
    taps = jnp.concatenate([rest[136:144, :], rest[144:152, :], rest[152:160, :GC]], axis=1)
    cw_o[...] = taps[:KW]
    cb_o[...] = taps[KW]
    for i in range(count):
        write(i).wait()


def whole(shape):
    zeros = (0,) * len(shape)
    return pl.BlockSpec(shape, lambda k: zeros, pipeline_mode=pl.Buffered(1))


def struct(shape, dtype=F32):
    return jax.ShapeDtypeStruct(shape, dtype)


def on_device(
    tokens, doc_starts, norm_gain, in_weight, conv_weight, conv_bias, dt_bias, decay_rate,
    skip_scale, out_gain, out_weight, cotangent,
):
    n = lax.axis_size("seq")
    rows, length, _ = tokens.shape
    docs = doc_starts.shape[1]
    chunks = length // C
    blocks = rows * chunks
    count = rows * length
    weight = in_weight.T
    tok, cot = tokens.reshape(count, D), cotangent.reshape(count, D)
    anywhere = pl.BlockSpec(memory_space=pl.ANY)

    params = dict(vmem_limit_bytes=VMEM_LIMIT)
    dims = ("arbitrary",)

    def col(k):
        return jnp.where(k == 0, G, jnp.minimum(k - 1, G - 1))

    def ycol(k):
        return jnp.clip(k - 1 - G, 0, G - 1)

    front_steps = max(2 * G, START + GAP * (G - 1) + n // 2) + 1
    rounded, c, p, xact, y, rowsv, q, q2, pexp, sin, wide, tall = pl.pallas_call(
        lambda *refs: front_kernel(n, rows, length, docs, *refs),
        grid=(front_steps,),
        in_specs=[
            whole((count, D)), whole((D,)),
            pl.BlockSpec((GC, D), lambda k: (G + col(k), 0)), anywhere,
            pl.BlockSpec((KW, GC), lambda k: (0, col(k))),
            whole((CONV,)), whole((2 * HEADS,)), whole((2 * HEADS,)), whole((HEADS,)),
            pl.BlockSpec(memory_space=pltpu.SMEM),
        ],
        out_specs=[
            whole((count, D)),
            pl.BlockSpec((count, GC), lambda k: (0, col(k))),
            pl.BlockSpec((rows, PAD + length, GC), lambda k: (0, 0, col(k))),
            whole((count, GC)),
            pl.BlockSpec((count, GC), lambda k: (0, ycol(k))),
            whole((blocks, 200, C)), whole((blocks, C, 128)), whole((blocks, C, 128)),
            whole((16, INNER)), whole((blocks, 2, STATE, INNER)), whole((16, CONV)),
            whole((2 * HEADS, 128)),
        ],
        out_shape=[
            struct((count, D), BF16), struct((count, CONV)), struct((rows, PAD + length, CONV)),
            struct((count, GC)), struct((count, INNER)), struct((blocks, 200, C)),
            struct((blocks, C, 128)), struct((blocks, C, 128)), struct((16, INNER)),
            struct((blocks, 2, STATE, INNER)), struct((16, CONV)), struct((2 * HEADS, 128)),
        ],
        scratch_shapes=[
            pltpu.VMEM((rows, PAD + length, D), BF16),
            pltpu.VMEM((G, count, GC), BF16), pltpu.VMEM((G, count, GC), BF16),
            pltpu.VMEM((blocks, C, C), F32), pltpu.VMEM((blocks, 2, STATE, INNER), F32),
            pltpu.VMEM((2 * HEADS, D), BF16),
            pltpu.VMEM((rows, 8, D), F32), pltpu.VMEM((rows, 8, D), F32),
            pltpu.SemaphoreType.DMA((1,)), pltpu.SemaphoreType.DMA((1,)),
            pltpu.SemaphoreType.DMA((1,)),
            *Exchange.scratch(rows),
        ],
        compiler_params=pltpu.CompilerParams(
            dimension_semantics=dims, collective_id=0, has_side_effects=True, **params),
        name="front",
    )(tok, norm_gain, weight, weight, conv_weight, conv_bias, dt_bias, decay_rate, skip_scale,
      doc_starts)

    def by_block(shape):
        zeros = (0,) * (len(shape) - 1)
        return pl.BlockSpec(shape, lambda k: (k,) + zeros)

    mixed, dy, drounded, ds, dread, dq, ogain_grad, w_grad = pl.pallas_call(
        middle_kernel,
        grid=(blocks,),
        in_specs=[
            by_block((C, INNER)), by_block((C, D)), by_block((C, D)), by_block((C, D)),
            by_block((1, C, 128)), by_block((C, GC)), by_block((1, 2, STATE, INNER)),
            whole((INNER, D)), whole((INNER, D)), whole((INNER,)),
        ],
        out_specs=[
            by_block((C, D)), by_block((C, INNER)), by_block((C, D)),
            by_block((1, 2, STATE, INNER)), by_block((C, 128)), by_block((1, C, 128)),
            whole((8, INNER)), whole((2 * INNER, D)),
        ],
        out_shape=[
            struct((count, D), BF16), struct((count, INNER)), struct((count, D)),
            struct((blocks, 2, STATE, INNER)), struct((count, 128)), struct((blocks, C, 128)),
            struct((8, INNER)), struct((2 * INNER, D)),
        ],
        compiler_params=pltpu.CompilerParams(dimension_semantics=dims, **params),
        name="middle",
    )(y, rounded, tok, cot, q, xact, sin, weight, out_weight, out_gain)

    far = max(G, n // 2 + 1)
    shared = n == 8 and lax.axis_size("rows") == 4

    def vcol(k):
        return jnp.where(k < far, jnp.minimum(k, G - 1), jnp.minimum(k - far, G))

    def first_pass(k):
        return jnp.minimum(k, G - 1)

    def second_pass(k):
        return jnp.clip(k - far, 0, G - 1)

    def conv_pass(k):
        return jnp.clip(k - far - 1, 0, G)

    far_pieces = 2 * INNER // PIECE
    total_rows = (far_pieces + G + 2) * PIECE
    tg, total = pl.pallas_call(
        lambda *refs: back_kernel(n, rows, length, far, shared, *refs),
        grid=(far + G + 2,),
        in_specs=[
            pl.BlockSpec((count, GC), lambda k: (0, vcol(k))),
            pl.BlockSpec((count, GC), lambda k: (0, first_pass(k))),
            pl.BlockSpec((rows, PAD + length, GC), lambda k: (0, 0, conv_pass(k))),
            pl.BlockSpec((KW, GC), lambda k: (0, conv_pass(k))),
            pl.BlockSpec((GC, D), lambda k: (G + conv_pass(k), 0)),
            pl.BlockSpec((blocks, 2, STATE, GC), lambda k: (0, 0, 0, second_pass(k))),
            whole((count, GC)), whole((blocks, 200, C)), whole((blocks, C, 128)),
            whole((blocks, C, 128)), whole((16, INNER)), whole((count, 128)),
            whole((blocks, C, 128)), whole((16, CONV)), whole((2 * HEADS, 128)),
            whole((count, D)), whole((count, D)), whole((count, D)), whole((D,)),
            whole((8, INNER)), anywhere, anywhere, anywhere, anywhere,
        ],
        out_specs=[whole((count, D)), anywhere if shared else whole((G + 2, PIECE, D))],
        out_shape=[
            struct((count, D), BF16),
            struct((total_rows, D) if shared else (G + 2, PIECE, D)),
        ],
        scratch_shapes=[
            pltpu.VMEM((blocks, C, C), F32), pltpu.VMEM((blocks, C, C), F32),
            pltpu.VMEM((G + 1, count, GC), F32), pltpu.VMEM((blocks, C, 128), F32),
            pltpu.VMEM((blocks, 2 * HEADS, C), F32), pltpu.VMEM((blocks, C, 128), F32),
            pltpu.VMEM((blocks, C, 128), F32), pltpu.VMEM((16, INNER), F32),
            pltpu.VMEM((blocks, 2, STATE, INNER), F32), pltpu.VMEM((count, D), F32),
            pltpu.VMEM((2 * HEADS, count), BF16), pltpu.VMEM((2 * HEADS, D), BF16),
            pltpu.VMEM((G + 2, PIECE, D) if shared else (8, 128), F32),
            pltpu.VMEM((G + 1, rows, 8, GC), F32), pltpu.VMEM((G + 1, rows, 8, GC), F32),
            pltpu.SemaphoreType.DMA((3,)), pltpu.SemaphoreType.DMA((G + 1,)),
            pltpu.SemaphoreType.DMA((G + 1,)),
            *Exchange.scratch(rows), *(Reduce.scratch(far_pieces) if shared else []),
        ],
        compiler_params=pltpu.CompilerParams(
            dimension_semantics=dims, collective_id=1, has_side_effects=True,
            vmem_limit_bytes=63 * 1024 * 1024),
        name="back",
    )(c, dy, p, conv_weight, weight, sin, xact, rowsv, q, q2, pexp, dread, dq, wide, tall,
      rounded, tok, cot, norm_gain, ogain_grad, ds, drounded, w_grad, weight)

    if not shared:
        total = lax.psum(jnp.concatenate([w_grad, total.reshape(-1, D)], axis=0), ("rows", "seq"))
    held = total_rows // PIECE
    inside = pl.BlockSpec(memory_space=pltpu.VMEM)
    in_grad, out_grad, ng, cw, cb, dtb, rate, skip, og = pl.pallas_call(
        finish_kernel,
        in_specs=[anywhere],
        out_specs=[anywhere, anywhere] + [inside] * 7,
        out_shape=[
            struct((2 * INNER + 4 * STATE + 2 * HEADS, D)), struct((INNER, D)), struct((D,)),
            struct((KW, CONV)), struct((CONV,)), struct((2 * HEADS,)), struct((2 * HEADS,)),
            struct((HEADS,)), struct((INNER,)),
        ],
        scratch_shapes=[
            pltpu.VMEM((held, PIECE, D), F32), pltpu.SemaphoreType.DMA((held,)),
            pltpu.SemaphoreType.DMA((held,)),
        ],
        compiler_params=pltpu.CompilerParams(**params),
        name="finish",
    )(total)
    return (
        mixed.reshape(tokens.shape), tg.reshape(tokens.shape), ng, in_grad.T, cw, cb, dtb, rate,
        skip, og, out_grad,
    )


def solution(mesh):
    local = P("rows", "seq", None)
    return jax.shard_map(
        on_device,
        mesh=mesh,
        in_specs=(local, P("rows", None)) + (P(),) * 9 + (local,),
        out_specs=(local, local) + (P(),) * 9,
        check_vma=False,
    )
```

```python
import jax
import jax.numpy as jnp
from jax import lax
from jax.experimental import pallas as pl
from jax.experimental.pallas import tpu as pltpu
from jax.sharding import PartitionSpec as P

D = 768
INNER = 1536
HEADS = 24
HEAD = 64
STATE = 64
KW = 4
EPS = 1e-05

C = 256
GC = 256
G = INNER // GC
HG = GC // HEAD
CONV = INNER + 4 * STATE
PAD = 16
LOG2E = 1.4426950408889634
F32, BF16 = jnp.float32, jnp.bfloat16
NN, NT, TN = ((1,), (0,)), ((1,), (1,)), ((0,), (0,))
MESH = pl.DeviceIdType.MESH
VMEM_LIMIT = 60 * 1024 * 1024


def mm(a, b, dims=NN):
    return lax.dot_general(a, b, (dims, ((), ())), preferred_element_type=F32)


def split2(a):
    hi = a.astype(BF16)
    return hi, (a - hi.astype(F32)).astype(BF16)


def split3(a):
    hi = a.astype(BF16)
    rest = a - hi.astype(F32)
    mid = rest.astype(BF16)
    return hi, mid, (rest - mid.astype(F32)).astype(BF16)


def mm2(a, b, dims=NN):
    count = a.shape[0]
    both = mm(jnp.concatenate(split2(a), axis=0), b, dims)
    return both[:count] + both[count:]


def mm3(a, b, dims=NN):
    count = a.shape[0]
    every = mm(jnp.concatenate(split3(a), axis=0), b, dims)
    return every[:count] + every[count : 2 * count] + every[2 * count :]


def mm22(a, b, dims=NN):
    ahi, alo = split2(a)
    bhi, blo = split2(b)
    return mm(ahi, bhi, dims) + mm(alo, bhi, dims) + mm(ahi, blo, dims)


def sigmoid(x):
    return 1.0 / (1.0 + jnp.exp(-x))


def softplus(x):
    return jnp.maximum(x, 0.0) + jnp.log1p(jnp.exp(-jnp.abs(x)))


def iota(shape, dim):
    return lax.broadcasted_iota(jnp.int32, shape, dim)


def pick(kind, g):
    return (iota((128, GC), 0) == kind * HEADS + HG * g + (iota((128, GC), 1) >> 6)).astype(BF16)


def pick_all(kind):
    return (iota((128, INNER), 0) == kind * HEADS + (iota((128, INNER), 1) >> 6)).astype(BF16)


def cols(g, width=GC):
    return pl.ds(pl.multiple_of(g * width, width), width)


class Exchange:
    def __init__(self, n, rows, chunks, x_ref, y_ref, passes, scratch, start=1, gap=1):
        self.n, self.rows, self.chunks, self.start, self.gap = n, rows, chunks, start, gap
        self.x, self.y, self.passes = x_ref, y_ref, passes
        (self.st, self.rp, self.qr, self.pm, self.pp) = scratch[:5]
        (self.ps, self.pr, self.as_, self.ar, self.bs, self.br) = scratch[5:]
        self.me = lax.axis_index("seq")
        self.partner = self.me + 1 - 2 * (self.me % 2)
        self.has_before = self.me >= 2
        self.has_after = self.me < n - 2

    @staticmethod
    def scratch(rows):
        state = pltpu.VMEM((G, 2, rows, STATE, GC), F32)
        small = pltpu.VMEM((8, INNER), F32)
        dma = pltpu.SemaphoreType.DMA
        return [
            state, state, state, small, small,
            dma((1,)), dma((1,)), dma((G,)), dma((G,)), dma((2, G)), dma((2, G)),
        ]

    def clear(self):
        @pl.when(jnp.logical_not(self.has_before))
        def _():
            self.qr[:, 0] = jnp.zeros_like(self.qr[:, 0])

        @pl.when(jnp.logical_not(self.has_after))
        def _():
            self.qr[:, 1] = jnp.zeros_like(self.qr[:, 1])

    def peers(self, halo):
        found = [(self.partner, True), (self.me - 2, self.has_before), (self.me + 2, self.has_after)]
        if halo:
            other = 2 * self.me - self.partner
            found.append((other, jnp.logical_and(other >= 0, other < self.n)))
        return found

    def greet(self, halo=False):
        for to, there in self.peers(halo):

            @pl.when(there)
            def _(to=to):
                pl.semaphore_signal(
                    pltpu.get_barrier_semaphore(), inc=1, device_id={"seq": to}, device_id_type=MESH)

    def met(self, halo=False):
        count = sum(jnp.asarray(there, jnp.int32) for _, there in self.peers(halo))
        pl.semaphore_wait(pltpu.get_barrier_semaphore(), count)

    def pass_copy(self):
        return pltpu.make_async_remote_copy(
            self.pm, self.pp, self.ps.at[0], self.pr.at[0],
            device_id={"seq": self.partner}, device_id_type=MESH)

    def pair_copy(self, g):
        return pltpu.make_async_remote_copy(
            self.st.at[g], self.rp.at[g], self.as_.at[g], self.ar.at[g],
            device_id={"seq": self.partner}, device_id_type=MESH)

    def chain_copy(self, d, g):
        return pltpu.make_async_remote_copy(
            self.st.at[g, d], self.qr.at[g, d], self.bs.at[d, g], self.br.at[d, g],
            device_id={"seq": self.me + 2 if d == 0 else self.me - 2}, device_id_type=MESH)

    def order(self, d):
        return range(self.chunks) if d == 0 else range(self.chunks - 1, -1, -1)

    def passing(self, d, b, where):
        row = 8 * self.passes[d] + b
        return self.p_ref[row : row + 1, where]

    def set_passes(self, p_ref):
        self.p_ref = p_ref

    def totals_of_passes(self):
        self.pm[...] = jnp.zeros_like(self.pm)
        for d in range(2):
            for r in range(self.rows):
                total = None
                for c in self.order(d):
                    one = self.passing(d, r * self.chunks + c, slice(None))
                    total = one if total is None else total * one
                self.pm[d * self.rows + r : d * self.rows + r + 1, :] = total

    def totals(self, g):
        for d in range(2):
            for r in range(self.rows):
                total = None
                for c in self.order(d):
                    b = r * self.chunks + c
                    one = self.x[b, d, :, cols(g)]
                    total = one if total is None else self.passing(d, b, cols(g)) * total + one
                self.st[g, d, r] = total

    def chain(self, d, g):
        has_in, has_out = (
            (self.has_before, self.has_after) if d == 0 else (self.has_after, self.has_before))
        copy = self.chain_copy(d, g)
        pl.when(has_in)(copy.wait_recv)
        first = self.me % 2 == d
        for r in range(self.rows):
            row = d * self.rows + r
            mine, theirs = self.st[g, d, r], self.rp[g, d, r]
            p_mine = self.pm[row : row + 1, cols(g)]
            p_theirs = self.pp[row : row + 1, cols(g)]
            before = self.qr[g, d, r]
            middle = jnp.where(first, p_mine, p_theirs) * before + jnp.where(first, mine, theirs)
            self.st[g, d, r] = (
                jnp.where(first, p_theirs, p_mine) * middle + jnp.where(first, theirs, mine))
            state = jnp.where(first, before, middle)
            order = list(self.order(d))
            for i, c in enumerate(order):
                b = r * self.chunks + c
                here = state
                if i < len(order) - 1:
                    state = (
                        self.passing(d, b, cols(g)) * state + self.x[b, d, :, cols(g)])
                self.y[b, d, :, cols(g)] = here
        pl.when(has_out)(copy.start)

    def advance(self, step):
        late = self.n // 2 - 1
        place = self.me // 2

        def due(delay, run):
            q = step - self.start - delay
            g = lax.div(jnp.maximum(q, 0), self.gap)
            pl.when(jnp.logical_and(q == g * self.gap, g < G))(lambda: run(g))

        due(0, lambda g: self.pair_copy(g).wait())

        @pl.when(step == self.start)
        def _():
            self.pass_copy().wait_recv()

        due(place, lambda g: self.chain(0, g))
        due(late - place, lambda g: self.chain(1, g))

    def steps(self):
        return self.start + self.gap * (G - 1) + self.n // 2

    def finish(self):
        self.pass_copy().wait_send()

        @pl.loop(0, G)
        def _(g):
            pl.when(self.has_after)(self.chain_copy(0, g).wait_send)
            pl.when(self.has_before)(self.chain_copy(1, g).wait_send)


PIECE = 256


class Reduce:
    STAGES = 8
    SPACE = 2
    LAG = 5

    def __init__(self, far, near_count, half, near, out, scratch):
        self.far, self.near_count, self.half, self.near, self.out = far, near_count, half, near, out
        (self.own, self.r0, self.r1, self.r2, self.r3, self.send, self.recv, self.local) = scratch
        rows, seq = lax.axis_index("rows"), lax.axis_index("seq")
        self.y, self.core, self.z, self.x = rows // 2, rows % 2, seq // 2, seq % 2

    @staticmethod
    def scratch(far):
        def slot(*shape):
            return pltpu.VMEM(shape + (D,), F32)

        dma = pltpu.SemaphoreType.DMA
        return [
            slot(2, 128), slot(far, 128), slot(far, 64), slot(far, 32), slot(far, 24),
            dma((12, far)), dma((12, far)), dma((2, far)),
        ]

    def device(self, x, y, z, core):
        return {"rows": y * 2 + core, "seq": z * 2 + x}

    def greet(self):
        barrier = pltpu.get_barrier_semaphore()
        x, y, z, core = self.x, self.y, self.z, self.core
        peers = [(x, y, z, 1 - core), (1 - x, y, z, core), (x, 1 - y, z, core)] + [
            (x, y, lax.rem(z + d, 4), core) for d in (1, 2, 3)]
        for peer in peers:
            pl.semaphore_signal(barrier, inc=1, device_id=self.device(*peer), device_id_type=MESH)

        @pl.when(self.has_next())
        def _():
            pl.semaphore_signal(
                barrier, inc=1, device_id=self.device(1 - x, y, z + 2 * x - 1, core),
                device_id_type=MESH)

    def has_next(self):
        return jnp.where(self.x == 0, self.z > 0, self.z < 3)

    def met(self):
        pl.semaphore_wait(pltpu.get_barrier_semaphore(), 6 + self.has_next().astype(jnp.int32))

    def turn(self, p):
        return lax.rem(p, 2) == 1

    def slot(self, p):
        return jnp.where(p < self.far, p, p - self.far)

    def places(self, p):
        x_first = self.turn(p)
        a, b = jnp.where(x_first, self.x, self.y), jnp.where(x_first, self.y, self.x)
        return a * 64, a * 64 + b * 32, a * 64 + b * 32 + self.z * 8

    def copies(self, s, p):
        x, y, z, core = self.x, self.y, self.z, self.core
        i = self.slot(p)
        one, two, three = self.places(p)
        flip_x, flip_y, flip_core = (1 - x, y, z, core), (x, 1 - y, z, core), (x, y, z, 1 - core)

        def mine(start, size):
            return self.r0.at[i, pl.ds(pl.multiple_of(start, 8), size)]

        def final(start, size):
            return self.out.at[pl.ds(pl.multiple_of(p * PIECE + core * 128 + start, 8), size)]

        def copy(src, dst, kind, to):
            return pltpu.make_async_remote_copy(
                src, dst, self.send.at[kind, i], self.recv.at[kind, i],
                device_id=self.device(*to), device_id_type=MESH)

        def over_z(src, dst, kind):
            peers = [(lax.rem(z + d, 4), d - 1) for d in (1, 2, 3)]
            return [copy(src(zz), dst(d), kind + d, (x, y, zz, core)) for zz, d in peers]

        x_first = self.turn(p)
        first = tuple(jnp.where(x_first, u, v) for u, v in zip(flip_x, flip_y))
        second = tuple(jnp.where(x_first, u, v) for u, v in zip(flip_y, flip_x))
        if s == 1:
            return [copy(mine(64 - one, 64), self.r1.at[i], 1, first)]
        if s == 2:
            return [copy(mine(one + 32 - (two - one), 32), self.r2.at[i], 2, second)]
        if s == 3:
            return over_z(
                lambda zz: mine(two + zz * 8, 8), lambda d: self.r3.at[i, pl.ds(8 * d, 8)], 3)
        if s == 4:
            return over_z(lambda zz: mine(three, 8), lambda d: final(three, 8), 6)
        if s == 5:
            return [copy(final(two, 32), final(two, 32), 9, second)]
        if s == 6:
            return [copy(final(one, 64), final(one, 64), 10, first)]
        return [copy(final(0, 128), final(0, 128), 11, flip_core)]

    def near_half(self, p, c):
        return self.near.at[p - self.far, pl.ds(pl.multiple_of(c * 128, 128), 128)]

    def core_copy(self, p, near):
        i = self.slot(p)
        half = (self.near_half if near else self.half)(p, 1 - self.core)
        return pltpu.make_async_remote_copy(
            half, self.r0.at[i], self.send.at[0, i], self.recv.at[0, i],
            device_id=self.device(self.x, self.y, self.z, 1 - self.core), device_id_type=MESH)

    def own_in(self, p):
        return pltpu.make_async_copy(
            self.half(p, self.core), self.own.at[lax.rem(p, 2)], self.local.at[0, self.slot(p)])

    def own_out(self, p):
        i, start = self.slot(p), pl.multiple_of(self.places(p)[2], 8)
        to = p * PIECE + self.core * 128 + start
        return pltpu.make_async_copy(
            self.r0.at[i, pl.ds(start, 8)], self.out.at[pl.ds(pl.multiple_of(to, 8), 8)],
            self.local.at[1, i])

    def begin(self, p):
        @pl.when(p < self.far)
        def _():
            self.own_in(p).start()
            self.core_copy(p, False).start()

        @pl.when(p >= self.far)
        def _():
            self.core_copy(p, True).start()

    def add_core(self, p):
        i = self.slot(p)

        @pl.when(p < self.far)
        def _():
            self.core_copy(p, False).wait()
            self.own_in(p).wait()
            self.r0[i] += self.own[lax.rem(p, 2)]

        @pl.when(p >= self.far)
        def _():
            self.core_copy(p, True).wait()
            self.r0[i] += self.near_half(p, self.core)[...]

    def stage(self, s, p):
        i = self.slot(p)
        starts = self.places(p)
        if s == 1:
            self.add_core(p)
        else:
            for copy in self.copies(s - 1, p):
                copy.wait_recv()

        def kept(which, size):
            return pl.ds(pl.multiple_of(starts[which], 8), size)

        if s == 2:
            self.r0[i, kept(0, 64)] += self.r1[i]
        elif s == 3:
            self.r0[i, kept(1, 32)] += self.r2[i]
        elif s == 4:
            self.r0[i, kept(2, 8)] += self.r3[i, 0:8] + self.r3[i, 8:16] + self.r3[i, 16:24]
            self.own_out(p).start()
        elif s == 5:
            self.own_out(p).wait()
            for done in (1, 2, 3, 4):
                for copy in self.copies(done, p):
                    copy.wait_send()
        if s < self.STAGES:
            for copy in self.copies(s, p):
                copy.start()
        else:
            for done in (5, 6, 7):
                for copy in self.copies(done, p):
                    copy.wait_send()

    def ticks(self):
        return self.far + self.near_count + self.LAG + self.SPACE * self.STAGES

    def tick(self, t):
        for s in range(self.STAGES, -1, -1):
            q = t - self.SPACE * s
            p = jnp.where(q < self.far, q, q - self.LAG)
            due = jnp.logical_and(q >= 0, p < self.far + self.near_count)
            due = jnp.logical_and(due, jnp.logical_or(q < self.far, p >= self.far))

            @pl.when(due)
            def _(s=s, p=p):
                if s == 0:
                    self.begin(p)
                else:
                    self.stage(s, p)


def pieces(x):
    return [x[:, i * STATE : (i + 1) * STATE] for i in range(4)]


START, GAP = 2, 1


def front_kernel(
    n, rows, length, docs,
    tok, ngain, w, weight, cw, cb_i, dtb_i, rate_i, skip_i, starts,
    rounded_o, c_o, p_o, xact_o, y_o, rows_o, q_o, q2_o, pexp_o, sin_o, wide_o, tall_o,
    rext, vhi, vlo, gc, sloc, wst, hsend, hrecv, loads, hs, hr, *scratch,
):
    k = pl.program_id(0)
    chunks = length // C
    blocks = rows * chunks
    ex = Exchange(n, rows, chunks, sloc, sin_o, (0, 1), scratch, START, GAP)
    ex.set_passes(pexp_o)

    def convolved(r, g):
        p = mm(rext[r], w[...], NT)
        p_o[r] = p
        first = PAD - (KW - 1)
        out = wide_o[0:1, cols(g)]
        for i in range(KW):
            out = out + cw[i : i + 1, :] * p[first + i : first + i + length]
        c_o[r * length : (r + 1) * length, :] = out
        return out * sigmoid(out)

    def normed(source):
        scale = lax.rsqrt(jnp.mean(source * source, axis=-1, keepdims=True) + EPS)
        return (source * scale * ngain[...][None, :]).astype(BF16)

    def label_at(r, position):
        found = jnp.int32(0)
        for d in range(docs):
            found += (starts[r, d] <= position).astype(jnp.int32)
        return found.astype(F32)

    def load_steps():
        return pltpu.make_async_copy(
            weight.at[pl.ds(2 * INNER + 4 * STATE, 2 * HEADS)], wst, loads.at[0])

    def halo_copy():
        return pltpu.make_async_remote_copy(
            hsend, hrecv, hs.at[0], hr.at[0],
            device_id={"seq": ex.me + 1}, device_id_type=MESH)

    def tall(ref, count):
        line = jnp.concatenate([ref[...], jnp.zeros((128 - count,), F32)])[None, :]
        return jnp.broadcast_to(line, (8, 128))

    @pl.when(k == 0)
    def _():
        load_steps().start()

        @pl.when(ex.me == 0)
        def _():
            hrecv[...] = jnp.zeros_like(hrecv)

        ex.clear()
        ex.greet(True)
        for r in range(rows):
            hsend[r] = tok[(r + 1) * length - 16 : (r + 1) * length, :].astype(F32)[8:]
        ex.met(True)
        pl.when(ex.me < n - 1)(halo_copy().start)
        for r in range(rows):
            here = slice(r * length, (r + 1) * length)
            out = normed(tok[here, :].astype(F32))
            rext[r, PAD:, :] = out
            rounded_o[here, :] = out
        dtb, rate = tall(dtb_i, 2 * HEADS).T[:48, 0:1], tall(rate_i, 2 * HEADS).T[:48, 0:1]
        lane = iota((48, 128), 1)
        tall_o[...] = jnp.where(lane == 0, dtb, jnp.where(lane == 1, rate, 0.0))
        pick_f, pick_r = pick_all(0), pick_all(2)
        wide_o[0:8, 0:CONV] = jnp.broadcast_to(cb_i[...][None, :], (8, CONV))
        lines = [tall(skip_i, HEADS)]
        upto = (iota((C, C), 0) <= iota((C, C), 1)).astype(BF16)
        load_steps().wait()
        for b in range(blocks):
            here = slice(b * C, (b + 1) * C)
            r, begin = b // chunks, ex.me * length + (b % chunks) * C
            own = jnp.zeros((1, C), F32)
            for d in range(docs):
                own += (starts[r, d] <= begin + iota((1, C), 1)).astype(F32)
            before, first = label_at(r, begin - 1), label_at(r, begin)
            last, after = label_at(r, begin + C - 1), label_at(r, begin + C)
            m0, m1, m2, m3 = [(own == edge).astype(F32) for edge in (before, last, after, first)]
            raw = mm(wst[...], rounded_o[here, :], NT)
            step = softplus(raw + dtb)
            log = -LOG2E * rate * step
            total = mm3(log, upto)
            size = jnp.log(step) * LOG2E
            lf, rc = total[:HEADS], total[HEADS:] - log[HEADS:]
            end_f, end_r = total[:HEADS, C - 1 : C], total[HEADS:, C - 1 : C]
            sf, sr = lf - size[:HEADS], rc + size[HEADS:]
            e_f = jnp.exp2(lf) * m0
            w_f = jnp.exp2(end_f - lf) * step[:HEADS] * m1
            e_r = jnp.exp2(end_r - rc) * m2
            w_r = jnp.exp2(rc) * step[HEADS:] * m3
            labels = jnp.broadcast_to(own, (8, C))
            none = jnp.zeros((24, C), F32)
            rows_o[b] = jnp.concatenate([step, lf, rc, sf, sr, raw, labels], axis=0)
            q = jnp.concatenate([e_f, w_f, e_r, w_r, labels, none], axis=0).T
            q_o[b] = q
            q2_o[b] = jnp.concatenate([lf, rc, sf, sr, labels, none], axis=0).T
            lines += [q[C - 8 :], q[:8]]
        if len(lines) % 2:
            lines.append(lines[0])
        wide_f, wide_r = [mm3(jnp.concatenate(lines, axis=0), pick) for pick in (pick_f, pick_r)]
        wide_o[8:16, 0:INNER] = wide_f[0:8]
        for b in range(blocks):
            pexp_o[b : b + 1, :] = wide_f[16 * b + 15 : 16 * b + 16]
            pexp_o[8 + b : 9 + b, :] = wide_r[16 * b + 16 : 16 * b + 17]
        ex.totals_of_passes()
        pl.when(ex.me > 0)(halo_copy().wait_recv)
        for r in range(rows):
            rext[r, 0:PAD, :] = normed(jnp.concatenate([jnp.zeros((8, D), F32), hrecv[r]], axis=0))
            xact_o[r * length : (r + 1) * length, :] = convolved(r, G)

    @pl.when(jnp.logical_and(k >= 1, k <= G))
    def _():
        g = k - 1
        picks = [pick(1, g), pick(3, g)]
        for r in range(rows):
            v = convolved(r, g)
            hi, lo = split2(v)
            vhi[g, r * length : (r + 1) * length, :] = hi
            vlo[g, r * length : (r + 1) * length, :] = lo
            for c in range(chunks):
                b = r * chunks + c
                vb = v[c * C : (c + 1) * C]
                x = xact_o[b * C : (b + 1) * C, :].astype(BF16)
                for d in range(2):
                    scale = mm2(q_o[b], picks[d])
                    sloc[b, d, :, cols(g)] = mm(
                        x[:, d * STATE : (d + 1) * STATE], (scale * vb).astype(BF16), TN)
        ex.totals(g)
        pl.when(g == 0)(ex.pass_copy().start)
        ex.pair_copy(g).start()

    pl.when(k > 0)(lambda: ex.advance(k - 1))

    @pl.when(k == G + 1)
    def _():
        t_id, s_id = iota((C, C), 0), iota((C, C), 1)
        for b in range(blocks):
            in_f, in_r, rd_f, rd_r = pieces(xact_o[b * C : (b + 1) * C, :])
            gf, gr = mm22(rd_f, in_f, NT), mm22(rd_r, in_r, NT)
            same = jnp.logical_and(q2_o[b][:, 96:97] == rows_o[b, 192:193], t_id != s_id)
            gc[b] = jnp.where(same, jnp.where(t_id > s_id, gf, gr), 0.0)

    @pl.when(jnp.logical_and(k > G, k <= 2 * G))
    def _():
        g = k - 1 - G
        later = iota((C, C), 0) > iota((C, C), 1)
        low = iota((C, 128), 1) < HEAD
        skip = wide_o[8:9, cols(g)]
        for b in range(blocks):
            here = slice(b * C, (b + 1) * C)
            q2 = pltpu.roll(q2_o[b], 128 - HG * g, 1)
            for pair in range(HG // 2):
                at = slice(pair * 128, (pair + 1) * 128)
                v2 = jnp.concatenate([vhi[g, here, at], vlo[g, here, at]], axis=1)
                outs = []
                for h in (2 * pair, 2 * pair + 1):
                    lt, rt = q2[:, h : h + 1], q2[:, HEADS + h : HEADS + h + 1]
                    ls = rows_o[b, pl.ds(96 + HG * g + h, 1), :]
                    rs = rows_o[b, pl.ds(96 + HEADS + HG * g + h, 1), :]
                    x = jnp.exp2(jnp.where(later, lt - ls, rs - rt))
                    o = mm((gc[b] * x).astype(BF16), v2)
                    outs.append(o[:, :128] + o[:, 128:])
                v = vhi[g, here, at].astype(F32) + vlo[g, here, at].astype(F32)
                y_o[here, at] = jnp.where(low, outs[0], outs[1]) + skip[:, at] * v

    @pl.when(k == pl.num_programs(0) - 1)
    def _():
        ex.finish()
        pl.when(ex.me < n - 1)(halo_copy().wait_send)


def middle_kernel(
    y, rounded, tok, cot, q, xact, sin, wg, wo, ogain,
    mixed_o, dy_o, drounded_o, ds_o, dread_o, dq_o, ogain_grad, w_grad,
    outs, dgates,
):
    k = pl.program_id(0)
    here = pl.ds(pl.multiple_of(k * C, C), C)
    rounded_b, cot_b = rounded[here, :], cot[here, :]
    x = xact[...].astype(BF16)
    rd_f, rd_r = x[:, 2 * STATE : 3 * STATE], x[:, 3 * STATE :]
    s_f, s_r = sin[0, 0].astype(BF16), sin[0, 1].astype(BF16)
    pick_f, pick_r = pick_all(0), pick_all(2)
    e_f, e_r = mm2(q[0], pick_f), mm2(q[0], pick_r)
    r_f, r_r = mm(rd_f, s_f), mm(rd_r, s_r)
    yv = y[...] + e_f * r_f + e_r * r_r
    gate = mm(rounded_b, wg[...], NT)
    sg = sigmoid(gate)
    silu = gate * sg
    gated = yv * silu
    scale = lax.rsqrt(jnp.mean(gated * gated, axis=-1, keepdims=True) + EPS)
    normed = gated * scale
    out = (normed * ogain[...][None, :]).astype(BF16)
    outs[here, :] = out
    mixed_o[...] = (tok[...].astype(F32) + mm(out, wo[...])).astype(BF16)
    dout = mm(cot_b, wo[...], NT)
    go = jnp.sum(dout * normed, axis=0, keepdims=True)
    dn = dout * ogain[...][None, :]
    dgated = scale * (dn - normed * jnp.mean(dn * normed, axis=-1, keepdims=True))
    dy = dgated * silu
    dy_o[...] = dy
    dgate = (dgated * yv * sg * (1.0 + gate * (1.0 - sg))).astype(BF16)
    dgates[here, :] = dgate
    drounded_o[...] = mm(dgate, wg[...])
    u_f, u_r = e_f * dy, e_r * dy
    dq_o[0] = mm2(u_f * r_f, pick_f, NT) + mm2(u_r * r_r, pick_r, NT)
    u_f, u_r = u_f.astype(BF16), u_r.astype(BF16)
    ds_o[0, 1] = mm(rd_f, u_f, TN)
    ds_o[0, 0] = mm(rd_r, u_r, TN)
    dread_o[...] = jnp.concatenate([mm(u_f, s_f, NT), mm(u_r, s_r, NT)], axis=1)

    @pl.when(k == 0)
    def _():
        ogain_grad[...] = jnp.broadcast_to(go, ogain_grad.shape)

    @pl.when(k > 0)
    def _():
        ogain_grad[...] += go

    @pl.when(k == pl.num_programs(0) - 1)
    def _():
        for i in range(G):
            at = slice(i * GC, (i + 1) * GC)
            w_grad[at] = mm(dgates[:, at], rounded[...], TN)
            w_grad[INNER + i * GC : INNER + (i + 1) * GC] = mm(outs[:, at], cot[...], TN)


def steps_backward(dq, col, row, pg_f, pg_r, raw, step, rate):
    from_t = (iota((C, C), 0) >= iota((C, C), 1)).astype(BF16)
    after_t = (iota((C, C), 0) > iota((C, C), 1)).astype(BF16)
    e_f, w_f, e_r, w_r = [dq[i * HEADS : (i + 1) * HEADS] for i in range(4)]
    cs_f, cs_r = col[:HEADS], col[HEADS : 2 * HEADS]
    d_lf = row[:HEADS] - cs_f + e_f - w_f
    d_rc = cs_r - row[HEADS:] - e_r + w_r
    d_size = jnp.concatenate([cs_f + w_f, cs_r + w_r], axis=0)
    end_f = jnp.sum(w_f, axis=1, keepdims=True) + pg_f
    end_r = jnp.sum(e_r, axis=1, keepdims=True) + pg_r
    d_log = jnp.concatenate([mm3(d_lf, from_t) + end_f, mm3(d_rc, after_t) + end_r], axis=0)
    sg = sigmoid(raw)
    ratio = jnp.where(raw < -15.0, 1.0, sg / jnp.maximum(step, 1e-30))
    d_raw = -rate * d_log * sg + d_size * ratio
    bias = jnp.sum(d_raw, axis=1, keepdims=True)
    rates = -jnp.sum(step * d_log, axis=1, keepdims=True)
    at = iota((2 * HEADS, 128), 1)
    return d_raw, jnp.where(at == 0, bias, jnp.where(at == 1, rates, 0.0))


def back_kernel(
    n, rows, length, far, shared,
    c_i, dy_i, p_i, cw, w, sin,
    xact, rows_i, q_i, q2_i, pexp, dread, dq_i, wide, tall,
    rounded, tok, cot, ngain, ogain_grad,
    ds_i, drounded, w_grad, weight,
    tg_o, total_o, *scratch,
):
    (gct, dgt, dvs, dss, dts, dqs, dins, pgs, z, acc, draw, wst, near, hsend, hrecv, loads, hs, hr) = (
        scratch[:18])
    k = pl.program_id(0)
    chunks = length // C
    blocks = rows * chunks
    near_count = G + 2
    st = near if shared else total_o
    ex = Exchange(n, rows, chunks, z, z, (1, 0), scratch[18:29])
    ex.set_passes(pexp)
    later = iota((C, C), 1) > iota((C, C), 0)
    if shared:

        def half(p, c):
            return w_grad.at[pl.ds(pl.multiple_of(p * PIECE + c * 128, 128), 128)]

        red = Reduce(2 * INNER // PIECE, near_count, half, near, total_o, scratch[29:])

    def load_states():
        return pltpu.make_async_copy(ds_i, z, loads.at[0])

    def load_sum():
        return pltpu.make_async_copy(drounded, acc, loads.at[1])

    def load_steps():
        return pltpu.make_async_copy(
            weight.at[pl.ds(2 * INNER + 4 * STATE, 2 * HEADS)], wst, loads.at[2])

    def halo_copy(g):
        return pltpu.make_async_remote_copy(
            hsend.at[g], hrecv.at[g], hs.at[g], hr.at[g],
            device_id={"seq": ex.me - 1}, device_id_type=MESH)

    @pl.when(k == 0)
    def _():
        load_states().start()
        load_sum().start()
        load_steps().start()

        @pl.when(ex.me == n - 1)
        def _():
            hrecv[...] = jnp.zeros_like(hrecv)

        ex.clear()
        if shared:
            red.greet()
        else:
            ex.greet(True)
        ex.totals_of_passes()
        load_states().wait()

        @pl.loop(0, G)
        def _(g):
            ex.totals(g)

        if shared:
            red.met()
        else:
            ex.met(True)
        ex.pass_copy().start()

        @pl.loop(0, G)
        def _(g):
            ex.pair_copy(g).start()

        differ = iota((C, C), 0) != iota((C, C), 1)
        for b in range(blocks):
            in_f, in_r, rd_f, rd_r = pieces(xact[b * C : (b + 1) * C, :])
            gf, gr = mm22(in_f, rd_f, NT), mm22(in_r, rd_r, NT)
            same = jnp.logical_and(q2_i[b][:, 96:97] == rows_i[b, 192:193], differ)
            gct[b] = jnp.where(same, jnp.where(later, gf, gr), 0.0)
        dgt[...] = jnp.zeros_like(dgt)
        dss[...] = jnp.zeros_like(dss)
        dins[...] = jnp.zeros_like(dins)
        pgs[...] = jnp.zeros_like(pgs)
        dqs[...] = dq_i[...]
        st[G + 1] = jnp.zeros((PIECE, D), F32)
        load_sum().wait()
        load_steps().wait()

    @pl.when(k < G)
    def _():
        g = k
        low = iota((C, 128), 1) < HEAD
        lane = iota((C, 128), 1)
        ones = jnp.ones((8, C), BF16)
        skips = jnp.zeros((1, GC), F32)
        skip = wide[8:9, cols(g)]
        for b in range(blocks):
            here = slice(b * C, (b + 1) * C)
            q2 = pltpu.roll(q2_i[b], 128 - HG * g, 1)
            cv = c_i[here, :]
            v = cv * sigmoid(cv)
            dy = dy_i[here, :]
            skips += jnp.sum(dy * v, axis=0, keepdims=True)
            dyhi, dylo = split2(dy)
            vb = v.astype(BF16)
            for pair in range(HG // 2):
                at = slice(pair * 128, (pair + 1) * 128)
                dy2 = jnp.concatenate([dyhi[:, at], dylo[:, at]], axis=1)
                outs = []
                for i in range(2):
                    h = 2 * pair + i
                    mine = low if i == 0 else jnp.logical_not(low)
                    dyh = jnp.where(mine, dyhi[:, at], jnp.zeros((), BF16))
                    dw = mm(vb[:, at], dyh, NT)
                    lt = rows_i[b, pl.ds(48 + HG * g + h, 1), :]
                    rt = rows_i[b, pl.ds(48 + HEADS + HG * g + h, 1), :]
                    ls, rs = q2[:, 48 + h : 49 + h], q2[:, 72 + h : 73 + h]
                    x = jnp.exp2(jnp.where(later, lt - ls, rs - rt))
                    dwx = dw * x
                    dgt[b] += dwx
                    gb = gct[b]
                    o = mm((gb * x).astype(BF16), dy2)
                    outs.append(o[:, :128] + o[:, 128:])
                    de = dwx * gb
                    de_f = jnp.where(later, de, 0.0).astype(BF16)
                    de_r = jnp.where(later, 0.0, de).astype(BF16)
                    hot_f = (lane == HG * g + h).astype(BF16)
                    hot_r = (lane == HEADS + HG * g + h).astype(BF16)
                    dss[b] += mm(de_f, hot_f) + mm(de_r, hot_r)
                    dts[b, pl.ds(HG * g + h, 1), :] = mm(ones, de_f)[0:1]
                    dts[b, pl.ds(HEADS + HG * g + h, 1), :] = mm(ones, de_r)[0:1]
                dvs[g, here, at] = jnp.where(low, outs[0], outs[1]) + skip[:, at] * dy[:, at]
        line = pl.multiple_of(120 + 8 * (g // 3), 8)
        st[G + 1, pl.ds(line, 8), cols(lax.rem(g, 3))] = jnp.broadcast_to(skips, (8, GC))

    ex.advance(k)

    def send_halo(g):
        for r in range(rows):
            hsend[g, r] = dvs[g, r * length : r * length + 8, :]
        pl.when(ex.me > 0)(halo_copy(g).start)

    @pl.when(jnp.logical_and(k >= far, k < far + G))
    def _():
        g = k - far
        picks = [pick(1, g), pick(3, g)]
        for b in range(blocks):
            here = slice(b * C, (b + 1) * C)
            cv = c_i[here, :]
            sg = sigmoid(cv)
            v = cv * sg
            x = xact[here, :].astype(BF16)
            dv = dvs[g, here, :]
            for d in range(2):
                zf = z[b, 1 - d, :, cols(g)]
                zb = zf.astype(BF16)
                weight = mm2(q_i[b], picks[d])
                m = mm(x[:, d * STATE : (d + 1) * STATE], zb)
                dv += weight * m
                u = weight * v
                dqs[b] += mm2(u * m, picks[d], NT)
                at = slice(d * STATE, (d + 1) * STATE)
                dins[b, :, at] += mm(u.astype(BF16), zb, NT)
                pgs[8 * d + b : 8 * d + b + 1, cols(g)] = pexp[
                    8 * d + b : 8 * d + b + 1, cols(g)
                ] * jnp.sum(zf * sin[b, d], axis=0, keepdims=True)
            dvs[g, here, :] = dv * (sg * (1.0 + cv * (1.0 - sg)))
        send_halo(g)

    @pl.when(k == far + G)
    def _():
        differ = iota((C, C), 0) != iota((C, C), 1)
        for b in range(blocks):
            here = slice(b * C, (b + 1) * C)
            same = jnp.logical_and(q2_i[b][:, 96:97] == rows_i[b, 192:193], differ)
            dg = jnp.where(same, dgt[b], 0.0)
            dg_f = jnp.where(later, dg, 0.0).astype(BF16)
            dg_r = jnp.where(later, 0.0, dg).astype(BF16)
            in_f, in_r, rd_f, rd_r = pieces(xact[here, :].astype(BF16))
            dx = jnp.concatenate(
                [
                    dins[b, :, :STATE] + mm(dg_f, rd_f),
                    dins[b, :, STATE:] + mm(dg_r, rd_r),
                    dread[here, :STATE] + mm(dg_f, in_f, TN),
                    dread[here, STATE:] + mm(dg_r, in_r, TN),
                ],
                axis=1,
            )
            cv = c_i[here, :]
            sg = sigmoid(cv)
            dvs[G, here, :] = dx * (sg * (1.0 + cv * (1.0 - sg)))
        send_halo(G)
        pg_f = mm2(pgs[...], pick_all(0), NT)[0:8].T
        pg_r = mm2(pgs[...], pick_all(2), NT)[8:16].T
        sums = jnp.zeros((2 * HEADS, 128), F32)
        for b in range(blocks):
            d_raw, small = steps_backward(
                dqs[b].T, dss[b].T, dts[b], pg_f[:HEADS, b : b + 1],
                pg_r[2 * HEADS : 3 * HEADS, b : b + 1], rows_i[b, 144:192] + tall[:, 0:1],
                rows_i[b, 0:48], tall[:, 1:2])
            draw[:, b * C : (b + 1) * C] = d_raw.astype(BF16)
            sums += small
        st[G + 1, 0:48] = mm(draw[...], rounded[...])
        st[G + 1, 48:96, 0:128] = sums

    def until(k):
        return jnp.maximum(2 * (k - 2), 0)

    if shared:

        @pl.loop(jnp.where(k == 0, 0, until(k - 1)), until(k))
        def _(t):
            red.tick(t)

    @pl.when(k > far)
    def _():
        g = k - far - 1
        pl.when(ex.me < n - 1)(halo_copy(g).wait_recv)
        parts = []
        taps = [jnp.zeros((1, GC), F32) for _ in range(KW)]
        bias = jnp.zeros((1, GC), F32)
        for r in range(rows):
            own = dvs[g, r * length : (r + 1) * length, :]
            ext = jnp.concatenate([own, hrecv[g, r]], axis=0)
            total = None
            for i in range(KW):
                one = cw[i : i + 1, :] * ext[KW - 1 - i : KW - 1 - i + length]
                total = one if total is None else total + one
                first = PAD - (KW - 1) + i
                taps[i] += jnp.sum(own * p_i[r, first : first + length, :], axis=0, keepdims=True)
            bias += jnp.sum(own, axis=0, keepdims=True)
            parts.append(total.astype(BF16))
        both = jnp.concatenate(parts, axis=0)
        st[g] = mm(both, rounded[...], TN)
        line = pl.multiple_of(136 + 8 * (g // 3), 8)
        st[G + 1, pl.ds(line, 8), cols(lax.rem(g, 3))] = jnp.concatenate(
            taps + [bias, jnp.zeros((3, GC), F32)], axis=0)
        acc[...] += mm(both, w[...])

    @pl.when(k == far + G + 1)
    def _():
        acc[...] += mm(draw[...], wst[...], TN)
        gains = jnp.zeros((1, D), F32)
        for b in range(blocks):
            here = slice(b * C, (b + 1) * C)
            source = tok[here, :].astype(F32)
            scale = lax.rsqrt(jnp.mean(source * source, axis=-1, keepdims=True) + EPS)
            m = source * scale
            d_rounded = acc[here, :]
            gains += jnp.sum(d_rounded * m, axis=0, keepdims=True)
            nn = d_rounded * ngain[...][None, :]
            d_source = scale * (nn - m * jnp.mean(nn * m, axis=-1, keepdims=True))
            tg_o[here, :] = (cot[here, :].astype(F32) + d_source).astype(BF16)
        st[G + 1, 96:104] = jnp.broadcast_to(gains, (8, D))
        for i in range(2):
            st[G + 1, 104 + 8 * i : 112 + 8 * i] = ogain_grad[:, i * D : (i + 1) * D]
        if shared:

            @pl.loop(until(k), red.ticks())
            def _(t):
                red.tick(t)

        ex.finish()

        @pl.loop(0, G + 1)
        def _(g):
            pl.when(ex.me > 0)(halo_copy(g).wait_send)


def finish_kernel(
    total, in_o, out_o, ng_o, cw_o, cb_o, dtb_o, rate_o, skip_o, og_o, held, arrive, leave,
):
    count = total.shape[0] // PIECE
    gates = INNER // PIECE

    def read(i):
        return pltpu.make_async_copy(
            total.at[pl.ds(i * PIECE, PIECE)], held.at[i], arrive.at[i])

    def write(i):
        size = PIECE
        if i < gates:
            to = in_o.at[pl.ds(i * PIECE, PIECE)]
        elif i < 2 * gates:
            to = out_o.at[pl.ds((i - gates) * PIECE, PIECE)]
        else:
            size = PIECE if i < count - 1 else 2 * HEADS
            to = in_o.at[pl.ds((i - gates) * PIECE, size)]
        return pltpu.make_async_copy(held.at[i, pl.ds(0, size)], to, leave.at[i])

    for i in range(count):
        read(i).start()
    for i in range(count):
        read(i).wait()
        write(i).start()
    rest = held.at[count - 1]
    ng_o[...] = rest[96:97, :][0]
    og_o[...] = jnp.concatenate([rest[104:105, :], rest[112:113, :]], axis=1)[0]
    lines = jnp.concatenate([rest[120:128, :], rest[128:136, :]], axis=1)
    skip_o[...] = mm3(jnp.concatenate([lines, lines], axis=0), pick_all(0), NT)[0, 0:HEADS]
    both = jnp.concatenate([rest[48:96, 0:128], jnp.zeros((80, 128), F32)], axis=0).T
    dtb_o[...] = both[0, 0 : 2 * HEADS]
    rate_o[...] = both[1, 0 : 2 * HEADS]
    taps = jnp.concatenate([rest[136:144, :], rest[144:152, :], rest[152:160, :GC]], axis=1)
    cw_o[...] = taps[:KW]
    cb_o[...] = taps[KW]
    for i in range(count):
        write(i).wait()


def whole(shape):
    zeros = (0,) * len(shape)
    return pl.BlockSpec(shape, lambda k: zeros, pipeline_mode=pl.Buffered(1))


def struct(shape, dtype=F32):
    return jax.ShapeDtypeStruct(shape, dtype)


def on_device(
    tokens, doc_starts, norm_gain, in_weight, conv_weight, conv_bias, dt_bias, decay_rate,
    skip_scale, out_gain, out_weight, cotangent,
):
    n = lax.axis_size("seq")
    rows, length, _ = tokens.shape
    docs = doc_starts.shape[1]
    chunks = length // C
    blocks = rows * chunks
    count = rows * length
    weight = in_weight.T
    tok, cot = tokens.reshape(count, D), cotangent.reshape(count, D)
    anywhere = pl.BlockSpec(memory_space=pl.ANY)

    params = dict(vmem_limit_bytes=VMEM_LIMIT)
    dims = ("arbitrary",)

    def col(k):
        return jnp.where(k == 0, G, jnp.minimum(k - 1, G - 1))

    def ycol(k):
        return jnp.clip(k - 1 - G, 0, G - 1)

    front_steps = max(2 * G, START + GAP * (G - 1) + n // 2) + 1
    rounded, c, p, xact, y, rowsv, q, q2, pexp, sin, wide, tall = pl.pallas_call(
        lambda *refs: front_kernel(n, rows, length, docs, *refs),
        grid=(front_steps,),
        in_specs=[
            whole((count, D)), whole((D,)),
            pl.BlockSpec((GC, D), lambda k: (G + col(k), 0)), anywhere,
            pl.BlockSpec((KW, GC), lambda k: (0, col(k))),
            whole((CONV,)), whole((2 * HEADS,)), whole((2 * HEADS,)), whole((HEADS,)),
            pl.BlockSpec(memory_space=pltpu.SMEM),
        ],
        out_specs=[
            whole((count, D)),
            pl.BlockSpec((count, GC), lambda k: (0, col(k))),
            pl.BlockSpec((rows, PAD + length, GC), lambda k: (0, 0, col(k))),
            whole((count, GC)),
            pl.BlockSpec((count, GC), lambda k: (0, ycol(k))),
            whole((blocks, 200, C)), whole((blocks, C, 128)), whole((blocks, C, 128)),
            whole((16, INNER)), whole((blocks, 2, STATE, INNER)), whole((16, CONV)),
            whole((2 * HEADS, 128)),
        ],
        out_shape=[
            struct((count, D), BF16), struct((count, CONV)), struct((rows, PAD + length, CONV)),
            struct((count, GC)), struct((count, INNER)), struct((blocks, 200, C)),
            struct((blocks, C, 128)), struct((blocks, C, 128)), struct((16, INNER)),
            struct((blocks, 2, STATE, INNER)), struct((16, CONV)), struct((2 * HEADS, 128)),
        ],
        scratch_shapes=[
            pltpu.VMEM((rows, PAD + length, D), BF16),
            pltpu.VMEM((G, count, GC), BF16), pltpu.VMEM((G, count, GC), BF16),
            pltpu.VMEM((blocks, C, C), F32), pltpu.VMEM((blocks, 2, STATE, INNER), F32),
            pltpu.VMEM((2 * HEADS, D), BF16),
            pltpu.VMEM((rows, 8, D), F32), pltpu.VMEM((rows, 8, D), F32),
            pltpu.SemaphoreType.DMA((1,)), pltpu.SemaphoreType.DMA((1,)),
            pltpu.SemaphoreType.DMA((1,)),
            *Exchange.scratch(rows),
        ],
        compiler_params=pltpu.CompilerParams(
            dimension_semantics=dims, collective_id=0, has_side_effects=True, **params),
        name="front",
    )(tok, norm_gain, weight, weight, conv_weight, conv_bias, dt_bias, decay_rate, skip_scale,
      doc_starts)

    def by_block(shape):
        zeros = (0,) * (len(shape) - 1)
        return pl.BlockSpec(shape, lambda k: (k,) + zeros)

    mixed, dy, drounded, ds, dread, dq, ogain_grad, w_grad = pl.pallas_call(
        middle_kernel,
        grid=(blocks,),
        in_specs=[
            by_block((C, INNER)), whole((count, D)), by_block((C, D)), whole((count, D)),
            by_block((1, C, 128)), by_block((C, GC)), by_block((1, 2, STATE, INNER)),
            whole((INNER, D)), whole((INNER, D)), whole((INNER,)),
        ],
        out_specs=[
            by_block((C, D)), by_block((C, INNER)), by_block((C, D)),
            by_block((1, 2, STATE, INNER)), by_block((C, 128)), by_block((1, C, 128)),
            whole((8, INNER)), whole((2 * INNER, D)),
        ],
        out_shape=[
            struct((count, D), BF16), struct((count, INNER)), struct((count, D)),
            struct((blocks, 2, STATE, INNER)), struct((count, 128)), struct((blocks, C, 128)),
            struct((8, INNER)), struct((2 * INNER, D)),
        ],
        scratch_shapes=[pltpu.VMEM((count, INNER), BF16), pltpu.VMEM((count, INNER), BF16)],
        compiler_params=pltpu.CompilerParams(dimension_semantics=dims, **params),
        name="middle",
    )(y, rounded, tok, cot, q, xact, sin, weight, out_weight, out_gain)

    far = max(G, n // 2 + 1)
    shared = n == 8 and lax.axis_size("rows") == 4

    def vcol(k):
        return jnp.where(k < far, jnp.minimum(k, G - 1), jnp.minimum(k - far, G))

    def first_pass(k):
        return jnp.minimum(k, G - 1)

    def second_pass(k):
        return jnp.clip(k - far, 0, G - 1)

    def conv_pass(k):
        return jnp.clip(k - far - 1, 0, G)

    far_pieces = 2 * INNER // PIECE
    total_rows = (far_pieces + G + 2) * PIECE
    tg, total = pl.pallas_call(
        lambda *refs: back_kernel(n, rows, length, far, shared, *refs),
        grid=(far + G + 2,),
        in_specs=[
            pl.BlockSpec((count, GC), lambda k: (0, vcol(k))),
            pl.BlockSpec((count, GC), lambda k: (0, first_pass(k))),
            pl.BlockSpec((rows, PAD + length, GC), lambda k: (0, 0, conv_pass(k))),
            pl.BlockSpec((KW, GC), lambda k: (0, conv_pass(k))),
            pl.BlockSpec((GC, D), lambda k: (G + conv_pass(k), 0)),
            pl.BlockSpec((blocks, 2, STATE, GC), lambda k: (0, 0, 0, second_pass(k))),
            whole((count, GC)), whole((blocks, 200, C)), whole((blocks, C, 128)),
            whole((blocks, C, 128)), whole((16, INNER)), whole((count, 128)),
            whole((blocks, C, 128)), whole((16, CONV)), whole((2 * HEADS, 128)),
            whole((count, D)), whole((count, D)), whole((count, D)), whole((D,)),
            whole((8, INNER)), anywhere, anywhere, anywhere, anywhere,
        ],
        out_specs=[whole((count, D)), anywhere if shared else whole((G + 2, PIECE, D))],
        out_shape=[
            struct((count, D), BF16),
            struct((total_rows, D) if shared else (G + 2, PIECE, D)),
        ],
        scratch_shapes=[
            pltpu.VMEM((blocks, C, C), F32), pltpu.VMEM((blocks, C, C), F32),
            pltpu.VMEM((G + 1, count, GC), F32), pltpu.VMEM((blocks, C, 128), F32),
            pltpu.VMEM((blocks, 2 * HEADS, C), F32), pltpu.VMEM((blocks, C, 128), F32),
            pltpu.VMEM((blocks, C, 128), F32), pltpu.VMEM((16, INNER), F32),
            pltpu.VMEM((blocks, 2, STATE, INNER), F32), pltpu.VMEM((count, D), F32),
            pltpu.VMEM((2 * HEADS, count), BF16), pltpu.VMEM((2 * HEADS, D), BF16),
            pltpu.VMEM((G + 2, PIECE, D) if shared else (8, 128), F32),
            pltpu.VMEM((G + 1, rows, 8, GC), F32), pltpu.VMEM((G + 1, rows, 8, GC), F32),
            pltpu.SemaphoreType.DMA((3,)), pltpu.SemaphoreType.DMA((G + 1,)),
            pltpu.SemaphoreType.DMA((G + 1,)),
            *Exchange.scratch(rows), *(Reduce.scratch(far_pieces) if shared else []),
        ],
        compiler_params=pltpu.CompilerParams(
            dimension_semantics=dims, collective_id=1, has_side_effects=True,
            vmem_limit_bytes=63 * 1024 * 1024),
        name="back",
    )(c, dy, p, conv_weight, weight, sin, xact, rowsv, q, q2, pexp, dread, dq, wide, tall,
      rounded, tok, cot, norm_gain, ogain_grad, ds, drounded, w_grad, weight)

    if not shared:
        total = lax.psum(jnp.concatenate([w_grad, total.reshape(-1, D)], axis=0), ("rows", "seq"))
    held = total_rows // PIECE
    inside = pl.BlockSpec(memory_space=pltpu.VMEM)
    in_grad, out_grad, ng, cw, cb, dtb, rate, skip, og = pl.pallas_call(
        finish_kernel,
        in_specs=[anywhere],
        out_specs=[anywhere, anywhere] + [inside] * 7,
        out_shape=[
            struct((2 * INNER + 4 * STATE + 2 * HEADS, D)), struct((INNER, D)), struct((D,)),
            struct((KW, CONV)), struct((CONV,)), struct((2 * HEADS,)), struct((2 * HEADS,)),
            struct((HEADS,)), struct((INNER,)),
        ],
        scratch_shapes=[
            pltpu.VMEM((held, PIECE, D), F32), pltpu.SemaphoreType.DMA((held,)),
            pltpu.SemaphoreType.DMA((held,)),
        ],
        compiler_params=pltpu.CompilerParams(**params),
        name="finish",
    )(total)
    return (
        mixed.reshape(tokens.shape), tg.reshape(tokens.shape), ng, in_grad.T, cw, cb, dtb, rate,
        skip, og, out_grad,
    )


def solution(mesh):
    local = P("rows", "seq", None)
    return jax.shard_map(
        on_device,
        mesh=mesh,
        in_specs=(local, P("rows", None)) + (P(),) * 9 + (local,),
        out_specs=(local, local) + (P(),) * 9,
        check_vma=False,
    )
```

```python
import jax
import jax.numpy as jnp
from jax import lax
from jax.experimental import pallas as pl
from jax.experimental.pallas import tpu as pltpu
from jax.sharding import PartitionSpec as P

D = 768
INNER = 1536
HEADS = 24
HEAD = 64
STATE = 64
KW = 4
EPS = 1e-05

C = 256
GC = 256
G = INNER // GC
HG = GC // HEAD
CONV = INNER + 4 * STATE
PAD = 16
LOG2E = 1.4426950408889634
F32, BF16 = jnp.float32, jnp.bfloat16
NN, NT, TN = ((1,), (0,)), ((1,), (1,)), ((0,), (0,))
MESH = pl.DeviceIdType.MESH
VMEM_LIMIT = 60 * 1024 * 1024


def mm(a, b, dims=NN):
    return lax.dot_general(a, b, (dims, ((), ())), preferred_element_type=F32)


def split2(a):
    hi = a.astype(BF16)
    return hi, (a - hi.astype(F32)).astype(BF16)


def split3(a):
    hi = a.astype(BF16)
    rest = a - hi.astype(F32)
    mid = rest.astype(BF16)
    return hi, mid, (rest - mid.astype(F32)).astype(BF16)


def mm2(a, b, dims=NN):
    count = a.shape[0]
    both = mm(jnp.concatenate(split2(a), axis=0), b, dims)
    return both[:count] + both[count:]


def mm3(a, b, dims=NN):
    count = a.shape[0]
    every = mm(jnp.concatenate(split3(a), axis=0), b, dims)
    return every[:count] + every[count : 2 * count] + every[2 * count :]


def mm22(a, b, dims=NN):
    ahi, alo = split2(a)
    bhi, blo = split2(b)
    return mm(ahi, bhi, dims) + mm(alo, bhi, dims) + mm(ahi, blo, dims)


def sigmoid(x):
    return 1.0 / (1.0 + jnp.exp(-x))


def softplus(x):
    return jnp.maximum(x, 0.0) + jnp.log1p(jnp.exp(-jnp.abs(x)))


def iota(shape, dim):
    return lax.broadcasted_iota(jnp.int32, shape, dim)


def pick(kind, g):
    return (iota((128, GC), 0) == kind * HEADS + HG * g + (iota((128, GC), 1) >> 6)).astype(BF16)


def pick_all(kind):
    return (iota((128, INNER), 0) == kind * HEADS + (iota((128, INNER), 1) >> 6)).astype(BF16)


def cols(g, width=GC):
    return pl.ds(pl.multiple_of(g * width, width), width)


class Exchange:
    def __init__(self, n, rows, chunks, x_ref, y_ref, passes, scratch, start=1, gap=1):
        self.n, self.rows, self.chunks, self.start, self.gap = n, rows, chunks, start, gap
        self.x, self.y, self.passes = x_ref, y_ref, passes
        (self.st, self.rp, self.qr, self.pm, self.pp) = scratch[:5]
        (self.ps, self.pr, self.as_, self.ar, self.bs, self.br) = scratch[5:]
        self.me = lax.axis_index("seq")
        self.partner = self.me + 1 - 2 * (self.me % 2)
        self.has_before = self.me >= 2
        self.has_after = self.me < n - 2

    @staticmethod
    def scratch(rows):
        state = pltpu.VMEM((G, 2, rows, STATE, GC), F32)
        small = pltpu.VMEM((8, INNER), F32)
        dma = pltpu.SemaphoreType.DMA
        return [
            state, state, state, small, small,
            dma((1,)), dma((1,)), dma((G,)), dma((G,)), dma((2, G)), dma((2, G)),
        ]

    def clear(self):
        @pl.when(jnp.logical_not(self.has_before))
        def _():
            self.qr[:, 0] = jnp.zeros_like(self.qr[:, 0])

        @pl.when(jnp.logical_not(self.has_after))
        def _():
            self.qr[:, 1] = jnp.zeros_like(self.qr[:, 1])

    def peers(self, halo):
        found = [(self.partner, True), (self.me - 2, self.has_before), (self.me + 2, self.has_after)]
        if halo:
            other = 2 * self.me - self.partner
            found.append((other, jnp.logical_and(other >= 0, other < self.n)))
        return found

    def greet(self, halo=False):
        for to, there in self.peers(halo):

            @pl.when(there)
            def _(to=to):
                pl.semaphore_signal(
                    pltpu.get_barrier_semaphore(), inc=1, device_id={"seq": to}, device_id_type=MESH)

    def met(self, halo=False):
        count = sum(jnp.asarray(there, jnp.int32) for _, there in self.peers(halo))
        pl.semaphore_wait(pltpu.get_barrier_semaphore(), count)

    def pass_copy(self):
        return pltpu.make_async_remote_copy(
            self.pm, self.pp, self.ps.at[0], self.pr.at[0],
            device_id={"seq": self.partner}, device_id_type=MESH)

    def pair_copy(self, g):
        return pltpu.make_async_remote_copy(
            self.st.at[g], self.rp.at[g], self.as_.at[g], self.ar.at[g],
            device_id={"seq": self.partner}, device_id_type=MESH)

    def chain_copy(self, d, g):
        return pltpu.make_async_remote_copy(
            self.st.at[g, d], self.qr.at[g, d], self.bs.at[d, g], self.br.at[d, g],
            device_id={"seq": self.me + 2 if d == 0 else self.me - 2}, device_id_type=MESH)

    def order(self, d):
        return range(self.chunks) if d == 0 else range(self.chunks - 1, -1, -1)

    def passing(self, d, b, where):
        row = 8 * self.passes[d] + b
        return self.p_ref[row : row + 1, where]

    def set_passes(self, p_ref):
        self.p_ref = p_ref

    def totals_of_passes(self):
        self.pm[...] = jnp.zeros_like(self.pm)
        for d in range(2):
            for r in range(self.rows):
                total = None
                for c in self.order(d):
                    one = self.passing(d, r * self.chunks + c, slice(None))
                    total = one if total is None else total * one
                self.pm[d * self.rows + r : d * self.rows + r + 1, :] = total

    def totals(self, g):
        for d in range(2):
            for r in range(self.rows):
                total = None
                for c in self.order(d):
                    b = r * self.chunks + c
                    one = self.x[b, d, :, cols(g)]
                    total = one if total is None else self.passing(d, b, cols(g)) * total + one
                self.st[g, d, r] = total

    def chain(self, d, g):
        has_in, has_out = (
            (self.has_before, self.has_after) if d == 0 else (self.has_after, self.has_before))
        copy = self.chain_copy(d, g)
        pl.when(has_in)(copy.wait_recv)
        first = self.me % 2 == d
        for r in range(self.rows):
            row = d * self.rows + r
            mine, theirs = self.st[g, d, r], self.rp[g, d, r]
            p_mine = self.pm[row : row + 1, cols(g)]
            p_theirs = self.pp[row : row + 1, cols(g)]
            before = self.qr[g, d, r]
            middle = jnp.where(first, p_mine, p_theirs) * before + jnp.where(first, mine, theirs)
            self.st[g, d, r] = (
                jnp.where(first, p_theirs, p_mine) * middle + jnp.where(first, theirs, mine))
            state = jnp.where(first, before, middle)
            order = list(self.order(d))
            for i, c in enumerate(order):
                b = r * self.chunks + c
                here = state
                if i < len(order) - 1:
                    state = (
                        self.passing(d, b, cols(g)) * state + self.x[b, d, :, cols(g)])
                self.y[b, d, :, cols(g)] = here
        pl.when(has_out)(copy.start)

    def advance(self, step):
        late = self.n // 2 - 1
        place = self.me // 2

        def due(delay, run):
            q = step - self.start - delay
            g = lax.div(jnp.maximum(q, 0), self.gap)
            pl.when(jnp.logical_and(q == g * self.gap, g < G))(lambda: run(g))

        due(0, lambda g: self.pair_copy(g).wait())

        @pl.when(step == self.start)
        def _():
            self.pass_copy().wait_recv()

        due(place, lambda g: self.chain(0, g))
        due(late - place, lambda g: self.chain(1, g))

    def steps(self):
        return self.start + self.gap * (G - 1) + self.n // 2

    def finish(self):
        self.pass_copy().wait_send()

        @pl.loop(0, G)
        def _(g):
            pl.when(self.has_after)(self.chain_copy(0, g).wait_send)
            pl.when(self.has_before)(self.chain_copy(1, g).wait_send)


PIECE = 256


class Reduce:
    STAGES = 8
    SPACE = 2
    SLOTS, LAG = 15, 2

    def __init__(self, far, near_count, half, near, out, scratch):
        self.far, self.near_count, self.half, self.near, self.out = far, near_count, half, near, out
        (self.own, self.r0, self.r1, self.r2, self.r3, self.send, self.recv, self.local) = scratch
        rows, seq = lax.axis_index("rows"), lax.axis_index("seq")
        self.y, self.core, self.z, self.x = rows // 2, rows % 2, seq // 2, seq % 2

    @staticmethod
    def scratch():
        def slot(*shape):
            return pltpu.VMEM(shape + (D,), F32)

        dma, count = pltpu.SemaphoreType.DMA, Reduce.SLOTS
        return [
            slot(3, 128), slot(count, 128), slot(count, 64), slot(count, 32), slot(count, 24),
            dma((12, count)), dma((12, count)), dma((2, count)),
        ]

    def device(self, x, y, z, core):
        return {"rows": y * 2 + core, "seq": z * 2 + x}

    def greet(self):
        barrier = pltpu.get_barrier_semaphore()
        x, y, z, core = self.x, self.y, self.z, self.core
        peers = [(x, y, z, 1 - core), (1 - x, y, z, core), (x, 1 - y, z, core)] + [
            (x, y, lax.rem(z + d, 4), core) for d in (1, 2, 3)]
        for peer in peers:
            pl.semaphore_signal(barrier, inc=1, device_id=self.device(*peer), device_id_type=MESH)

        @pl.when(self.has_next())
        def _():
            pl.semaphore_signal(
                barrier, inc=1, device_id=self.device(1 - x, y, z + 2 * x - 1, core),
                device_id_type=MESH)

    def has_next(self):
        return jnp.where(self.x == 0, self.z > 0, self.z < 3)

    def met(self):
        pl.semaphore_wait(pltpu.get_barrier_semaphore(), 6 + self.has_next().astype(jnp.int32))

    def turn(self, p):
        return lax.rem(p, 2) == 1

    def slot(self, p):
        return jnp.where(p < self.SLOTS, p, p - self.SLOTS)

    def places(self, p):
        x_first = self.turn(p)
        a, b = jnp.where(x_first, self.x, self.y), jnp.where(x_first, self.y, self.x)
        return a * 64, a * 64 + b * 32, a * 64 + b * 32 + self.z * 8

    def copies(self, s, p):
        x, y, z, core = self.x, self.y, self.z, self.core
        i = self.slot(p)
        one, two, three = self.places(p)
        flip_x, flip_y, flip_core = (1 - x, y, z, core), (x, 1 - y, z, core), (x, y, z, 1 - core)

        def mine(start, size):
            return self.r0.at[i, pl.ds(pl.multiple_of(start, 8), size)]

        def final(start, size):
            return self.out.at[pl.ds(pl.multiple_of(p * PIECE + core * 128 + start, 8), size)]

        def copy(src, dst, kind, to):
            return pltpu.make_async_remote_copy(
                src, dst, self.send.at[kind, i], self.recv.at[kind, i],
                device_id=self.device(*to), device_id_type=MESH)

        def over_z(src, dst, kind):
            peers = [(lax.rem(z + d, 4), d - 1) for d in (1, 2, 3)]
            return [copy(src(zz), dst(d), kind + d, (x, y, zz, core)) for zz, d in peers]

        x_first = self.turn(p)
        first = tuple(jnp.where(x_first, u, v) for u, v in zip(flip_x, flip_y))
        second = tuple(jnp.where(x_first, u, v) for u, v in zip(flip_y, flip_x))
        if s == 1:
            return [copy(mine(64 - one, 64), self.r1.at[i], 1, first)]
        if s == 2:
            return [copy(mine(one + 32 - (two - one), 32), self.r2.at[i], 2, second)]
        if s == 3:
            return over_z(
                lambda zz: mine(two + zz * 8, 8), lambda d: self.r3.at[i, pl.ds(8 * d, 8)], 3)
        if s == 4:
            return over_z(lambda zz: mine(three, 8), lambda d: final(three, 8), 6)
        if s == 5:
            return [copy(final(two, 32), final(two, 32), 9, second)]
        if s == 6:
            return [copy(final(one, 64), final(one, 64), 10, first)]
        return [copy(final(0, 128), final(0, 128), 11, flip_core)]

    def near_half(self, p, c):
        return self.near.at[p - self.far, pl.ds(pl.multiple_of(c * 128, 128), 128)]

    def core_copy(self, p, near):
        i = self.slot(p)
        half = (self.near_half if near else self.half)(p, 1 - self.core)
        return pltpu.make_async_remote_copy(
            half, self.r0.at[i], self.send.at[0, i], self.recv.at[0, i],
            device_id=self.device(self.x, self.y, self.z, 1 - self.core), device_id_type=MESH)

    def own_in(self, p):
        return pltpu.make_async_copy(
            self.half(p, self.core), self.own.at[lax.rem(p, 3)], self.local.at[0, self.slot(p)])

    def own_out(self, p):
        i, start = self.slot(p), pl.multiple_of(self.places(p)[2], 8)
        to = p * PIECE + self.core * 128 + start
        return pltpu.make_async_copy(
            self.r0.at[i, pl.ds(start, 8)], self.out.at[pl.ds(pl.multiple_of(to, 8), 8)],
            self.local.at[1, i])

    def begin(self, p):
        @pl.when(p < self.far)
        def _():
            self.own_in(p).start()
            self.core_copy(p, False).start()

        @pl.when(p >= self.far)
        def _():
            self.core_copy(p, True).start()

    def add_core(self, p):
        i = self.slot(p)

        @pl.when(p < self.far)
        def _():
            self.core_copy(p, False).wait()
            self.own_in(p).wait()
            self.r0[i] += self.own[lax.rem(p, 3)]

        @pl.when(p >= self.far)
        def _():
            self.core_copy(p, True).wait()
            self.r0[i] += self.near_half(p, self.core)[...]

    def stage(self, s, p):
        i = self.slot(p)
        starts = self.places(p)
        if s == 1:
            self.add_core(p)
        else:
            for copy in self.copies(s - 1, p):
                copy.wait_recv()

        def kept(which, size):
            return pl.ds(pl.multiple_of(starts[which], 8), size)

        if s == 2:
            self.r0[i, kept(0, 64)] += self.r1[i]
        elif s == 3:
            self.r0[i, kept(1, 32)] += self.r2[i]
        elif s == 4:
            self.r0[i, kept(2, 8)] += self.r3[i, 0:8] + self.r3[i, 8:16] + self.r3[i, 16:24]
            self.own_out(p).start()
        elif s == 5:
            self.own_out(p).wait()
            for done in (1, 2, 3, 4):
                for copy in self.copies(done, p):
                    copy.wait_send()
        if s < self.STAGES:
            for copy in self.copies(s, p):
                copy.start()
        else:
            for done in (5, 6, 7):
                for copy in self.copies(done, p):
                    copy.wait_send()

    def ticks(self):
        return self.far + self.near_count + self.LAG + self.SPACE * self.STAGES

    def tick(self, t):
        for s in range(self.STAGES + 1):
            q = t - self.SPACE * s
            p = jnp.where(q < self.SLOTS, q, q - self.LAG)
            due = jnp.logical_and(q >= 0, p < self.far + self.near_count)
            due = jnp.logical_and(due, jnp.logical_or(q < self.SLOTS, p >= self.SLOTS))

            @pl.when(due)
            def _(s=s, p=p):
                if s == 0:
                    self.begin(p)
                else:
                    self.stage(s, p)


def pieces(x):
    return [x[:, i * STATE : (i + 1) * STATE] for i in range(4)]


START, GAP = 4, 1


def front_kernel(
    n, rows, length, docs,
    tok, ngain, w, weight, cw, cb_i, dtb_i, rate_i, skip_i, starts,
    rounded_o, c_o, p_o, xact_o, y_o, rows_o, q_o, q2_o, pexp_o, sin_o, wide_o, tall_o,
    rext, vhi, vlo, gc, sloc, wst, hsend, hrecv, loads, hs, hr, *scratch,
):
    k = pl.program_id(0)
    chunks = length // C
    blocks = rows * chunks
    ex = Exchange(n, rows, chunks, sloc, sin_o, (0, 1), scratch, START, GAP)
    ex.set_passes(pexp_o)

    def convolved(r, g):
        p = mm(rext[r], w[...], NT)
        p_o[r] = p
        first = PAD - (KW - 1)
        out = wide_o[0:1, cols(g)]
        for i in range(KW):
            out = out + cw[i : i + 1, :] * p[first + i : first + i + length]
        c_o[r * length : (r + 1) * length, :] = out
        return out * sigmoid(out)

    def normed(source):
        scale = lax.rsqrt(jnp.mean(source * source, axis=-1, keepdims=True) + EPS)
        return (source * scale * ngain[...][None, :]).astype(BF16)

    def label_at(r, position):
        found = jnp.int32(0)
        for d in range(docs):
            found += (starts[r, d] <= position).astype(jnp.int32)
        return found.astype(F32)

    def load_steps():
        return pltpu.make_async_copy(
            weight.at[pl.ds(2 * INNER + 4 * STATE, 2 * HEADS)], wst, loads.at[0])

    def halo_copy():
        return pltpu.make_async_remote_copy(
            hsend, hrecv, hs.at[0], hr.at[0],
            device_id={"seq": ex.me + 1}, device_id_type=MESH)

    def tall(ref, count):
        line = jnp.concatenate([ref[...], jnp.zeros((128 - count,), F32)])[None, :]
        return jnp.broadcast_to(line, (8, 128))

    @pl.when(k == 0)
    def _():
        load_steps().start()

        @pl.when(ex.me == 0)
        def _():
            hrecv[...] = jnp.zeros_like(hrecv)

        ex.clear()
        ex.greet(True)
        for r in range(rows):
            hsend[r] = tok[(r + 1) * length - 16 : (r + 1) * length, :].astype(F32)[8:]
        ex.met(True)
        pl.when(ex.me < n - 1)(halo_copy().start)
        for r in range(rows):
            here = slice(r * length, (r + 1) * length)
            out = normed(tok[here, :].astype(F32))
            rext[r, PAD:, :] = out
            rounded_o[here, :] = out
        dtb, rate = tall(dtb_i, 2 * HEADS).T[:48, 0:1], tall(rate_i, 2 * HEADS).T[:48, 0:1]
        lane = iota((48, 128), 1)
        tall_o[...] = jnp.where(lane == 0, dtb, jnp.where(lane == 1, rate, 0.0))
        pick_f, pick_r = pick_all(0), pick_all(2)
        wide_o[0:8, 0:CONV] = jnp.broadcast_to(cb_i[...][None, :], (8, CONV))
        lines = [tall(skip_i, HEADS)]
        upto = (iota((C, C), 0) <= iota((C, C), 1)).astype(BF16)
        load_steps().wait()
        for b in range(blocks):
            here = slice(b * C, (b + 1) * C)
            r, begin = b // chunks, ex.me * length + (b % chunks) * C
            own = jnp.zeros((1, C), F32)
            for d in range(docs):
                own += (starts[r, d] <= begin + iota((1, C), 1)).astype(F32)
            before, first = label_at(r, begin - 1), label_at(r, begin)
            last, after = label_at(r, begin + C - 1), label_at(r, begin + C)
            m0, m1, m2, m3 = [(own == edge).astype(F32) for edge in (before, last, after, first)]
            raw = mm(wst[...], rounded_o[here, :], NT)
            step = softplus(raw + dtb)
            log = -LOG2E * rate * step
            total = mm3(log, upto)
            size = jnp.log(step) * LOG2E
            lf, rc = total[:HEADS], total[HEADS:] - log[HEADS:]
            end_f, end_r = total[:HEADS, C - 1 : C], total[HEADS:, C - 1 : C]
            sf, sr = lf - size[:HEADS], rc + size[HEADS:]
            e_f = jnp.exp2(lf) * m0
            w_f = jnp.exp2(end_f - lf) * step[:HEADS] * m1
            e_r = jnp.exp2(end_r - rc) * m2
            w_r = jnp.exp2(rc) * step[HEADS:] * m3
            labels = jnp.broadcast_to(own, (8, C))
            none = jnp.zeros((24, C), F32)
            rows_o[b] = jnp.concatenate([step, lf, rc, sf, sr, raw, labels], axis=0)
            q = jnp.concatenate([e_f, w_f, e_r, w_r, labels, none], axis=0).T
            q_o[b] = q
            q2_o[b] = jnp.concatenate([lf, rc, sf, sr, labels, none], axis=0).T
            lines += [q[C - 8 :], q[:8]]
        if len(lines) % 2:
            lines.append(lines[0])
        wide_f, wide_r = [mm3(jnp.concatenate(lines, axis=0), pick) for pick in (pick_f, pick_r)]
        wide_o[8:16, 0:INNER] = wide_f[0:8]
        for b in range(blocks):
            pexp_o[b : b + 1, :] = wide_f[16 * b + 15 : 16 * b + 16]
            pexp_o[8 + b : 9 + b, :] = wide_r[16 * b + 16 : 16 * b + 17]
        ex.totals_of_passes()
        pl.when(ex.me > 0)(halo_copy().wait_recv)
        for r in range(rows):
            rext[r, 0:PAD, :] = normed(jnp.concatenate([jnp.zeros((8, D), F32), hrecv[r]], axis=0))
            xact_o[r * length : (r + 1) * length, :] = convolved(r, G)

    @pl.when(jnp.logical_and(k >= 1, k <= G))
    def _():
        g = k - 1
        picks = [pick(1, g), pick(3, g)]
        for r in range(rows):
            v = convolved(r, g)
            hi, lo = split2(v)
            vhi[g, r * length : (r + 1) * length, :] = hi
            vlo[g, r * length : (r + 1) * length, :] = lo
            for c in range(chunks):
                b = r * chunks + c
                vb = v[c * C : (c + 1) * C]
                x = xact_o[b * C : (b + 1) * C, :].astype(BF16)
                for d in range(2):
                    scale = mm2(q_o[b], picks[d])
                    sloc[b, d, :, cols(g)] = mm(
                        x[:, d * STATE : (d + 1) * STATE], (scale * vb).astype(BF16), TN)
        ex.totals(g)
        pl.when(g == 0)(ex.pass_copy().start)
        ex.pair_copy(g).start()

    pl.when(k > 0)(lambda: ex.advance(k - 1))

    @pl.when(k == G + 1)
    def _():
        t_id, s_id = iota((C, C), 0), iota((C, C), 1)
        for b in range(blocks):
            in_f, in_r, rd_f, rd_r = pieces(xact_o[b * C : (b + 1) * C, :])
            gf, gr = mm22(rd_f, in_f, NT), mm22(rd_r, in_r, NT)
            same = jnp.logical_and(q2_o[b][:, 96:97] == rows_o[b, 192:193], t_id != s_id)
            gc[b] = jnp.where(same, jnp.where(t_id > s_id, gf, gr), 0.0)

    @pl.when(jnp.logical_and(k > G, k <= 2 * G))
    def _():
        g = k - 1 - G
        later = iota((C, C), 0) > iota((C, C), 1)
        low = iota((C, 128), 1) < HEAD
        skip = wide_o[8:9, cols(g)]
        for b in range(blocks):
            here = slice(b * C, (b + 1) * C)
            q2 = pltpu.roll(q2_o[b], 128 - HG * g, 1)
            for pair in range(HG // 2):
                at = slice(pair * 128, (pair + 1) * 128)
                v2 = jnp.concatenate([vhi[g, here, at], vlo[g, here, at]], axis=1)
                outs = []
                for h in (2 * pair, 2 * pair + 1):
                    lt, rt = q2[:, h : h + 1], q2[:, HEADS + h : HEADS + h + 1]
                    ls = rows_o[b, pl.ds(96 + HG * g + h, 1), :]
                    rs = rows_o[b, pl.ds(96 + HEADS + HG * g + h, 1), :]
                    x = jnp.exp2(jnp.where(later, lt - ls, rs - rt))
                    o = mm((gc[b] * x).astype(BF16), v2)
                    outs.append(o[:, :128] + o[:, 128:])
                v = vhi[g, here, at].astype(F32) + vlo[g, here, at].astype(F32)
                y_o[here, at] = jnp.where(low, outs[0], outs[1]) + skip[:, at] * v

    @pl.when(k == pl.num_programs(0) - 1)
    def _():
        ex.finish()
        pl.when(ex.me < n - 1)(halo_copy().wait_send)


def middle_kernel(
    y, rounded, tok, cot, q, xact, sin, wg, wo, ogain,
    mixed_o, dy_o, drounded_o, ds_o, dread_o, dq_o, ogain_grad, w_grad,
    outs, dgates,
):
    k = pl.program_id(0)
    here = pl.ds(pl.multiple_of(k * C, C), C)
    rounded_b, cot_b = rounded[here, :], cot[here, :]
    x = xact[...].astype(BF16)
    rd_f, rd_r = x[:, 2 * STATE : 3 * STATE], x[:, 3 * STATE :]
    s_f, s_r = sin[0, 0].astype(BF16), sin[0, 1].astype(BF16)
    pick_f, pick_r = pick_all(0), pick_all(2)
    factors = q[0].astype(BF16)
    e_f, e_r = mm(factors, pick_f), mm(factors, pick_r)
    r_f, r_r = mm(rd_f, s_f), mm(rd_r, s_r)
    yv = y[...] + e_f * r_f + e_r * r_r
    gate = mm(rounded_b, wg[...], NT)
    sg = sigmoid(gate)
    silu = gate * sg
    gated = yv * silu
    scale = lax.rsqrt(jnp.mean(gated * gated, axis=-1, keepdims=True) + EPS)
    normed = gated * scale
    out = (normed * ogain[...][None, :]).astype(BF16)
    outs[here, :] = out
    mixed_o[...] = (tok[...].astype(F32) + mm(out, wo[...])).astype(BF16)
    dout = mm(cot_b, wo[...], NT)
    go = jnp.sum(dout * normed, axis=0, keepdims=True)
    dn = dout * ogain[...][None, :]
    dgated = scale * (dn - normed * jnp.mean(dn * normed, axis=-1, keepdims=True))
    dy = dgated * silu
    dy_o[...] = dy
    dgate = (dgated * yv * sg * (1.0 + gate * (1.0 - sg))).astype(BF16)
    dgates[here, :] = dgate
    drounded_o[...] = mm(dgate, wg[...])
    u_f, u_r = e_f * dy, e_r * dy
    dq_o[0] = mm((u_f * r_f).astype(BF16), pick_f, NT) + mm((u_r * r_r).astype(BF16), pick_r, NT)
    u_f, u_r = u_f.astype(BF16), u_r.astype(BF16)
    ds_o[0, 1] = mm(rd_f, u_f, TN)
    ds_o[0, 0] = mm(rd_r, u_r, TN)
    dread_o[...] = jnp.concatenate([mm(u_f, s_f, NT), mm(u_r, s_r, NT)], axis=1)

    @pl.when(k == 0)
    def _():
        ogain_grad[...] = jnp.broadcast_to(go, ogain_grad.shape)

    @pl.when(k > 0)
    def _():
        ogain_grad[...] += go

    @pl.when(k == pl.num_programs(0) - 1)
    def _():
        for i in range(G):
            at = slice(i * GC, (i + 1) * GC)
            w_grad[at] = mm(dgates[:, at], rounded[...], TN)
            w_grad[INNER + i * GC : INNER + (i + 1) * GC] = mm(outs[:, at], cot[...], TN)


def steps_backward(dq, col, row, pg_f, pg_r, raw, step, rate):
    from_t = (iota((C, C), 0) >= iota((C, C), 1)).astype(BF16)
    after_t = (iota((C, C), 0) > iota((C, C), 1)).astype(BF16)
    e_f, w_f, e_r, w_r = [dq[i * HEADS : (i + 1) * HEADS] for i in range(4)]
    cs_f, cs_r = col[:HEADS], col[HEADS : 2 * HEADS]
    d_lf = row[:HEADS] - cs_f + e_f - w_f
    d_rc = cs_r - row[HEADS:] - e_r + w_r
    d_size = jnp.concatenate([cs_f + w_f, cs_r + w_r], axis=0)
    end_f = jnp.sum(w_f, axis=1, keepdims=True) + pg_f
    end_r = jnp.sum(e_r, axis=1, keepdims=True) + pg_r
    d_log = jnp.concatenate([mm3(d_lf, from_t) + end_f, mm3(d_rc, after_t) + end_r], axis=0)
    sg = sigmoid(raw)
    ratio = jnp.where(raw < -15.0, 1.0, sg / jnp.maximum(step, 1e-30))
    d_raw = -rate * d_log * sg + d_size * ratio
    bias = jnp.sum(d_raw, axis=1, keepdims=True)
    rates = -jnp.sum(step * d_log, axis=1, keepdims=True)
    at = iota((2 * HEADS, 128), 1)
    return d_raw, jnp.where(at == 0, bias, jnp.where(at == 1, rates, 0.0))


def back_kernel(
    n, rows, length, far, shared,
    c_i, dy_i, p_i, cw, w, sin,
    xact, rows_i, q_i, q2_i, pexp, dread, dq_i, wide, tall,
    rounded, tok, cot, ngain, ogain_grad,
    ds_i, drounded, w_grad, weight,
    tg_o, total_o, *scratch,
):
    (gct, dgt, dvs, dss, dts, dqs, dins, pgs, z, acc, draw, wst, near, hsend, hrecv, loads, hs, hr) = (
        scratch[:18])
    k = pl.program_id(0)
    chunks = length // C
    blocks = rows * chunks
    near_count = G + 2
    st = near if shared else total_o
    ex = Exchange(n, rows, chunks, z, z, (1, 0), scratch[18:29])
    ex.set_passes(pexp)
    later = iota((C, C), 1) > iota((C, C), 0)
    if shared:

        def half(p, c):
            return w_grad.at[pl.ds(pl.multiple_of(p * PIECE + c * 128, 128), 128)]

        red = Reduce(2 * INNER // PIECE, near_count, half, near, total_o, scratch[29:])

    def load_states():
        return pltpu.make_async_copy(ds_i, z, loads.at[0])

    def load_sum():
        return pltpu.make_async_copy(drounded, acc, loads.at[1])

    def load_steps():
        return pltpu.make_async_copy(
            weight.at[pl.ds(2 * INNER + 4 * STATE, 2 * HEADS)], wst, loads.at[2])

    def halo_copy(g):
        return pltpu.make_async_remote_copy(
            hsend.at[g], hrecv.at[g], hs.at[g], hr.at[g],
            device_id={"seq": ex.me - 1}, device_id_type=MESH)

    @pl.when(k == 0)
    def _():
        load_states().start()
        load_sum().start()
        load_steps().start()

        @pl.when(ex.me == n - 1)
        def _():
            hrecv[...] = jnp.zeros_like(hrecv)

        ex.clear()
        if shared:
            red.greet()
        else:
            ex.greet(True)
        ex.totals_of_passes()
        load_states().wait()

        @pl.loop(0, G)
        def _(g):
            ex.totals(g)

        if shared:
            red.met()
        else:
            ex.met(True)
        ex.pass_copy().start()

        @pl.loop(0, G)
        def _(g):
            ex.pair_copy(g).start()

        differ = iota((C, C), 0) != iota((C, C), 1)
        for b in range(blocks):
            in_f, in_r, rd_f, rd_r = pieces(xact[b * C : (b + 1) * C, :])
            gf, gr = mm22(in_f, rd_f, NT), mm22(in_r, rd_r, NT)
            same = jnp.logical_and(q2_i[b][:, 96:97] == rows_i[b, 192:193], differ)
            gct[b] = jnp.where(same, jnp.where(later, gf, gr), 0.0)
        dgt[...] = jnp.zeros_like(dgt)
        dss[...] = jnp.zeros_like(dss)
        dins[...] = jnp.zeros_like(dins)
        pgs[...] = jnp.zeros_like(pgs)
        dqs[...] = dq_i[...]
        st[G + 1] = jnp.zeros((PIECE, D), F32)
        load_sum().wait()
        load_steps().wait()

    @pl.when(k < G)
    def _():
        g = k
        low = iota((C, 128), 1) < HEAD
        lane = iota((C, 128), 1)
        ones = jnp.ones((8, C), BF16)
        skips = jnp.zeros((1, GC), F32)
        skip = wide[8:9, cols(g)]
        for b in range(blocks):
            here = slice(b * C, (b + 1) * C)
            q2 = pltpu.roll(q2_i[b], 128 - HG * g, 1)
            cv = c_i[here, :]
            v = cv * sigmoid(cv)
            dy = dy_i[here, :]
            skips += jnp.sum(dy * v, axis=0, keepdims=True)
            dyhi, dylo = split2(dy)
            vb = v.astype(BF16)
            for pair in range(HG // 2):
                at = slice(pair * 128, (pair + 1) * 128)
                dy2 = jnp.concatenate([dyhi[:, at], dylo[:, at]], axis=1)
                outs = []
                for i in range(2):
                    h = 2 * pair + i
                    mine = low if i == 0 else jnp.logical_not(low)
                    dyh = jnp.where(mine, dyhi[:, at], jnp.zeros((), BF16))
                    dw = mm(vb[:, at], dyh, NT)
                    lt = rows_i[b, pl.ds(48 + HG * g + h, 1), :]
                    rt = rows_i[b, pl.ds(48 + HEADS + HG * g + h, 1), :]
                    ls, rs = q2[:, 48 + h : 49 + h], q2[:, 72 + h : 73 + h]
                    x = jnp.exp2(jnp.where(later, lt - ls, rs - rt))
                    dwx = dw * x
                    dgt[b] += dwx
                    gb = gct[b]
                    o = mm((gb * x).astype(BF16), dy2)
                    outs.append(o[:, :128] + o[:, 128:])
                    de = dwx * gb
                    de_f = jnp.where(later, de, 0.0).astype(BF16)
                    de_r = jnp.where(later, 0.0, de).astype(BF16)
                    hot_f = (lane == HG * g + h).astype(BF16)
                    hot_r = (lane == HEADS + HG * g + h).astype(BF16)
                    dss[b] += mm(de_f, hot_f) + mm(de_r, hot_r)
                    dts[b, pl.ds(HG * g + h, 1), :] = mm(ones, de_f)[0:1]
                    dts[b, pl.ds(HEADS + HG * g + h, 1), :] = mm(ones, de_r)[0:1]
                dvs[g, here, at] = jnp.where(low, outs[0], outs[1]) + skip[:, at] * dy[:, at]
        line = pl.multiple_of(120 + 8 * (g // 3), 8)
        st[G + 1, pl.ds(line, 8), cols(lax.rem(g, 3))] = jnp.broadcast_to(skips, (8, GC))

    ex.advance(k)

    def send_halo(g):
        for r in range(rows):
            hsend[g, r] = dvs[g, r * length : r * length + 8, :]
        pl.when(ex.me > 0)(halo_copy(g).start)

    @pl.when(jnp.logical_and(k >= far, k < far + G))
    def _():
        g = k - far
        picks = [pick(1, g), pick(3, g)]
        for b in range(blocks):
            here = slice(b * C, (b + 1) * C)
            cv = c_i[here, :]
            sg = sigmoid(cv)
            v = cv * sg
            x = xact[here, :].astype(BF16)
            dv = dvs[g, here, :]
            for d in range(2):
                zf = z[b, 1 - d, :, cols(g)]
                zb = zf.astype(BF16)
                weight = mm2(q_i[b], picks[d])
                m = mm(x[:, d * STATE : (d + 1) * STATE], zb)
                dv += weight * m
                u = weight * v
                dqs[b] += mm2(u * m, picks[d], NT)
                at = slice(d * STATE, (d + 1) * STATE)
                dins[b, :, at] += mm(u.astype(BF16), zb, NT)
                pgs[8 * d + b : 8 * d + b + 1, cols(g)] = pexp[
                    8 * d + b : 8 * d + b + 1, cols(g)
                ] * jnp.sum(zf * sin[b, d], axis=0, keepdims=True)
            dvs[g, here, :] = dv * (sg * (1.0 + cv * (1.0 - sg)))
        send_halo(g)

    @pl.when(k == far + G)
    def _():
        differ = iota((C, C), 0) != iota((C, C), 1)
        for b in range(blocks):
            here = slice(b * C, (b + 1) * C)
            same = jnp.logical_and(q2_i[b][:, 96:97] == rows_i[b, 192:193], differ)
            dg = jnp.where(same, dgt[b], 0.0)
            dg_f = jnp.where(later, dg, 0.0).astype(BF16)
            dg_r = jnp.where(later, 0.0, dg).astype(BF16)
            in_f, in_r, rd_f, rd_r = pieces(xact[here, :].astype(BF16))
            dx = jnp.concatenate(
                [
                    dins[b, :, :STATE] + mm(dg_f, rd_f),
                    dins[b, :, STATE:] + mm(dg_r, rd_r),
                    dread[here, :STATE] + mm(dg_f, in_f, TN),
                    dread[here, STATE:] + mm(dg_r, in_r, TN),
                ],
                axis=1,
            )
            cv = c_i[here, :]
            sg = sigmoid(cv)
            dvs[G, here, :] = dx * (sg * (1.0 + cv * (1.0 - sg)))
        send_halo(G)
        pg_f = mm2(pgs[...], pick_all(0), NT)[0:8].T
        pg_r = mm2(pgs[...], pick_all(2), NT)[8:16].T
        sums = jnp.zeros((2 * HEADS, 128), F32)
        for b in range(blocks):
            d_raw, small = steps_backward(
                dqs[b].T, dss[b].T, dts[b], pg_f[:HEADS, b : b + 1],
                pg_r[2 * HEADS : 3 * HEADS, b : b + 1], rows_i[b, 144:192] + tall[:, 0:1],
                rows_i[b, 0:48], tall[:, 1:2])
            draw[:, b * C : (b + 1) * C] = d_raw.astype(BF16)
            sums += small
        st[G + 1, 0:48] = mm(draw[...], rounded[...])
        st[G + 1, 48:96, 0:128] = sums

    @pl.when(k > far)
    def _():
        g = k - far - 1
        pl.when(ex.me < n - 1)(halo_copy(g).wait_recv)
        parts = []
        taps = [jnp.zeros((1, GC), F32) for _ in range(KW)]
        bias = jnp.zeros((1, GC), F32)
        for r in range(rows):
            own = dvs[g, r * length : (r + 1) * length, :]
            ext = jnp.concatenate([own, hrecv[g, r]], axis=0)
            total = None
            for i in range(KW):
                one = cw[i : i + 1, :] * ext[KW - 1 - i : KW - 1 - i + length]
                total = one if total is None else total + one
                first = PAD - (KW - 1) + i
                taps[i] += jnp.sum(own * p_i[r, first : first + length, :], axis=0, keepdims=True)
            bias += jnp.sum(own, axis=0, keepdims=True)
            parts.append(total.astype(BF16))
        both = jnp.concatenate(parts, axis=0)
        st[g] = mm(both, rounded[...], TN)
        line = pl.multiple_of(136 + 8 * (g // 3), 8)
        st[G + 1, pl.ds(line, 8), cols(lax.rem(g, 3))] = jnp.concatenate(
            taps + [bias, jnp.zeros((3, GC), F32)], axis=0)
        acc[...] += mm(both, w[...])

    def until(k):
        return jnp.clip(2 * (k - 2), 0, k + far + 1)

    if shared:

        @pl.loop(jnp.where(k == 0, 0, until(k - 1)), until(k))
        def _(t):
            red.tick(t)

    @pl.when(k == far + G + 1)
    def _():
        acc[...] += mm(draw[...], wst[...], TN)
        gains = jnp.zeros((1, D), F32)
        for b in range(blocks):
            here = slice(b * C, (b + 1) * C)
            source = tok[here, :].astype(F32)
            scale = lax.rsqrt(jnp.mean(source * source, axis=-1, keepdims=True) + EPS)
            m = source * scale
            d_rounded = acc[here, :]
            gains += jnp.sum(d_rounded * m, axis=0, keepdims=True)
            nn = d_rounded * ngain[...][None, :]
            d_source = scale * (nn - m * jnp.mean(nn * m, axis=-1, keepdims=True))
            tg_o[here, :] = (cot[here, :].astype(F32) + d_source).astype(BF16)
        st[G + 1, 96:104] = jnp.broadcast_to(gains, (8, D))
        for i in range(2):
            st[G + 1, 104 + 8 * i : 112 + 8 * i] = ogain_grad[:, i * D : (i + 1) * D]
        if shared:

            @pl.loop(until(k), red.ticks())
            def _(t):
                red.tick(t)

        ex.finish()

        @pl.loop(0, G + 1)
        def _(g):
            pl.when(ex.me > 0)(halo_copy(g).wait_send)


def finish_kernel(
    total, in_o, out_o, ng_o, cw_o, cb_o, dtb_o, rate_o, skip_o, og_o, held, arrive, leave,
):
    count = total.shape[0] // PIECE
    gates = INNER // PIECE

    def read(i):
        return pltpu.make_async_copy(
            total.at[pl.ds(i * PIECE, PIECE)], held.at[i], arrive.at[i])

    def write(i):
        size = PIECE
        if i < gates:
            to = in_o.at[pl.ds(i * PIECE, PIECE)]
        elif i < 2 * gates:
            to = out_o.at[pl.ds((i - gates) * PIECE, PIECE)]
        else:
            size = PIECE if i < count - 1 else 2 * HEADS
            to = in_o.at[pl.ds((i - gates) * PIECE, size)]
        return pltpu.make_async_copy(held.at[i, pl.ds(0, size)], to, leave.at[i])

    for i in range(count):
        read(i).start()
    for i in range(count):
        read(i).wait()
        write(i).start()
    rest = held.at[count - 1]
    ng_o[...] = rest[96:97, :][0]
    og_o[...] = jnp.concatenate([rest[104:105, :], rest[112:113, :]], axis=1)[0]
    lines = jnp.concatenate([rest[120:128, :], rest[128:136, :]], axis=1)
    skip_o[...] = mm3(jnp.concatenate([lines, lines], axis=0), pick_all(0), NT)[0, 0:HEADS]
    both = jnp.concatenate([rest[48:96, 0:128], jnp.zeros((80, 128), F32)], axis=0).T
    dtb_o[...] = both[0, 0 : 2 * HEADS]
    rate_o[...] = both[1, 0 : 2 * HEADS]
    taps = jnp.concatenate([rest[136:144, :], rest[144:152, :], rest[152:160, :GC]], axis=1)
    cw_o[...] = taps[:KW]
    cb_o[...] = taps[KW]
    for i in range(count):
        write(i).wait()


def whole(shape):
    zeros = (0,) * len(shape)
    return pl.BlockSpec(shape, lambda k: zeros, pipeline_mode=pl.Buffered(1))


def struct(shape, dtype=F32):
    return jax.ShapeDtypeStruct(shape, dtype)


def on_device(
    tokens, doc_starts, norm_gain, in_weight, conv_weight, conv_bias, dt_bias, decay_rate,
    skip_scale, out_gain, out_weight, cotangent,
):
    n = lax.axis_size("seq")
    rows, length, _ = tokens.shape
    docs = doc_starts.shape[1]
    chunks = length // C
    blocks = rows * chunks
    count = rows * length
    weight = in_weight.T
    tok, cot = tokens.reshape(count, D), cotangent.reshape(count, D)
    anywhere = pl.BlockSpec(memory_space=pl.ANY)

    params = dict(vmem_limit_bytes=VMEM_LIMIT)
    dims = ("arbitrary",)

    def col(k):
        return jnp.where(k == 0, G, jnp.minimum(k - 1, G - 1))

    def ycol(k):
        return jnp.clip(k - 1 - G, 0, G - 1)

    front_steps = max(2 * G, START + GAP * (G - 1) + n // 2) + 1
    rounded, c, p, xact, y, rowsv, q, q2, pexp, sin, wide, tall = pl.pallas_call(
        lambda *refs: front_kernel(n, rows, length, docs, *refs),
        grid=(front_steps,),
        in_specs=[
            whole((count, D)), whole((D,)),
            pl.BlockSpec((GC, D), lambda k: (G + col(k), 0)), anywhere,
            pl.BlockSpec((KW, GC), lambda k: (0, col(k))),
            whole((CONV,)), whole((2 * HEADS,)), whole((2 * HEADS,)), whole((HEADS,)),
            pl.BlockSpec(memory_space=pltpu.SMEM),
        ],
        out_specs=[
            whole((count, D)),
            pl.BlockSpec((count, GC), lambda k: (0, col(k))),
            pl.BlockSpec((rows, PAD + length, GC), lambda k: (0, 0, col(k))),
            whole((count, GC)),
            pl.BlockSpec((count, GC), lambda k: (0, ycol(k))),
            whole((blocks, 200, C)), whole((blocks, C, 128)), whole((blocks, C, 128)),
            whole((16, INNER)), whole((blocks, 2, STATE, INNER)), whole((16, CONV)),
            whole((2 * HEADS, 128)),
        ],
        out_shape=[
            struct((count, D), BF16), struct((count, CONV)), struct((rows, PAD + length, CONV)),
            struct((count, GC)), struct((count, INNER)), struct((blocks, 200, C)),
            struct((blocks, C, 128)), struct((blocks, C, 128)), struct((16, INNER)),
            struct((blocks, 2, STATE, INNER)), struct((16, CONV)), struct((2 * HEADS, 128)),
        ],
        scratch_shapes=[
            pltpu.VMEM((rows, PAD + length, D), BF16),
            pltpu.VMEM((G, count, GC), BF16), pltpu.VMEM((G, count, GC), BF16),
            pltpu.VMEM((blocks, C, C), F32), pltpu.VMEM((blocks, 2, STATE, INNER), F32),
            pltpu.VMEM((2 * HEADS, D), BF16),
            pltpu.VMEM((rows, 8, D), F32), pltpu.VMEM((rows, 8, D), F32),
            pltpu.SemaphoreType.DMA((1,)), pltpu.SemaphoreType.DMA((1,)),
            pltpu.SemaphoreType.DMA((1,)),
            *Exchange.scratch(rows),
        ],
        compiler_params=pltpu.CompilerParams(
            dimension_semantics=dims, collective_id=0, has_side_effects=True, **params),
        name="front",
    )(tok, norm_gain, weight, weight, conv_weight, conv_bias, dt_bias, decay_rate, skip_scale,
      doc_starts)

    def by_block(shape):
        zeros = (0,) * (len(shape) - 1)
        return pl.BlockSpec(shape, lambda k: (k,) + zeros)

    mixed, dy, drounded, ds, dread, dq, ogain_grad, w_grad = pl.pallas_call(
        middle_kernel,
        grid=(blocks,),
        in_specs=[
            by_block((C, INNER)), whole((count, D)), by_block((C, D)), whole((count, D)),
            by_block((1, C, 128)), by_block((C, GC)), by_block((1, 2, STATE, INNER)),
            whole((INNER, D)), whole((INNER, D)), whole((INNER,)),
        ],
        out_specs=[
            by_block((C, D)), by_block((C, INNER)), by_block((C, D)),
            by_block((1, 2, STATE, INNER)), by_block((C, 128)), by_block((1, C, 128)),
            whole((8, INNER)), whole((2 * INNER, D)),
        ],
        out_shape=[
            struct((count, D), BF16), struct((count, INNER)), struct((count, D)),
            struct((blocks, 2, STATE, INNER)), struct((count, 128)), struct((blocks, C, 128)),
            struct((8, INNER)), struct((2 * INNER, D)),
        ],
        scratch_shapes=[pltpu.VMEM((count, INNER), BF16), pltpu.VMEM((count, INNER), BF16)],
        compiler_params=pltpu.CompilerParams(dimension_semantics=dims, **params),
        name="middle",
    )(y, rounded, tok, cot, q, xact, sin, weight, out_weight, out_gain)

    far = max(G, n // 2 + 1)
    shared = n == 8 and lax.axis_size("rows") == 4

    def vcol(k):
        return jnp.where(k < far, jnp.minimum(k, G - 1), jnp.minimum(k - far, G))

    def first_pass(k):
        return jnp.minimum(k, G - 1)

    def second_pass(k):
        return jnp.clip(k - far, 0, G - 1)

    def conv_pass(k):
        return jnp.clip(k - far - 1, 0, G)

    far_pieces = 2 * INNER // PIECE
    total_rows = (far_pieces + G + 2) * PIECE
    tg, total = pl.pallas_call(
        lambda *refs: back_kernel(n, rows, length, far, shared, *refs),
        grid=(far + G + 2,),
        in_specs=[
            pl.BlockSpec((count, GC), lambda k: (0, vcol(k))),
            pl.BlockSpec((count, GC), lambda k: (0, first_pass(k))),
            pl.BlockSpec((rows, PAD + length, GC), lambda k: (0, 0, conv_pass(k))),
            pl.BlockSpec((KW, GC), lambda k: (0, conv_pass(k))),
            pl.BlockSpec((GC, D), lambda k: (G + conv_pass(k), 0)),
            pl.BlockSpec((blocks, 2, STATE, GC), lambda k: (0, 0, 0, second_pass(k))),
            whole((count, GC)), whole((blocks, 200, C)), whole((blocks, C, 128)),
            whole((blocks, C, 128)), whole((16, INNER)), whole((count, 128)),
            whole((blocks, C, 128)), whole((16, CONV)), whole((2 * HEADS, 128)),
            whole((count, D)), whole((count, D)), whole((count, D)), whole((D,)),
            whole((8, INNER)), anywhere, anywhere, anywhere, anywhere,
        ],
        out_specs=[whole((count, D)), anywhere if shared else whole((G + 2, PIECE, D))],
        out_shape=[
            struct((count, D), BF16),
            struct((total_rows, D) if shared else (G + 2, PIECE, D)),
        ],
        scratch_shapes=[
            pltpu.VMEM((blocks, C, C), F32), pltpu.VMEM((blocks, C, C), F32),
            pltpu.VMEM((G + 1, count, GC), F32), pltpu.VMEM((blocks, C, 128), F32),
            pltpu.VMEM((blocks, 2 * HEADS, C), F32), pltpu.VMEM((blocks, C, 128), F32),
            pltpu.VMEM((blocks, C, 128), F32), pltpu.VMEM((16, INNER), F32),
            pltpu.VMEM((blocks, 2, STATE, INNER), F32), pltpu.VMEM((count, D), F32),
            pltpu.VMEM((2 * HEADS, count), BF16), pltpu.VMEM((2 * HEADS, D), BF16),
            pltpu.VMEM((G + 2, PIECE, D) if shared else (8, 128), F32),
            pltpu.VMEM((G + 1, rows, 8, GC), F32), pltpu.VMEM((G + 1, rows, 8, GC), F32),
            pltpu.SemaphoreType.DMA((3,)), pltpu.SemaphoreType.DMA((G + 1,)),
            pltpu.SemaphoreType.DMA((G + 1,)),
            *Exchange.scratch(rows), *(Reduce.scratch() if shared else []),
        ],
        compiler_params=pltpu.CompilerParams(
            dimension_semantics=dims, collective_id=1, has_side_effects=True,
            vmem_limit_bytes=63 * 1024 * 1024),
        name="back",
    )(c, dy, p, conv_weight, weight, sin, xact, rowsv, q, q2, pexp, dread, dq, wide, tall,
      rounded, tok, cot, norm_gain, ogain_grad, ds, drounded, w_grad, weight)

    if not shared:
        total = lax.psum(jnp.concatenate([w_grad, total.reshape(-1, D)], axis=0), ("rows", "seq"))
    held = total_rows // PIECE
    inside = pl.BlockSpec(memory_space=pltpu.VMEM)
    in_grad, out_grad, ng, cw, cb, dtb, rate, skip, og = pl.pallas_call(
        finish_kernel,
        in_specs=[anywhere],
        out_specs=[anywhere, anywhere] + [inside] * 7,
        out_shape=[
            struct((2 * INNER + 4 * STATE + 2 * HEADS, D)), struct((INNER, D)), struct((D,)),
            struct((KW, CONV)), struct((CONV,)), struct((2 * HEADS,)), struct((2 * HEADS,)),
            struct((HEADS,)), struct((INNER,)),
        ],
        scratch_shapes=[
            pltpu.VMEM((held, PIECE, D), F32), pltpu.SemaphoreType.DMA((held,)),
            pltpu.SemaphoreType.DMA((held,)),
        ],
        compiler_params=pltpu.CompilerParams(**params),
        name="finish",
    )(total)
    return (
        mixed.reshape(tokens.shape), tg.reshape(tokens.shape), ng, in_grad.T, cw, cb, dtb, rate,
        skip, og, out_grad,
    )


def solution(mesh):
    local = P("rows", "seq", None)
    return jax.shard_map(
        on_device,
        mesh=mesh,
        in_specs=(local, P("rows", None)) + (P(),) * 9 + (local,),
        out_specs=(local, local) + (P(),) * 9,
        check_vma=False,
    )
```

```python
import jax
import jax.numpy as jnp
from jax import lax
from jax.experimental import pallas as pl
from jax.experimental.pallas import tpu as pltpu
from jax.sharding import PartitionSpec as P

D = 768
INNER = 1536
HEADS = 24
HEAD = 64
STATE = 64
KW = 4
EPS = 1e-05

C = 256
GC = 256
G = INNER // GC
HG = GC // HEAD
CONV = INNER + 4 * STATE
PAD = 16
LOG2E = 1.4426950408889634
F32, BF16 = jnp.float32, jnp.bfloat16
NN, NT, TN = ((1,), (0,)), ((1,), (1,)), ((0,), (0,))
MESH = pl.DeviceIdType.MESH
VMEM_LIMIT = 60 * 1024 * 1024


def mm(a, b, dims=NN):
    return lax.dot_general(a, b, (dims, ((), ())), preferred_element_type=F32)


def split2(a):
    hi = a.astype(BF16)
    return hi, (a - hi.astype(F32)).astype(BF16)


def split3(a):
    hi = a.astype(BF16)
    rest = a - hi.astype(F32)
    mid = rest.astype(BF16)
    return hi, mid, (rest - mid.astype(F32)).astype(BF16)


def mm2(a, b, dims=NN):
    count = a.shape[0]
    both = mm(jnp.concatenate(split2(a), axis=0), b, dims)
    return both[:count] + both[count:]


def mm3(a, b, dims=NN):
    count = a.shape[0]
    every = mm(jnp.concatenate(split3(a), axis=0), b, dims)
    return every[:count] + every[count : 2 * count] + every[2 * count :]


def mm22(a, b, dims=NN):
    ahi, alo = split2(a)
    bhi, blo = split2(b)
    return mm(ahi, bhi, dims) + mm(alo, bhi, dims) + mm(ahi, blo, dims)


def sigmoid(x):
    return 1.0 / (1.0 + jnp.exp(-x))


def softplus(x):
    return jnp.maximum(x, 0.0) + jnp.log1p(jnp.exp(-jnp.abs(x)))


def iota(shape, dim):
    return lax.broadcasted_iota(jnp.int32, shape, dim)


def pick(kind, g):
    return (iota((128, GC), 0) == kind * HEADS + HG * g + (iota((128, GC), 1) >> 6)).astype(BF16)


def pick_all(kind):
    return (iota((128, INNER), 0) == kind * HEADS + (iota((128, INNER), 1) >> 6)).astype(BF16)


def cols(g, width=GC):
    return pl.ds(pl.multiple_of(g * width, width), width)


class Exchange:
    def __init__(self, n, rows, chunks, x_ref, y_ref, passes, scratch, start=1, gap=1):
        self.n, self.rows, self.chunks, self.start, self.gap = n, rows, chunks, start, gap
        self.x, self.y, self.passes = x_ref, y_ref, passes
        (self.st, self.rp, self.qr, self.pm, self.pp) = scratch[:5]
        (self.ps, self.pr, self.as_, self.ar, self.bs, self.br) = scratch[5:]
        self.me = lax.axis_index("seq")
        self.partner = self.me + 1 - 2 * (self.me % 2)
        self.has_before = self.me >= 2
        self.has_after = self.me < n - 2

    @staticmethod
    def scratch(rows):
        state = pltpu.VMEM((G, 2, rows, STATE, GC), F32)
        small = pltpu.VMEM((8, INNER), F32)
        dma = pltpu.SemaphoreType.DMA
        return [
            state, state, state, small, small,
            dma((1,)), dma((1,)), dma((G,)), dma((G,)), dma((2, G)), dma((2, G)),
        ]

    def clear(self):
        @pl.when(jnp.logical_not(self.has_before))
        def _():
            self.qr[:, 0] = jnp.zeros_like(self.qr[:, 0])

        @pl.when(jnp.logical_not(self.has_after))
        def _():
            self.qr[:, 1] = jnp.zeros_like(self.qr[:, 1])

    def peers(self, halo):
        found = [(self.partner, True), (self.me - 2, self.has_before), (self.me + 2, self.has_after)]
        if halo:
            other = 2 * self.me - self.partner
            found.append((other, jnp.logical_and(other >= 0, other < self.n)))
        return found

    def greet(self, halo=False):
        for to, there in self.peers(halo):

            @pl.when(there)
            def _(to=to):
                pl.semaphore_signal(
                    pltpu.get_barrier_semaphore(), inc=1, device_id={"seq": to}, device_id_type=MESH)

    def met(self, halo=False):
        count = sum(jnp.asarray(there, jnp.int32) for _, there in self.peers(halo))
        pl.semaphore_wait(pltpu.get_barrier_semaphore(), count)

    def pass_copy(self):
        return pltpu.make_async_remote_copy(
            self.pm, self.pp, self.ps.at[0], self.pr.at[0],
            device_id={"seq": self.partner}, device_id_type=MESH)

    def pair_copy(self, g):
        return pltpu.make_async_remote_copy(
            self.st.at[g], self.rp.at[g], self.as_.at[g], self.ar.at[g],
            device_id={"seq": self.partner}, device_id_type=MESH)

    def chain_copy(self, d, g):
        return pltpu.make_async_remote_copy(
            self.st.at[g, d], self.qr.at[g, d], self.bs.at[d, g], self.br.at[d, g],
            device_id={"seq": self.me + 2 if d == 0 else self.me - 2}, device_id_type=MESH)

    def order(self, d):
        return range(self.chunks) if d == 0 else range(self.chunks - 1, -1, -1)

    def passing(self, d, b, where):
        row = 8 * self.passes[d] + b
        return self.p_ref[row : row + 1, where]

    def set_passes(self, p_ref):
        self.p_ref = p_ref

    def totals_of_passes(self):
        self.pm[...] = jnp.zeros_like(self.pm)
        for d in range(2):
            for r in range(self.rows):
                total = None
                for c in self.order(d):
                    one = self.passing(d, r * self.chunks + c, slice(None))
                    total = one if total is None else total * one
                self.pm[d * self.rows + r : d * self.rows + r + 1, :] = total

    def totals(self, g):
        for d in range(2):
            for r in range(self.rows):
                total = None
                for c in self.order(d):
                    b = r * self.chunks + c
                    one = self.x[b, d, :, cols(g)]
                    total = one if total is None else self.passing(d, b, cols(g)) * total + one
                self.st[g, d, r] = total

    def chain(self, d, g):
        has_in, has_out = (
            (self.has_before, self.has_after) if d == 0 else (self.has_after, self.has_before))
        copy = self.chain_copy(d, g)
        pl.when(has_in)(copy.wait_recv)
        first = self.me % 2 == d
        for r in range(self.rows):
            row = d * self.rows + r
            mine, theirs = self.st[g, d, r], self.rp[g, d, r]
            p_mine = self.pm[row : row + 1, cols(g)]
            p_theirs = self.pp[row : row + 1, cols(g)]
            before = self.qr[g, d, r]
            middle = jnp.where(first, p_mine, p_theirs) * before + jnp.where(first, mine, theirs)
            self.st[g, d, r] = (
                jnp.where(first, p_theirs, p_mine) * middle + jnp.where(first, theirs, mine))
            state = jnp.where(first, before, middle)
            order = list(self.order(d))
            for i, c in enumerate(order):
                b = r * self.chunks + c
                here = state
                if i < len(order) - 1:
                    state = (
                        self.passing(d, b, cols(g)) * state + self.x[b, d, :, cols(g)])
                self.y[b, d, :, cols(g)] = here
        pl.when(has_out)(copy.start)

    def advance(self, step):
        late = self.n // 2 - 1
        place = self.me // 2

        def due(delay, run):
            q = step - self.start - delay
            g = lax.div(jnp.maximum(q, 0), self.gap)
            pl.when(jnp.logical_and(q == g * self.gap, g < G))(lambda: run(g))

        due(0, lambda g: self.pair_copy(g).wait())

        @pl.when(step == self.start)
        def _():
            self.pass_copy().wait_recv()

        due(place, lambda g: self.chain(0, g))
        due(late - place, lambda g: self.chain(1, g))

    def steps(self):
        return self.start + self.gap * (G - 1) + self.n // 2

    def finish(self):
        self.pass_copy().wait_send()

        @pl.loop(0, G)
        def _(g):
            pl.when(self.has_after)(self.chain_copy(0, g).wait_send)
            pl.when(self.has_before)(self.chain_copy(1, g).wait_send)


PIECE = 256


class Reduce:
    STAGES = 8
    SPACE = 2
    SLOTS, LAG = 15, 2

    def __init__(self, far, near_count, half, near, out, scratch):
        self.far, self.near_count, self.half, self.near, self.out = far, near_count, half, near, out
        (self.own, self.r0, self.r1, self.r2, self.r3, self.send, self.recv, self.local) = scratch
        rows, seq = lax.axis_index("rows"), lax.axis_index("seq")
        self.y, self.core, self.z, self.x = rows // 2, rows % 2, seq // 2, seq % 2

    @staticmethod
    def scratch():
        def slot(*shape):
            return pltpu.VMEM(shape + (D,), F32)

        dma, count = pltpu.SemaphoreType.DMA, Reduce.SLOTS
        return [
            slot(3, 128), slot(count, 128), slot(count, 64), slot(count, 32), slot(count, 24),
            dma((12, count)), dma((12, count)), dma((2, count)),
        ]

    def device(self, x, y, z, core):
        return {"rows": y * 2 + core, "seq": z * 2 + x}

    def greet(self):
        barrier = pltpu.get_barrier_semaphore()
        x, y, z, core = self.x, self.y, self.z, self.core
        peers = [(x, y, z, 1 - core), (1 - x, y, z, core), (x, 1 - y, z, core)] + [
            (x, y, lax.rem(z + d, 4), core) for d in (1, 2, 3)]
        for peer in peers:
            pl.semaphore_signal(barrier, inc=1, device_id=self.device(*peer), device_id_type=MESH)

        @pl.when(self.has_next())
        def _():
            pl.semaphore_signal(
                barrier, inc=1, device_id=self.device(1 - x, y, z + 2 * x - 1, core),
                device_id_type=MESH)

    def has_next(self):
        return jnp.where(self.x == 0, self.z > 0, self.z < 3)

    def met(self):
        pl.semaphore_wait(pltpu.get_barrier_semaphore(), 6 + self.has_next().astype(jnp.int32))

    def turn(self, p):
        return lax.rem(p, 2) == 1

    def slot(self, p):
        return jnp.where(p < self.SLOTS, p, p - self.SLOTS)

    def places(self, p):
        x_first = self.turn(p)
        a, b = jnp.where(x_first, self.x, self.y), jnp.where(x_first, self.y, self.x)
        return a * 64, a * 64 + b * 32, a * 64 + b * 32 + self.z * 8

    def copies(self, s, p):
        x, y, z, core = self.x, self.y, self.z, self.core
        i = self.slot(p)
        one, two, three = self.places(p)
        flip_x, flip_y, flip_core = (1 - x, y, z, core), (x, 1 - y, z, core), (x, y, z, 1 - core)

        def mine(start, size):
            return self.r0.at[i, pl.ds(pl.multiple_of(start, 8), size)]

        def final(start, size):
            return self.out.at[pl.ds(pl.multiple_of(p * PIECE + core * 128 + start, 8), size)]

        def copy(src, dst, kind, to):
            return pltpu.make_async_remote_copy(
                src, dst, self.send.at[kind, i], self.recv.at[kind, i],
                device_id=self.device(*to), device_id_type=MESH)

        def over_z(src, dst, kind):
            peers = [(lax.rem(z + d, 4), d - 1) for d in (1, 2, 3)]
            return [copy(src(zz), dst(d), kind + d, (x, y, zz, core)) for zz, d in peers]

        x_first = self.turn(p)
        first = tuple(jnp.where(x_first, u, v) for u, v in zip(flip_x, flip_y))
        second = tuple(jnp.where(x_first, u, v) for u, v in zip(flip_y, flip_x))
        if s == 1:
            return [copy(mine(64 - one, 64), self.r1.at[i], 1, first)]
        if s == 2:
            return [copy(mine(one + 32 - (two - one), 32), self.r2.at[i], 2, second)]
        if s == 3:
            return over_z(
                lambda zz: mine(two + zz * 8, 8), lambda d: self.r3.at[i, pl.ds(8 * d, 8)], 3)
        if s == 4:
            return over_z(lambda zz: mine(three, 8), lambda d: final(three, 8), 6)
        if s == 5:
            return [copy(final(two, 32), final(two, 32), 9, second)]
        if s == 6:
            return [copy(final(one, 64), final(one, 64), 10, first)]
        return [copy(final(0, 128), final(0, 128), 11, flip_core)]

    def near_half(self, p, c):
        return self.near.at[p - self.far, pl.ds(pl.multiple_of(c * 128, 128), 128)]

    def core_copy(self, p, near):
        i = self.slot(p)
        half = (self.near_half if near else self.half)(p, 1 - self.core)
        return pltpu.make_async_remote_copy(
            half, self.r0.at[i], self.send.at[0, i], self.recv.at[0, i],
            device_id=self.device(self.x, self.y, self.z, 1 - self.core), device_id_type=MESH)

    def own_in(self, p):
        return pltpu.make_async_copy(
            self.half(p, self.core), self.own.at[lax.rem(p, 3)], self.local.at[0, self.slot(p)])

    def own_out(self, p):
        i, start = self.slot(p), pl.multiple_of(self.places(p)[2], 8)
        to = p * PIECE + self.core * 128 + start
        return pltpu.make_async_copy(
            self.r0.at[i, pl.ds(start, 8)], self.out.at[pl.ds(pl.multiple_of(to, 8), 8)],
            self.local.at[1, i])

    def begin(self, p):
        @pl.when(p < self.far)
        def _():
            self.own_in(p).start()
            self.core_copy(p, False).start()

        @pl.when(p >= self.far)
        def _():
            self.core_copy(p, True).start()

    def add_core(self, p):
        i = self.slot(p)

        @pl.when(p < self.far)
        def _():
            self.core_copy(p, False).wait()
            self.own_in(p).wait()
            self.r0[i] += self.own[lax.rem(p, 3)]

        @pl.when(p >= self.far)
        def _():
            self.core_copy(p, True).wait()
            self.r0[i] += self.near_half(p, self.core)[...]

    def stage(self, s, p):
        i = self.slot(p)
        starts = self.places(p)
        if s == 1:
            self.add_core(p)
        else:
            for copy in self.copies(s - 1, p):
                copy.wait_recv()

        def kept(which, size):
            return pl.ds(pl.multiple_of(starts[which], 8), size)

        if s == 2:
            self.r0[i, kept(0, 64)] += self.r1[i]
        elif s == 3:
            self.r0[i, kept(1, 32)] += self.r2[i]
        elif s == 4:
            self.r0[i, kept(2, 8)] += self.r3[i, 0:8] + self.r3[i, 8:16] + self.r3[i, 16:24]
            self.own_out(p).start()
        elif s == 5:
            self.own_out(p).wait()
            for done in (1, 2, 3, 4):
                for copy in self.copies(done, p):
                    copy.wait_send()
        if s < self.STAGES:
            for copy in self.copies(s, p):
                copy.start()
        else:
            for done in (5, 6, 7):
                for copy in self.copies(done, p):
                    copy.wait_send()

    def ticks(self):
        return self.far + self.near_count + self.LAG + self.SPACE * self.STAGES

    def tick(self, t):
        for s in range(self.STAGES + 1):
            q = t - self.SPACE * s
            p = jnp.where(q < self.SLOTS, q, q - self.LAG)
            due = jnp.logical_and(q >= 0, p < self.far + self.near_count)
            due = jnp.logical_and(due, jnp.logical_or(q < self.SLOTS, p >= self.SLOTS))

            @pl.when(due)
            def _(s=s, p=p):
                if s == 0:
                    self.begin(p)
                else:
                    self.stage(s, p)


def pieces(x):
    return [x[:, i * STATE : (i + 1) * STATE] for i in range(4)]


START, GAP = 4, 1


def front_kernel(
    n, rows, length, docs,
    tok, ngain, w, weight, cw, cb_i, dtb_i, rate_i, skip_i, starts,
    rounded_o, c_o, p_o, xact_o, y_o, rows_o, q_o, q2_o, pexp_o, sin_o, wide_o, tall_o,
    rext, vhi, vlo, gc, sloc, wst, hsend, hrecv, loads, hs, hr, *scratch,
):
    k = pl.program_id(0)
    chunks = length // C
    blocks = rows * chunks
    ex = Exchange(n, rows, chunks, sloc, sin_o, (0, 1), scratch, START, GAP)
    ex.set_passes(pexp_o)

    def convolved(r, g):
        p = mm(rext[r], w[...], NT)
        p_o[r] = p
        first = PAD - (KW - 1)
        out = wide_o[0:1, cols(g)]
        for i in range(KW):
            out = out + cw[i : i + 1, :] * p[first + i : first + i + length]
        c_o[r * length : (r + 1) * length, :] = out
        return out * sigmoid(out)

    def normed(source):
        scale = lax.rsqrt(jnp.mean(source * source, axis=-1, keepdims=True) + EPS)
        return (source * scale * ngain[...][None, :]).astype(BF16)

    def label_at(r, position):
        found = jnp.int32(0)
        for d in range(docs):
            found += (starts[r, d] <= position).astype(jnp.int32)
        return found.astype(F32)

    def load_steps():
        return pltpu.make_async_copy(
            weight.at[pl.ds(2 * INNER + 4 * STATE, 2 * HEADS)], wst, loads.at[0])

    def halo_copy():
        return pltpu.make_async_remote_copy(
            hsend, hrecv, hs.at[0], hr.at[0],
            device_id={"seq": ex.me + 1}, device_id_type=MESH)

    def tall(ref, count):
        line = jnp.concatenate([ref[...], jnp.zeros((128 - count,), F32)])[None, :]
        return jnp.broadcast_to(line, (8, 128))

    @pl.when(k == 0)
    def _():
        load_steps().start()

        @pl.when(ex.me == 0)
        def _():
            hrecv[...] = jnp.zeros_like(hrecv)

        ex.clear()
        ex.greet(True)
        for r in range(rows):
            hsend[r] = tok[(r + 1) * length - 16 : (r + 1) * length, :].astype(F32)[8:]
        for r in range(rows):
            here = slice(r * length, (r + 1) * length)
            out = normed(tok[here, :].astype(F32))
            rext[r, PAD:, :] = out
            rounded_o[here, :] = out
        ex.met(True)
        pl.when(ex.me < n - 1)(halo_copy().start)
        dtb, rate = tall(dtb_i, 2 * HEADS).T[:48, 0:1], tall(rate_i, 2 * HEADS).T[:48, 0:1]
        lane = iota((48, 128), 1)
        tall_o[...] = jnp.where(lane == 0, dtb, jnp.where(lane == 1, rate, 0.0))
        pick_f, pick_r = pick_all(0), pick_all(2)
        wide_o[0:8, 0:CONV] = jnp.broadcast_to(cb_i[...][None, :], (8, CONV))
        lines = [tall(skip_i, HEADS)]
        upto = (iota((C, C), 0) <= iota((C, C), 1)).astype(BF16)
        load_steps().wait()
        for b in range(blocks):
            here = slice(b * C, (b + 1) * C)
            r, begin = b // chunks, ex.me * length + (b % chunks) * C
            own = jnp.zeros((1, C), F32)
            for d in range(docs):
                own += (starts[r, d] <= begin + iota((1, C), 1)).astype(F32)
            before, first = label_at(r, begin - 1), label_at(r, begin)
            last, after = label_at(r, begin + C - 1), label_at(r, begin + C)
            m0, m1, m2, m3 = [(own == edge).astype(F32) for edge in (before, last, after, first)]
            raw = mm(wst[...], rounded_o[here, :], NT)
            step = softplus(raw + dtb)
            log = -LOG2E * rate * step
            total = mm3(log, upto)
            size = jnp.log(step) * LOG2E
            lf, rc = total[:HEADS], total[HEADS:] - log[HEADS:]
            end_f, end_r = total[:HEADS, C - 1 : C], total[HEADS:, C - 1 : C]
            sf, sr = lf - size[:HEADS], rc + size[HEADS:]
            e_f = jnp.exp2(lf) * m0
            w_f = jnp.exp2(end_f - lf) * step[:HEADS] * m1
            e_r = jnp.exp2(end_r - rc) * m2
            w_r = jnp.exp2(rc) * step[HEADS:] * m3
            labels = jnp.broadcast_to(own, (8, C))
            none = jnp.zeros((24, C), F32)
            rows_o[b] = jnp.concatenate([step, lf, rc, sf, sr, raw, labels], axis=0)
            q = jnp.concatenate([e_f, w_f, e_r, w_r, labels, none], axis=0).T
            q_o[b] = q
            q2_o[b] = jnp.concatenate([lf, rc, sf, sr, labels, none], axis=0).T
            lines += [q[C - 8 :], q[:8]]
        if len(lines) % 2:
            lines.append(lines[0])
        wide_f, wide_r = [mm3(jnp.concatenate(lines, axis=0), pick) for pick in (pick_f, pick_r)]
        wide_o[8:16, 0:INNER] = wide_f[0:8]
        for b in range(blocks):
            pexp_o[b : b + 1, :] = wide_f[16 * b + 15 : 16 * b + 16]
            pexp_o[8 + b : 9 + b, :] = wide_r[16 * b + 16 : 16 * b + 17]
        ex.totals_of_passes()
        pl.when(ex.me > 0)(halo_copy().wait_recv)
        for r in range(rows):
            rext[r, 0:PAD, :] = normed(jnp.concatenate([jnp.zeros((8, D), F32), hrecv[r]], axis=0))
            xact_o[r * length : (r + 1) * length, :] = convolved(r, G)

    @pl.when(jnp.logical_and(k >= 1, k <= G))
    def _():
        g = k - 1
        picks = [pick(1, g), pick(3, g)]
        for r in range(rows):
            v = convolved(r, g)
            hi, lo = split2(v)
            vhi[g, r * length : (r + 1) * length, :] = hi
            vlo[g, r * length : (r + 1) * length, :] = lo
            for c in range(chunks):
                b = r * chunks + c
                vb = v[c * C : (c + 1) * C]
                x = xact_o[b * C : (b + 1) * C, :].astype(BF16)
                for d in range(2):
                    scale = mm2(q_o[b], picks[d])
                    sloc[b, d, :, cols(g)] = mm(
                        x[:, d * STATE : (d + 1) * STATE], (scale * vb).astype(BF16), TN)
        ex.totals(g)
        pl.when(g == 0)(ex.pass_copy().start)
        ex.pair_copy(g).start()

    pl.when(k > 0)(lambda: ex.advance(k - 1))

    @pl.when(k == G + 1)
    def _():
        t_id, s_id = iota((C, C), 0), iota((C, C), 1)
        for b in range(blocks):
            in_f, in_r, rd_f, rd_r = pieces(xact_o[b * C : (b + 1) * C, :])
            gf, gr = mm22(rd_f, in_f, NT), mm22(rd_r, in_r, NT)
            same = jnp.logical_and(q2_o[b][:, 96:97] == rows_o[b, 192:193], t_id != s_id)
            gc[b] = jnp.where(same, jnp.where(t_id > s_id, gf, gr), 0.0)

    @pl.when(jnp.logical_and(k > G, k <= 2 * G))
    def _():
        g = k - 1 - G
        later = iota((C, C), 0) > iota((C, C), 1)
        low = iota((C, 128), 1) < HEAD
        skip = wide_o[8:9, cols(g)]
        for b in range(blocks):
            here = slice(b * C, (b + 1) * C)
            q2 = pltpu.roll(q2_o[b], 128 - HG * g, 1)
            for pair in range(HG // 2):
                at = slice(pair * 128, (pair + 1) * 128)
                v2 = jnp.concatenate([vhi[g, here, at], vlo[g, here, at]], axis=1)
                outs = []
                for h in (2 * pair, 2 * pair + 1):
                    lt, rt = q2[:, h : h + 1], q2[:, HEADS + h : HEADS + h + 1]
                    ls = rows_o[b, pl.ds(96 + HG * g + h, 1), :]
                    rs = rows_o[b, pl.ds(96 + HEADS + HG * g + h, 1), :]
                    x = jnp.exp2(jnp.where(later, lt - ls, rs - rt))
                    o = mm((gc[b] * x).astype(BF16), v2)
                    outs.append(o[:, :128] + o[:, 128:])
                v = vhi[g, here, at].astype(F32) + vlo[g, here, at].astype(F32)
                y_o[here, at] = jnp.where(low, outs[0], outs[1]) + skip[:, at] * v

    @pl.when(k == pl.num_programs(0) - 1)
    def _():
        ex.finish()
        pl.when(ex.me < n - 1)(halo_copy().wait_send)


def middle_kernel(
    y, rounded, tok, cot, q, xact, sin, wg, wo, ogain,
    mixed_o, dy_o, drounded_o, ds_o, dread_o, dq_o, ogain_grad, w_grad,
    outs, dgates,
):
    k = pl.program_id(0)
    here = pl.ds(pl.multiple_of(k * C, C), C)
    rounded_b, cot_b = rounded[here, :], cot[here, :]
    x = xact[...].astype(BF16)
    rd_f, rd_r = x[:, 2 * STATE : 3 * STATE], x[:, 3 * STATE :]
    s_f, s_r = sin[0, 0].astype(BF16), sin[0, 1].astype(BF16)
    pick_f, pick_r = pick_all(0), pick_all(2)
    factors = q[0].astype(BF16)
    e_f, e_r = mm(factors, pick_f), mm(factors, pick_r)
    r_f, r_r = mm(rd_f, s_f), mm(rd_r, s_r)
    yv = y[...] + e_f * r_f + e_r * r_r
    gate = mm(rounded_b, wg[...], NT)
    sg = sigmoid(gate)
    silu = gate * sg
    gated = yv * silu
    scale = lax.rsqrt(jnp.mean(gated * gated, axis=-1, keepdims=True) + EPS)
    normed = gated * scale
    out = (normed * ogain[...][None, :]).astype(BF16)
    outs[here, :] = out
    mixed_o[...] = (tok[...].astype(F32) + mm(out, wo[...])).astype(BF16)
    dout = mm(cot_b, wo[...], NT)
    go = jnp.sum(dout * normed, axis=0, keepdims=True)
    dn = dout * ogain[...][None, :]
    dgated = scale * (dn - normed * jnp.mean(dn * normed, axis=-1, keepdims=True))
    dy = dgated * silu
    dy_o[...] = dy
    dgate = (dgated * yv * sg * (1.0 + gate * (1.0 - sg))).astype(BF16)
    dgates[here, :] = dgate
    drounded_o[...] = mm(dgate, wg[...])
    u_f, u_r = e_f * dy, e_r * dy
    dq_o[0] = mm((u_f * r_f).astype(BF16), pick_f, NT) + mm((u_r * r_r).astype(BF16), pick_r, NT)
    u_f, u_r = u_f.astype(BF16), u_r.astype(BF16)
    ds_o[0, 1] = mm(rd_f, u_f, TN)
    ds_o[0, 0] = mm(rd_r, u_r, TN)
    dread_o[...] = jnp.concatenate([mm(u_f, s_f, NT), mm(u_r, s_r, NT)], axis=1)

    @pl.when(k == 0)
    def _():
        ogain_grad[...] = jnp.broadcast_to(go, ogain_grad.shape)

    @pl.when(k > 0)
    def _():
        ogain_grad[...] += go

    @pl.when(k == pl.num_programs(0) - 1)
    def _():
        for i in range(G):
            at = slice(i * GC, (i + 1) * GC)
            w_grad[at] = mm(dgates[:, at], rounded[...], TN)
            w_grad[INNER + i * GC : INNER + (i + 1) * GC] = mm(outs[:, at], cot[...], TN)


def steps_backward(dq, col, row, pg_f, pg_r, raw, step, rate):
    from_t = (iota((C, C), 0) >= iota((C, C), 1)).astype(BF16)
    after_t = (iota((C, C), 0) > iota((C, C), 1)).astype(BF16)
    e_f, w_f, e_r, w_r = [dq[i * HEADS : (i + 1) * HEADS] for i in range(4)]
    cs_f, cs_r = col[:HEADS], col[HEADS : 2 * HEADS]
    d_lf = row[:HEADS] - cs_f + e_f - w_f
    d_rc = cs_r - row[HEADS:] - e_r + w_r
    d_size = jnp.concatenate([cs_f + w_f, cs_r + w_r], axis=0)
    end_f = jnp.sum(w_f, axis=1, keepdims=True) + pg_f
    end_r = jnp.sum(e_r, axis=1, keepdims=True) + pg_r
    d_log = jnp.concatenate([mm3(d_lf, from_t) + end_f, mm3(d_rc, after_t) + end_r], axis=0)
    sg = sigmoid(raw)
    ratio = jnp.where(raw < -15.0, 1.0, sg / jnp.maximum(step, 1e-30))
    d_raw = -rate * d_log * sg + d_size * ratio
    bias = jnp.sum(d_raw, axis=1, keepdims=True)
    rates = -jnp.sum(step * d_log, axis=1, keepdims=True)
    at = iota((2 * HEADS, 128), 1)
    return d_raw, jnp.where(at == 0, bias, jnp.where(at == 1, rates, 0.0))


def back_kernel(
    n, rows, length, far, shared,
    c_i, dy_i, p_i, cw, w, sin,
    xact, rows_i, q_i, q2_i, pexp, dread, dq_i, wide, tall,
    rounded, tok, cot, ngain, ogain_grad,
    ds_i, drounded, w_grad, weight,
    tg_o, total_o, *scratch,
):
    (gct, dgt, dvs, dss, dts, dqs, dins, pgs, z, acc, draw, wst, near, hsend, hrecv, loads, hs, hr) = (
        scratch[:18])
    k = pl.program_id(0)
    chunks = length // C
    blocks = rows * chunks
    near_count = G + 2
    st = near if shared else total_o
    ex = Exchange(n, rows, chunks, z, z, (1, 0), scratch[18:29])
    ex.set_passes(pexp)
    later = iota((C, C), 1) > iota((C, C), 0)
    if shared:

        def half(p, c):
            return w_grad.at[pl.ds(pl.multiple_of(p * PIECE + c * 128, 128), 128)]

        red = Reduce(2 * INNER // PIECE, near_count, half, near, total_o, scratch[29:])

    def load_states():
        return pltpu.make_async_copy(ds_i, z, loads.at[0])

    def load_sum():
        return pltpu.make_async_copy(drounded, acc, loads.at[1])

    def load_steps():
        return pltpu.make_async_copy(
            weight.at[pl.ds(2 * INNER + 4 * STATE, 2 * HEADS)], wst, loads.at[2])

    def halo_copy(g):
        return pltpu.make_async_remote_copy(
            hsend.at[g], hrecv.at[g], hs.at[g], hr.at[g],
            device_id={"seq": ex.me - 1}, device_id_type=MESH)

    @pl.when(k == 0)
    def _():
        load_states().start()
        load_sum().start()
        load_steps().start()

        @pl.when(ex.me == n - 1)
        def _():
            hrecv[...] = jnp.zeros_like(hrecv)

        ex.clear()
        if shared:
            red.greet()
        else:
            ex.greet(True)
        ex.totals_of_passes()
        load_states().wait()

        if shared:
            red.met()
        else:
            ex.met(True)
        ex.pass_copy().start()

        @pl.loop(0, G)
        def _(g):
            ex.totals(g)
            ex.pair_copy(g).start()

        differ = iota((C, C), 0) != iota((C, C), 1)
        for b in range(blocks):
            in_f, in_r, rd_f, rd_r = pieces(xact[b * C : (b + 1) * C, :])
            gf, gr = mm22(in_f, rd_f, NT), mm22(in_r, rd_r, NT)
            same = jnp.logical_and(q2_i[b][:, 96:97] == rows_i[b, 192:193], differ)
            gct[b] = jnp.where(same, jnp.where(later, gf, gr), 0.0)
        dgt[...] = jnp.zeros_like(dgt)
        dss[...] = jnp.zeros_like(dss)
        dins[...] = jnp.zeros_like(dins)
        pgs[...] = jnp.zeros_like(pgs)
        dqs[...] = dq_i[...]
        st[G + 1] = jnp.zeros((PIECE, D), F32)
        load_sum().wait()
        load_steps().wait()

    @pl.when(k < G)
    def _():
        g = k
        low = iota((C, 128), 1) < HEAD
        lane = iota((C, 128), 1)
        ones = jnp.ones((8, C), BF16)
        skips = jnp.zeros((1, GC), F32)
        skip = wide[8:9, cols(g)]
        for b in range(blocks):
            here = slice(b * C, (b + 1) * C)
            q2 = pltpu.roll(q2_i[b], 128 - HG * g, 1)
            cv = c_i[here, :]
            v = cv * sigmoid(cv)
            dy = dy_i[here, :]
            skips += jnp.sum(dy * v, axis=0, keepdims=True)
            dyhi, dylo = split2(dy)
            vb = v.astype(BF16)
            for pair in range(HG // 2):
                at = slice(pair * 128, (pair + 1) * 128)
                dy2 = jnp.concatenate([dyhi[:, at], dylo[:, at]], axis=1)
                outs = []
                for i in range(2):
                    h = 2 * pair + i
                    mine = low if i == 0 else jnp.logical_not(low)
                    dyh = jnp.where(mine, dyhi[:, at], jnp.zeros((), BF16))
                    dw = mm(vb[:, at], dyh, NT)
                    lt = rows_i[b, pl.ds(48 + HG * g + h, 1), :]
                    rt = rows_i[b, pl.ds(48 + HEADS + HG * g + h, 1), :]
                    ls, rs = q2[:, 48 + h : 49 + h], q2[:, 72 + h : 73 + h]
                    x = jnp.exp2(jnp.where(later, lt - ls, rs - rt))
                    dwx = dw * x
                    dgt[b] += dwx
                    gb = gct[b]
                    o = mm((gb * x).astype(BF16), dy2)
                    outs.append(o[:, :128] + o[:, 128:])
                    de = dwx * gb
                    de_f = jnp.where(later, de, 0.0).astype(BF16)
                    de_r = jnp.where(later, 0.0, de).astype(BF16)
                    hot_f = (lane == HG * g + h).astype(BF16)
                    hot_r = (lane == HEADS + HG * g + h).astype(BF16)
                    dss[b] += mm(de_f, hot_f) + mm(de_r, hot_r)
                    dts[b, pl.ds(HG * g + h, 1), :] = mm(ones, de_f)[0:1]
                    dts[b, pl.ds(HEADS + HG * g + h, 1), :] = mm(ones, de_r)[0:1]
                dvs[g, here, at] = jnp.where(low, outs[0], outs[1]) + skip[:, at] * dy[:, at]
        line = pl.multiple_of(120 + 8 * (g // 3), 8)
        st[G + 1, pl.ds(line, 8), cols(lax.rem(g, 3))] = jnp.broadcast_to(skips, (8, GC))

    ex.advance(k)

    def send_halo(g):
        for r in range(rows):
            hsend[g, r] = dvs[g, r * length : r * length + 8, :]
        pl.when(ex.me > 0)(halo_copy(g).start)

    @pl.when(jnp.logical_and(k >= far, k < far + G))
    def _():
        g = k - far
        picks = [pick(1, g), pick(3, g)]
        for b in range(blocks):
            here = slice(b * C, (b + 1) * C)
            cv = c_i[here, :]
            sg = sigmoid(cv)
            v = cv * sg
            x = xact[here, :].astype(BF16)
            dv = dvs[g, here, :]
            for d in range(2):
                zf = z[b, 1 - d, :, cols(g)]
                zb = zf.astype(BF16)
                weight = mm2(q_i[b], picks[d])
                m = mm(x[:, d * STATE : (d + 1) * STATE], zb)
                dv += weight * m
                u = weight * v
                dqs[b] += mm2(u * m, picks[d], NT)
                at = slice(d * STATE, (d + 1) * STATE)
                dins[b, :, at] += mm(u.astype(BF16), zb, NT)
                pgs[8 * d + b : 8 * d + b + 1, cols(g)] = pexp[
                    8 * d + b : 8 * d + b + 1, cols(g)
                ] * jnp.sum(zf * sin[b, d], axis=0, keepdims=True)
            dvs[g, here, :] = dv * (sg * (1.0 + cv * (1.0 - sg)))
        send_halo(g)

    @pl.when(k == far + G)
    def _():
        differ = iota((C, C), 0) != iota((C, C), 1)
        for b in range(blocks):
            here = slice(b * C, (b + 1) * C)
            same = jnp.logical_and(q2_i[b][:, 96:97] == rows_i[b, 192:193], differ)
            dg = jnp.where(same, dgt[b], 0.0)
            dg_f = jnp.where(later, dg, 0.0).astype(BF16)
            dg_r = jnp.where(later, 0.0, dg).astype(BF16)
            in_f, in_r, rd_f, rd_r = pieces(xact[here, :].astype(BF16))
            dx = jnp.concatenate(
                [
                    dins[b, :, :STATE] + mm(dg_f, rd_f),
                    dins[b, :, STATE:] + mm(dg_r, rd_r),
                    dread[here, :STATE] + mm(dg_f, in_f, TN),
                    dread[here, STATE:] + mm(dg_r, in_r, TN),
                ],
                axis=1,
            )
            cv = c_i[here, :]
            sg = sigmoid(cv)
            dvs[G, here, :] = dx * (sg * (1.0 + cv * (1.0 - sg)))
        send_halo(G)
        pg_f = mm2(pgs[...], pick_all(0), NT)[0:8].T
        pg_r = mm2(pgs[...], pick_all(2), NT)[8:16].T
        sums = jnp.zeros((2 * HEADS, 128), F32)
        for b in range(blocks):
            d_raw, small = steps_backward(
                dqs[b].T, dss[b].T, dts[b], pg_f[:HEADS, b : b + 1],
                pg_r[2 * HEADS : 3 * HEADS, b : b + 1], rows_i[b, 144:192] + tall[:, 0:1],
                rows_i[b, 0:48], tall[:, 1:2])
            draw[:, b * C : (b + 1) * C] = d_raw.astype(BF16)
            sums += small
        st[G + 1, 0:48] = mm(draw[...], rounded[...])
        st[G + 1, 48:96, 0:128] = sums

    @pl.when(k > far)
    def _():
        g = k - far - 1
        pl.when(ex.me < n - 1)(halo_copy(g).wait_recv)
        parts = []
        taps = [jnp.zeros((1, GC), F32) for _ in range(KW)]
        bias = jnp.zeros((1, GC), F32)
        for r in range(rows):
            own = dvs[g, r * length : (r + 1) * length, :]
            ext = jnp.concatenate([own, hrecv[g, r]], axis=0)
            total = None
            for i in range(KW):
                one = cw[i : i + 1, :] * ext[KW - 1 - i : KW - 1 - i + length]
                total = one if total is None else total + one
                first = PAD - (KW - 1) + i
                taps[i] += jnp.sum(own * p_i[r, first : first + length, :], axis=0, keepdims=True)
            bias += jnp.sum(own, axis=0, keepdims=True)
            parts.append(total.astype(BF16))
        both = jnp.concatenate(parts, axis=0)
        st[g] = mm(both, rounded[...], TN)
        line = pl.multiple_of(136 + 8 * (g // 3), 8)
        st[G + 1, pl.ds(line, 8), cols(lax.rem(g, 3))] = jnp.concatenate(
            taps + [bias, jnp.zeros((3, GC), F32)], axis=0)
        acc[...] += mm(both, w[...])

    def until(k):
        return jnp.clip(2 * (k - 2), 0, k + far + 1)

    if shared:

        @pl.loop(jnp.where(k == 0, 0, until(k - 1)), until(k))
        def _(t):
            red.tick(t)

    @pl.when(k == far + G + 1)
    def _():
        acc[...] += mm(draw[...], wst[...], TN)
        gains = jnp.zeros((1, D), F32)
        for b in range(blocks):
            here = slice(b * C, (b + 1) * C)
            source = tok[here, :].astype(F32)
            scale = lax.rsqrt(jnp.mean(source * source, axis=-1, keepdims=True) + EPS)
            m = source * scale
            d_rounded = acc[here, :]
            gains += jnp.sum(d_rounded * m, axis=0, keepdims=True)
            nn = d_rounded * ngain[...][None, :]
            d_source = scale * (nn - m * jnp.mean(nn * m, axis=-1, keepdims=True))
            tg_o[here, :] = (cot[here, :].astype(F32) + d_source).astype(BF16)
        st[G + 1, 96:104] = jnp.broadcast_to(gains, (8, D))
        for i in range(2):
            st[G + 1, 104 + 8 * i : 112 + 8 * i] = ogain_grad[:, i * D : (i + 1) * D]
        if shared:

            @pl.loop(until(k), red.ticks())
            def _(t):
                red.tick(t)

        ex.finish()

        @pl.loop(0, G + 1)
        def _(g):
            pl.when(ex.me > 0)(halo_copy(g).wait_send)


def finish_kernel(
    total, in_o, out_o, ng_o, cw_o, cb_o, dtb_o, rate_o, skip_o, og_o, held, arrive, leave,
):
    count = total.shape[0] // PIECE
    gates = INNER // PIECE

    def read(i):
        return pltpu.make_async_copy(
            total.at[pl.ds(i * PIECE, PIECE)], held.at[i], arrive.at[i])

    def write(i):
        size = PIECE
        if i < gates:
            to = in_o.at[pl.ds(i * PIECE, PIECE)]
        elif i < 2 * gates:
            to = out_o.at[pl.ds((i - gates) * PIECE, PIECE)]
        else:
            size = PIECE if i < count - 1 else 2 * HEADS
            to = in_o.at[pl.ds((i - gates) * PIECE, size)]
        return pltpu.make_async_copy(held.at[i, pl.ds(0, size)], to, leave.at[i])

    for i in range(count):
        read(i).start()
    for i in range(count):
        read(i).wait()
        write(i).start()
    rest = held.at[count - 1]
    ng_o[...] = rest[96:97, :][0]
    og_o[...] = jnp.concatenate([rest[104:105, :], rest[112:113, :]], axis=1)[0]
    lines = jnp.concatenate([rest[120:128, :], rest[128:136, :]], axis=1)
    skip_o[...] = mm3(jnp.concatenate([lines, lines], axis=0), pick_all(0), NT)[0, 0:HEADS]
    both = jnp.concatenate([rest[48:96, 0:128], jnp.zeros((80, 128), F32)], axis=0).T
    dtb_o[...] = both[0, 0 : 2 * HEADS]
    rate_o[...] = both[1, 0 : 2 * HEADS]
    taps = jnp.concatenate([rest[136:144, :], rest[144:152, :], rest[152:160, :GC]], axis=1)
    cw_o[...] = taps[:KW]
    cb_o[...] = taps[KW]
    for i in range(count):
        write(i).wait()


def whole(shape):
    zeros = (0,) * len(shape)
    return pl.BlockSpec(shape, lambda k: zeros, pipeline_mode=pl.Buffered(1))


def struct(shape, dtype=F32):
    return jax.ShapeDtypeStruct(shape, dtype)


def on_device(
    tokens, doc_starts, norm_gain, in_weight, conv_weight, conv_bias, dt_bias, decay_rate,
    skip_scale, out_gain, out_weight, cotangent,
):
    n = lax.axis_size("seq")
    rows, length, _ = tokens.shape
    docs = doc_starts.shape[1]
    chunks = length // C
    blocks = rows * chunks
    count = rows * length
    weight = in_weight.T
    tok, cot = tokens.reshape(count, D), cotangent.reshape(count, D)
    anywhere = pl.BlockSpec(memory_space=pl.ANY)

    params = dict(vmem_limit_bytes=VMEM_LIMIT)
    dims = ("arbitrary",)

    def col(k):
        return jnp.where(k == 0, G, jnp.minimum(k - 1, G - 1))

    def ycol(k):
        return jnp.clip(k - 1 - G, 0, G - 1)

    front_steps = max(2 * G, START + GAP * (G - 1) + n // 2) + 1
    rounded, c, p, xact, y, rowsv, q, q2, pexp, sin, wide, tall = pl.pallas_call(
        lambda *refs: front_kernel(n, rows, length, docs, *refs),
        grid=(front_steps,),
        in_specs=[
            whole((count, D)), whole((D,)),
            pl.BlockSpec((GC, D), lambda k: (G + col(k), 0)), anywhere,
            pl.BlockSpec((KW, GC), lambda k: (0, col(k))),
            whole((CONV,)), whole((2 * HEADS,)), whole((2 * HEADS,)), whole((HEADS,)),
            pl.BlockSpec(memory_space=pltpu.SMEM),
        ],
        out_specs=[
            whole((count, D)),
            pl.BlockSpec((count, GC), lambda k: (0, col(k))),
            pl.BlockSpec((rows, PAD + length, GC), lambda k: (0, 0, col(k))),
            whole((count, GC)),
            pl.BlockSpec((count, GC), lambda k: (0, ycol(k))),
            whole((blocks, 200, C)), whole((blocks, C, 128)), whole((blocks, C, 128)),
            whole((16, INNER)), whole((blocks, 2, STATE, INNER)), whole((16, CONV)),
            whole((2 * HEADS, 128)),
        ],
        out_shape=[
            struct((count, D), BF16), struct((count, CONV)), struct((rows, PAD + length, CONV)),
            struct((count, GC)), struct((count, INNER)), struct((blocks, 200, C)),
            struct((blocks, C, 128)), struct((blocks, C, 128)), struct((16, INNER)),
            struct((blocks, 2, STATE, INNER)), struct((16, CONV)), struct((2 * HEADS, 128)),
        ],
        scratch_shapes=[
            pltpu.VMEM((rows, PAD + length, D), BF16),
            pltpu.VMEM((G, count, GC), BF16), pltpu.VMEM((G, count, GC), BF16),
            pltpu.VMEM((blocks, C, C), F32), pltpu.VMEM((blocks, 2, STATE, INNER), F32),
            pltpu.VMEM((2 * HEADS, D), BF16),
            pltpu.VMEM((rows, 8, D), F32), pltpu.VMEM((rows, 8, D), F32),
            pltpu.SemaphoreType.DMA((1,)), pltpu.SemaphoreType.DMA((1,)),
            pltpu.SemaphoreType.DMA((1,)),
            *Exchange.scratch(rows),
        ],
        compiler_params=pltpu.CompilerParams(
            dimension_semantics=dims, collective_id=0, has_side_effects=True, **params),
        name="front",
    )(tok, norm_gain, weight, weight, conv_weight, conv_bias, dt_bias, decay_rate, skip_scale,
      doc_starts)

    def by_block(shape):
        zeros = (0,) * (len(shape) - 1)
        return pl.BlockSpec(shape, lambda k: (k,) + zeros)

    mixed, dy, drounded, ds, dread, dq, ogain_grad, w_grad = pl.pallas_call(
        middle_kernel,
        grid=(blocks,),
        in_specs=[
            by_block((C, INNER)), whole((count, D)), by_block((C, D)), whole((count, D)),
            by_block((1, C, 128)), by_block((C, GC)), by_block((1, 2, STATE, INNER)),
            whole((INNER, D)), whole((INNER, D)), whole((INNER,)),
        ],
        out_specs=[
            by_block((C, D)), by_block((C, INNER)), by_block((C, D)),
            by_block((1, 2, STATE, INNER)), by_block((C, 128)), by_block((1, C, 128)),
            whole((8, INNER)), whole((2 * INNER, D)),
        ],
        out_shape=[
            struct((count, D), BF16), struct((count, INNER)), struct((count, D)),
            struct((blocks, 2, STATE, INNER)), struct((count, 128)), struct((blocks, C, 128)),
            struct((8, INNER)), struct((2 * INNER, D)),
        ],
        scratch_shapes=[pltpu.VMEM((count, INNER), BF16), pltpu.VMEM((count, INNER), BF16)],
        compiler_params=pltpu.CompilerParams(dimension_semantics=dims, **params),
        name="middle",
    )(y, rounded, tok, cot, q, xact, sin, weight, out_weight, out_gain)

    far = max(G, n // 2 + 1)
    shared = n == 8 and lax.axis_size("rows") == 4

    def vcol(k):
        return jnp.where(k < far, jnp.minimum(k, G - 1), jnp.minimum(k - far, G))

    def first_pass(k):
        return jnp.minimum(k, G - 1)

    def second_pass(k):
        return jnp.clip(k - far, 0, G - 1)

    def conv_pass(k):
        return jnp.clip(k - far - 1, 0, G)

    far_pieces = 2 * INNER // PIECE
    total_rows = (far_pieces + G + 2) * PIECE
    tg, total = pl.pallas_call(
        lambda *refs: back_kernel(n, rows, length, far, shared, *refs),
        grid=(far + G + 2,),
        in_specs=[
            pl.BlockSpec((count, GC), lambda k: (0, vcol(k))),
            pl.BlockSpec((count, GC), lambda k: (0, first_pass(k))),
            pl.BlockSpec((rows, PAD + length, GC), lambda k: (0, 0, conv_pass(k))),
            pl.BlockSpec((KW, GC), lambda k: (0, conv_pass(k))),
            pl.BlockSpec((GC, D), lambda k: (G + conv_pass(k), 0)),
            pl.BlockSpec((blocks, 2, STATE, GC), lambda k: (0, 0, 0, second_pass(k))),
            whole((count, GC)), whole((blocks, 200, C)), whole((blocks, C, 128)),
            whole((blocks, C, 128)), whole((16, INNER)), whole((count, 128)),
            whole((blocks, C, 128)), whole((16, CONV)), whole((2 * HEADS, 128)),
            whole((count, D)), whole((count, D)), whole((count, D)), whole((D,)),
            whole((8, INNER)), anywhere, anywhere, anywhere, anywhere,
        ],
        out_specs=[whole((count, D)), anywhere if shared else whole((G + 2, PIECE, D))],
        out_shape=[
            struct((count, D), BF16),
            struct((total_rows, D) if shared else (G + 2, PIECE, D)),
        ],
        scratch_shapes=[
            pltpu.VMEM((blocks, C, C), F32), pltpu.VMEM((blocks, C, C), F32),
            pltpu.VMEM((G + 1, count, GC), F32), pltpu.VMEM((blocks, C, 128), F32),
            pltpu.VMEM((blocks, 2 * HEADS, C), F32), pltpu.VMEM((blocks, C, 128), F32),
            pltpu.VMEM((blocks, C, 128), F32), pltpu.VMEM((16, INNER), F32),
            pltpu.VMEM((blocks, 2, STATE, INNER), F32), pltpu.VMEM((count, D), F32),
            pltpu.VMEM((2 * HEADS, count), BF16), pltpu.VMEM((2 * HEADS, D), BF16),
            pltpu.VMEM((G + 2, PIECE, D) if shared else (8, 128), F32),
            pltpu.VMEM((G + 1, rows, 8, GC), F32), pltpu.VMEM((G + 1, rows, 8, GC), F32),
            pltpu.SemaphoreType.DMA((3,)), pltpu.SemaphoreType.DMA((G + 1,)),
            pltpu.SemaphoreType.DMA((G + 1,)),
            *Exchange.scratch(rows), *(Reduce.scratch() if shared else []),
        ],
        compiler_params=pltpu.CompilerParams(
            dimension_semantics=dims, collective_id=1, has_side_effects=True,
            vmem_limit_bytes=63 * 1024 * 1024),
        name="back",
    )(c, dy, p, conv_weight, weight, sin, xact, rowsv, q, q2, pexp, dread, dq, wide, tall,
      rounded, tok, cot, norm_gain, ogain_grad, ds, drounded, w_grad, weight)

    if not shared:
        total = lax.psum(jnp.concatenate([w_grad, total.reshape(-1, D)], axis=0), ("rows", "seq"))
    held = total_rows // PIECE
    inside = pl.BlockSpec(memory_space=pltpu.VMEM)
    in_grad, out_grad, ng, cw, cb, dtb, rate, skip, og = pl.pallas_call(
        finish_kernel,
        in_specs=[anywhere],
        out_specs=[anywhere, anywhere] + [inside] * 7,
        out_shape=[
            struct((2 * INNER + 4 * STATE + 2 * HEADS, D)), struct((INNER, D)), struct((D,)),
            struct((KW, CONV)), struct((CONV,)), struct((2 * HEADS,)), struct((2 * HEADS,)),
            struct((HEADS,)), struct((INNER,)),
        ],
        scratch_shapes=[
            pltpu.VMEM((held, PIECE, D), F32), pltpu.SemaphoreType.DMA((held,)),
            pltpu.SemaphoreType.DMA((held,)),
        ],
        compiler_params=pltpu.CompilerParams(**params),
        name="finish",
    )(total)
    return (
        mixed.reshape(tokens.shape), tg.reshape(tokens.shape), ng, in_grad.T, cw, cb, dtb, rate,
        skip, og, out_grad,
    )


def solution(mesh):
    local = P("rows", "seq", None)
    return jax.shard_map(
        on_device,
        mesh=mesh,
        in_specs=(local, P("rows", None)) + (P(),) * 9 + (local,),
        out_specs=(local, local) + (P(),) * 9,
        check_vma=False,
    )
```
